32 devices in a mesh: dp: 8 (over z, y), mp: 4 (over x, core).
Axes of the slice: x: 2, y: 2, z: 4, core: 2. Of those that a mesh axis runs over, the one named last changes fastest.
Arguments:
- embeddings: bfloat16 [2048, 768], P('dp'), may hold values from -8192 to 8192
- cluster_ids: int32 [2048], P('dp'), may hold values from 0 to 31, as said below
Outputs:
- scores: float32 [2048], P('dp')
The draws below stay inside these ranges and needn't reach their ends.
Inputs may be any that keep to these rules, and one draw needn't show every extreme that they name: `cluster_ids`: the owner of cluster c is the index c // 4 of dp. Of the 256 rows of one index of dp, at most 64 lie in the clusters of one owner, and some owner gets exactly 64 rows from every index of dp.
All inputs are finite; a program needn't handle non-finite values.
Results may differ from the reference program's by a relative error of at most 0.0018.
Values may be sent and summed in bfloat16 or wider, within the bound.
No kernel may reach another device: no remote copies, remote signals or barrier semaphores. Data moves between devices by JAX's collectives and lax.ppermute only.
A program may use at most 64 MiB of HBM per device.

```python
import math
import jax
import jax.numpy as jnp
from jax import lax

D = 768
ROWS_DEV = 256
CPO = 4
PAIR = 64
SLOTS = 512
BLOCKS = 32
RQ = 64
N_DP = 8


def layout_draw(key):
    base_key = jax.random.fold_in(key, 11)
    slot_total = 2 * ROWS_DEV
    owner_count = slot_total // PAIR
    groups = max(ROWS_DEV // 16, 1)
    levels = jax.random.randint(jax.random.fold_in(base_key, 1), (owner_count,), 0, 4) * (slot_total // 2)
    hottest = jax.random.randint(jax.random.fold_in(base_key, 2), (), 0, owner_count)
    owner_range = jnp.arange(owner_count)
    forced = (owner_range == hottest) | (owner_range == 0) | (owner_range == owner_count - 1)
    levels = jnp.where(forced, 8 * slot_total, levels)
    slot_owner = jnp.arange(slot_total) // PAIR

    def one_source(source):
        source_key = jax.random.fold_in(base_key, 100 + source)
        shuffled = jax.random.permutation(jax.random.fold_in(source_key, 1), slot_total)
        priority = (levels[slot_owner] + shuffled) * slot_total + jnp.arange(slot_total)
        chosen = jnp.argsort(-priority, stable=True)[:ROWS_DEV]
        mixing = jax.random.permutation(jax.random.fold_in(source_key, 2), ROWS_DEV)
        picked = chosen[mixing]
        owners = picked // PAIR
        within = jax.random.randint(jax.random.fold_in(source_key, 3), (ROWS_DEV,), 0, CPO)
        first_slot = picked % PAIR == 0
        within = jnp.where(first_slot & (owners == 0), 0, within)
        within = jnp.where(first_slot & (owners == owner_count - 1), CPO - 1, within)
        group_ids = jax.random.randint(jax.random.fold_in(source_key, 4), (ROWS_DEV,), 0, groups)
        return (owners * CPO + within, group_ids)
    cluster_ids, group_ids = jax.vmap(one_source)(jnp.arange(owner_count))
    return (cluster_ids.reshape(-1).astype(jnp.int32), group_ids.reshape(-1).astype(jnp.int32))


def draw_cluster_ids(key, part):
    cluster_ids, group_ids = layout_draw(key)
    return cluster_ids


def draw_embeddings(key, part):
    cluster_ids, group_ids = layout_draw(key)
    row_total = cluster_ids.shape[0]
    groups = max(ROWS_DEV // 16, 1)
    float_key = jax.random.fold_in(key, 29)
    shared_key = jax.random.fold_in(key, 31)
    direction_key = jax.random.fold_in(key, 37)
    direction_count = 32
    group_codes = cluster_ids * groups + group_ids
    own_part = jax.random.truncated_normal(jax.random.fold_in(float_key, 1), -4.0, 4.0, (row_total, D), jnp.float32)
    directions = jax.random.truncated_normal(direction_key, -4.0, 4.0, (direction_count, D), jnp.float32)

    def group_vector(code):
        return jax.random.truncated_normal(jax.random.fold_in(shared_key, code), -4.0, 4.0, (D,), jnp.float32)
    shared_part = jax.vmap(group_vector)(group_codes)
    own_weight = jnp.exp(jax.random.uniform(jax.random.fold_in(float_key, 2), (row_total, 1), jnp.float32, math.log(0.15), 0.0))
    is_copy = (jax.random.randint(jax.random.fold_in(float_key, 3), (row_total, 1), 0, 10) < 7).astype(jnp.float32)
    row_scale = jnp.exp(jax.random.uniform(jax.random.fold_in(float_key, 4), (row_total, 1), jnp.float32, 0.0, math.log(10.0)))
    col_scale = jnp.exp(jax.random.uniform(jax.random.fold_in(float_key, 5), (D,), jnp.float32, 0.0, math.log(3.0)))
    blocks_share = max(BLOCKS // D, 1)
    amplitude = math.sqrt(2.0 * BLOCKS / blocks_share)
    block_of_row = jnp.arange(row_total) // RQ
    spike_cols = jax.random.permutation(jax.random.fold_in(float_key, 6), D)[block_of_row % D]
    spike_value = jax.random.truncated_normal(jax.random.fold_in(float_key, 7), -4.0, 4.0, (row_total,), jnp.float32) * amplitude
    direction_index = jax.random.randint(jax.random.fold_in(float_key, 8), (row_total, 4), 0, direction_count)
    direction_weight = jax.random.uniform(jax.random.fold_in(float_key, 9), (row_total, 4), jnp.float32, -1.0, 1.0)
    correlated = direction_weight[:, 0:1] * directions[direction_index[:, 0]]
    correlated = correlated + direction_weight[:, 1:2] * directions[direction_index[:, 1]]
    correlated = correlated + direction_weight[:, 2:3] * directions[direction_index[:, 2]]
    correlated = correlated + direction_weight[:, 3:4] * directions[direction_index[:, 3]]
    mixed = own_weight * own_part + is_copy * shared_part + correlated
    mixed = mixed.at[jnp.arange(row_total), spike_cols].add(spike_value)
    values = row_scale * col_scale[None, :] * mixed
    return values.astype(jnp.bfloat16)


def setup_inputs(seed: int = 0) -> dict:
    keys = jax.random.split(jax.random.key(seed), 3)
    return {
        "embeddings": draw_embeddings(jax.random.fold_in(keys[2], 71), 0),
        "cluster_ids": draw_cluster_ids(jax.random.fold_in(keys[2], 71), 0),
    }


def normalize_rows(values):
    widened = values.astype(jnp.float32)
    square_sum = lax.optimization_barrier(jnp.sum(widened * widened, axis=1, keepdims=True))
    inverse_norm = lax.rsqrt(square_sum + 1e-06)
    return (widened * inverse_norm).astype(jnp.bfloat16)

def reference(embeddings, cluster_ids):
    row_total = embeddings.shape[0]
    identity = jnp.eye(D, dtype=jnp.float32)
    moments = lax.dot_general(embeddings.astype(jnp.float32), embeddings.astype(jnp.float32), (((0,), (0,)), ((), ())), preferred_element_type=jnp.float32)
    chol_factor = jnp.linalg.cholesky(moments / row_total + 0.001 * identity)
    whitening = jax.scipy.linalg.solve_triangular(chol_factor, identity, lower=True).astype(jnp.bfloat16)
    whitened = lax.dot_general(embeddings.astype(jnp.float32), whitening.astype(jnp.float32), (((1,), (1,)), ((), ())), preferred_element_type=jnp.float32).astype(jnp.bfloat16)
    unit = normalize_rows(whitened)
    owner_ids = (cluster_ids // CPO).astype(jnp.int32)
    sort_order = jnp.argsort(owner_ids, stable=True).astype(jnp.int32)
    counts = jax.ops.segment_sum(jnp.ones((row_total,), jnp.int32), owner_ids, num_segments=N_DP).astype(jnp.int32)
    starts = (jnp.cumsum(counts) - counts).astype(jnp.int32)
    capacity = SLOTS
    unit_sorted = jnp.concatenate([unit[sort_order], jnp.zeros((capacity, D), jnp.bfloat16)], axis=0)
    ids_sorted = jnp.concatenate([cluster_ids[sort_order], jnp.full((capacity,), -1, jnp.int32)], axis=0)
    local_pos = jnp.arange(capacity, dtype=jnp.int32)

    def per_owner(owner_index):
        first_row = starts[owner_index]
        key_units = lax.dynamic_slice_in_dim(unit_sorted, first_row, capacity, 0)
        key_ids = lax.dynamic_slice_in_dim(ids_sorted, first_row, capacity, 0)
        key_ids = jnp.where(local_pos < counts[owner_index], key_ids, -1)
        similarity = lax.dot_general(key_units.astype(jnp.float32), key_units.astype(jnp.float32), (((1,), (1,)), ((), ())), preferred_element_type=jnp.float32)
        same_cluster = (key_ids[:, None] == key_ids[None, :]) & (key_ids[:, None] >= 0) & (local_pos[:, None] != local_pos[None, :])
        return lax.optimization_barrier(jnp.max(jnp.where(same_cluster, similarity, -1.0), axis=1))
    owner_table = lax.map(per_owner, jnp.arange(N_DP, dtype=jnp.int32))
    owner_sorted = owner_ids[sort_order]
    position = (jnp.arange(row_total, dtype=jnp.int32) - starts[owner_sorted]).astype(jnp.int32)
    sorted_scores = owner_table[owner_sorted, position]
    return jnp.zeros((row_total,), jnp.float32).at[sort_order].set(sorted_scores)
```

```python
import jax
import jax.numpy as jnp
from jax import lax
from jax.sharding import PartitionSpec as P

CPO = 4
GATHER_LIMIT = 8 * 1024 * 1024


def contract_rows(left_rows, right_rows):
    return lax.dot_general(
        left_rows, right_rows, (((0,), (0,)), ((), ())), preferred_element_type=jnp.float32
    )


def normalize_rows(values):
    widened = values.astype(jnp.float32)
    square_sum = jnp.sum(widened * widened, axis=1, keepdims=True)
    inverse_norm = lax.rsqrt(square_sum + 1e-06)
    return (widened * inverse_norm).astype(jnp.bfloat16)


def best_match(queries, query_ids, query_start, key_units, key_ids):
    similarity = lax.dot_general(
        queries, key_units, (((1,), (1,)), ((), ())), preferred_element_type=jnp.float32
    )
    query_pos = query_start + jnp.arange(queries.shape[0], dtype=jnp.int32)
    key_pos = jnp.arange(key_units.shape[0], dtype=jnp.int32)
    same_cluster = (
        (query_ids[:, None] == key_ids[None, :])
        & (query_ids[:, None] >= 0)
        & (query_pos[:, None] != key_pos[None, :])
    )
    return jnp.max(jnp.where(same_cluster, similarity, -1.0), axis=1)


def whitening_of(moments, row_total):
    identity = jnp.eye(moments.shape[0], dtype=jnp.float32)
    chol_factor = jnp.linalg.cholesky(moments / float(row_total) + 0.001 * identity)
    return jax.scipy.linalg.solve_triangular(chol_factor, identity, lower=True).astype(
        jnp.bfloat16
    )


def local_gathered(embeddings, cluster_ids):
    row_count = embeddings.shape[0]
    mp_count = lax.axis_size("mp")
    quarter = row_count // mp_count
    own = lax.dynamic_slice_in_dim(embeddings, lax.axis_index("mp") * quarter, quarter, 0)
    rows = lax.all_gather(own, ("dp", "mp"), axis=0, tiled=True)
    ids = lax.all_gather(cluster_ids, "dp", axis=0, tiled=True)
    whitening = whitening_of(contract_rows(rows, rows), rows.shape[0])
    whitened = lax.dot_general(
        rows, whitening, (((1,), (1,)), ((), ())), preferred_element_type=jnp.float32
    ).astype(jnp.bfloat16)
    unit = normalize_rows(whitened)
    start = lax.axis_index("dp") * row_count
    queries = lax.dynamic_slice_in_dim(unit, start, row_count, 0)
    return best_match(queries, cluster_ids, start, unit, ids)


def local_routed(embeddings, cluster_ids):
    row_count, feat_width = embeddings.shape
    dp_count = lax.axis_size("dp")
    mp_count = lax.axis_size("mp")
    mp_index = lax.axis_index("mp")
    pair_cap = 2 * row_count // dp_count
    slot_count = dp_count * pair_cap
    quarter_len = slot_count // mp_count
    col_share = feat_width // mp_count
    own_cols = lax.dynamic_slice_in_dim(embeddings, mp_index * col_share, col_share, 1)
    column_sums = lax.psum(contract_rows(embeddings, own_cols), "dp")
    moments = lax.all_gather(column_sums, "mp", axis=1, tiled=True)
    whitening = whitening_of(moments, row_count * dp_count)
    owner_ids = cluster_ids // CPO
    owner_hits = (owner_ids[:, None] == jnp.arange(dp_count, dtype=jnp.int32)[None, :]).astype(
        jnp.int32
    )
    earlier_hits = jnp.cumsum(owner_hits, axis=0) - owner_hits
    row_rank = jnp.sum(earlier_hits * owner_hits, axis=1)
    whiten_part = lax.dynamic_slice_in_dim(whitening, mp_index * col_share, col_share, 0)
    whitened = lax.dot_general(
        embeddings, whiten_part, (((1,), (1,)), ((), ())), preferred_element_type=jnp.float32
    ).astype(jnp.bfloat16)
    slot_index = owner_ids * pair_cap + row_rank
    send_rows = jnp.zeros((slot_count, col_share), jnp.bfloat16).at[slot_index].set(whitened)
    send_ids = jnp.full((slot_count,), -1, jnp.int32).at[slot_index].set(cluster_ids)
    got_rows, got_ids = (
        lax.all_to_all(send_rows, "dp", split_axis=0, concat_axis=0, tiled=True),
        lax.all_to_all(send_ids, "dp", split_axis=0, concat_axis=0, tiled=True),
    )
    key_rows = lax.all_gather(got_rows, "mp", axis=1, tiled=True)
    unit = normalize_rows(key_rows)
    query_start = mp_index * quarter_len
    queries = lax.dynamic_slice_in_dim(unit, query_start, quarter_len, 0)
    query_ids = lax.dynamic_slice_in_dim(got_ids, query_start, quarter_len, 0)
    best_score = best_match(queries, query_ids, query_start, unit, got_ids)
    all_scores = lax.all_gather(best_score, "mp", axis=0, tiled=True)
    returned = lax.all_to_all(all_scores, "dp", split_axis=0, concat_axis=0, tiled=True)
    return returned[slot_index]


def local(embeddings, cluster_ids):
    gathered_bytes = embeddings.size * 2 * lax.axis_size("dp")
    if gathered_bytes <= GATHER_LIMIT:
        return local_gathered(embeddings, cluster_ids)
    return local_routed(embeddings, cluster_ids)


def solution(mesh):
    in_specs = (P("dp", None), P("dp"))
    out_specs = P("dp")
    return jax.shard_map(local, mesh=mesh, in_specs=in_specs, out_specs=out_specs, check_vma=False)
```

```python
import functools
import jax
import jax.numpy as jnp
from jax import lax
from jax.experimental import pallas as pl
from jax.experimental.pallas import tpu as pltpu
from jax.sharding import PartitionSpec as P

CPO = 4
GATHER_LIMIT = 8 * 1024 * 1024
BLK = 128
SUB = 8
HI = lax.Precision.HIGHEST


def invert_factor(block):
    shape = (SUB, BLK)
    lane = lax.broadcasted_iota(jnp.int32, shape, 1)
    sub = lax.broadcasted_iota(jnp.int32, shape, 0)
    count = BLK // SUB
    rows = [block[SUB * i : SUB * (i + 1), :] for i in range(count)]
    done = []
    for t in range(count):
        first = SUB * t
        here = (lane >= first) & (lane < first + SUB)
        cols = {
            i: [jnp.broadcast_to(rows[i][:, first + q : first + q + 1], shape) for q in range(SUB)]
            for i in range(t, count)
        }
        for i in range(t, count):
            rows[i] = jnp.where(here, (lane - first == sub).astype(jnp.float32) if i == t else 0.0, rows[i])
        pivots = jnp.ones(shape, jnp.float32)
        for p in range(SUB):
            pivot = jnp.broadcast_to(cols[t][p][p : p + 1, :], shape)
            guess = pl.reciprocal(pivot, approx=True)
            inverse = guess * (2.0 - pivot * guess)
            pivots = jnp.where(sub == p, pivot, pivots)
            pivot_row = jnp.broadcast_to(rows[t][p : p + 1, :], shape)
            tops = {q: jnp.broadcast_to(cols[t][q][p : p + 1, :], shape) for q in range(p + 1, SUB)}
            for i in range(t, count):
                if i == t and p == SUB - 1:
                    continue
                factor = cols[i][p] * inverse
                if i == t:
                    factor = jnp.where(sub > p, factor, 0.0)
                for q in range(p + 1, SUB):
                    cols[i][q] = cols[i][q] - factor * tops[q]
                rows[i] = rows[i] - factor * pivot_row
        done.append(jnp.where(lane <= first + sub, rows[t] * lax.rsqrt(pivots), 0.0))
    return jnp.concatenate(done, axis=0)


def dot_nn(a, b, precision=None):
    return lax.dot_general(a, b, (((1,), (0,)), ((), ())), precision=precision, preferred_element_type=jnp.float32)


def dot_nt(a, b, precision=None):
    return lax.dot_general(a, b, (((1,), (1,)), ((), ())), precision=precision, preferred_element_type=jnp.float32)


def score_kernel(row_total, parts, start_ref, moments_ref, rows_ref, ids_ref, own_ids_ref, out_ref, work, white, unit):
    width = moments_ref.shape[0]
    own = own_ids_ref.shape[1]
    row_i = lax.broadcasted_iota(jnp.int32, (width, width), 0)
    col_i = lax.broadcasted_iota(jnp.int32, (width, width), 1)
    work[...] = moments_ref[...] * (1.0 / row_total) + jnp.where(row_i == col_i, 0.001, 0.0)
    eye = (lax.broadcasted_iota(jnp.int32, (BLK, BLK), 0) == lax.broadcasted_iota(jnp.int32, (BLK, BLK), 1)).astype(jnp.float32)

    @pl.loop(0, width // BLK)
    def _(k):
        at = pl.multiple_of(k * BLK, BLK)
        here = pl.ds(at, BLK)
        inv = invert_factor(work[here, here])
        later = lax.broadcasted_iota(jnp.int32, (width, BLK), 0) >= at + BLK
        left = jnp.where(later, dot_nt(work[:, here], inv, HI), 0.0)
        work[:, here] = jnp.zeros((width, BLK), jnp.float32)
        work[here, here] = eye
        right = dot_nn(inv, work[here, :], HI)
        work[here, :] = right
        work[...] -= dot_nn(left, right, HI)

    white[...] = work[...].astype(jnp.bfloat16)

    @pl.loop(0, row_total // own)
    def _(c):
        chunk = pl.ds(pl.multiple_of(c * own, own), own)
        whitened = dot_nt(rows_ref[chunk, :], white[...]).astype(jnp.bfloat16).astype(jnp.float32)
        square_sum = jnp.sum(whitened * whitened, axis=1, keepdims=True)
        unit[chunk, :] = (whitened * lax.rsqrt(square_sum + 1e-06)).astype(jnp.bfloat16)

    piece, stride = own // parts, row_total // parts
    start = pl.multiple_of(start_ref[0], piece)
    queries = jnp.concatenate([unit[pl.ds(n * stride + start, piece), :] for n in range(parts)], axis=0)
    flipped = jnp.broadcast_to(own_ids_ref[...], (BLK, own)).T
    own_col = flipped[:, 0:1]
    own_row = lax.broadcasted_iota(jnp.int32, (own, BLK), 0)
    own_pos = (own_row // piece) * stride + start + own_row % piece
    best = jnp.full((own, BLK), -1.0, jnp.float32)
    for c in range(row_total // BLK):
        keys = unit[c * BLK : (c + 1) * BLK, :]
        sims = dot_nt(queries, keys)
        pos = c * BLK + lax.broadcasted_iota(jnp.int32, (own, BLK), 1)
        same = (own_col == ids_ref[:, c * BLK : (c + 1) * BLK]) & (own_pos != pos)
        best = jnp.maximum(best, jnp.where(same, sims, -1.0))
    top = jnp.max(best, axis=1, keepdims=True)
    out_ref[...] = jnp.broadcast_to(top, (own, BLK)).T[0:1, :]


def scores_of(moments, rows, ids, own_ids, start, parts):
    row_total, width = rows.shape
    own = own_ids.shape[0]
    vmem = pl.BlockSpec(memory_space=pltpu.VMEM)
    out = pl.pallas_call(
        functools.partial(score_kernel, row_total, parts),
        out_shape=jax.ShapeDtypeStruct((1, own), jnp.float32),
        in_specs=[pl.BlockSpec(memory_space=pltpu.SMEM), vmem, vmem, vmem, vmem],
        out_specs=vmem,
        scratch_shapes=[
            pltpu.VMEM((width, width), jnp.float32),
            pltpu.VMEM((width, width), jnp.bfloat16),
            pltpu.VMEM((row_total, width), jnp.bfloat16),
        ],
        compiler_params=pltpu.CompilerParams(vmem_limit_bytes=48 * 1024 * 1024),
    )(start.reshape(1).astype(jnp.int32), moments, rows, ids.reshape(1, -1), own_ids.reshape(1, -1))
    return out.reshape(own)


def contract_rows(left_rows, right_rows):
    return lax.dot_general(
        left_rows, right_rows, (((0,), (0,)), ((), ())), preferred_element_type=jnp.float32
    )


def normalize_rows(values):
    widened = values.astype(jnp.float32)
    square_sum = jnp.sum(widened * widened, axis=1, keepdims=True)
    inverse_norm = lax.rsqrt(square_sum + 1e-06)
    return (widened * inverse_norm).astype(jnp.bfloat16)


def best_match(queries, query_ids, query_start, key_units, key_ids):
    similarity = lax.dot_general(
        queries, key_units, (((1,), (1,)), ((), ())), preferred_element_type=jnp.float32
    )
    query_pos = query_start + jnp.arange(queries.shape[0], dtype=jnp.int32)
    key_pos = jnp.arange(key_units.shape[0], dtype=jnp.int32)
    same_cluster = (
        (query_ids[:, None] == key_ids[None, :])
        & (query_ids[:, None] >= 0)
        & (query_pos[:, None] != key_pos[None, :])
    )
    return jnp.max(jnp.where(same_cluster, similarity, -1.0), axis=1)


def whitening_of(moments, row_total):
    identity = jnp.eye(moments.shape[0], dtype=jnp.float32)
    chol_factor = jnp.linalg.cholesky(moments / float(row_total) + 0.001 * identity)
    return jax.scipy.linalg.solve_triangular(chol_factor, identity, lower=True).astype(
        jnp.bfloat16
    )


def local_gathered(embeddings, cluster_ids):
    row_count = embeddings.shape[0]
    dp_count, mp_count = lax.axis_size("dp"), lax.axis_size("mp")
    piece = row_count // mp_count
    own = lax.dynamic_slice_in_dim(embeddings, lax.axis_index("mp") * piece, piece, 0)
    ids = lax.all_gather(cluster_ids, "dp", axis=0, tiled=True)
    key_ids = ids.reshape(dp_count, mp_count, piece).swapaxes(0, 1).reshape(-1)
    rows = lax.all_gather(lax.all_gather(own, "dp", axis=0, tiled=True), "mp", axis=0, tiled=True)
    moments = contract_rows(rows, rows)
    return scores_of(moments, rows, key_ids, cluster_ids, lax.axis_index("dp") * piece, mp_count)


def local_routed(embeddings, cluster_ids):
    row_count, feat_width = embeddings.shape
    dp_count = lax.axis_size("dp")
    mp_count = lax.axis_size("mp")
    mp_index = lax.axis_index("mp")
    pair_cap = 2 * row_count // dp_count
    slot_count = dp_count * pair_cap
    quarter_len = slot_count // mp_count
    col_share = feat_width // mp_count
    own_cols = lax.dynamic_slice_in_dim(embeddings, mp_index * col_share, col_share, 1)
    column_sums = lax.psum(contract_rows(embeddings, own_cols), "dp")
    moments = lax.all_gather(column_sums, "mp", axis=1, tiled=True)
    whitening = whitening_of(moments, row_count * dp_count)
    owner_ids = cluster_ids // CPO
    owner_hits = (owner_ids[:, None] == jnp.arange(dp_count, dtype=jnp.int32)[None, :]).astype(
        jnp.int32
    )
    earlier_hits = jnp.cumsum(owner_hits, axis=0) - owner_hits
    row_rank = jnp.sum(earlier_hits * owner_hits, axis=1)
    whiten_part = lax.dynamic_slice_in_dim(whitening, mp_index * col_share, col_share, 0)
    whitened = lax.dot_general(
        embeddings, whiten_part, (((1,), (1,)), ((), ())), preferred_element_type=jnp.float32
    ).astype(jnp.bfloat16)
    slot_index = owner_ids * pair_cap + row_rank
    send_rows = jnp.zeros((slot_count, col_share), jnp.bfloat16).at[slot_index].set(whitened)
    send_ids = jnp.full((slot_count,), -1, jnp.int32).at[slot_index].set(cluster_ids)
    got_rows, got_ids = (
        lax.all_to_all(send_rows, "dp", split_axis=0, concat_axis=0, tiled=True),
        lax.all_to_all(send_ids, "dp", split_axis=0, concat_axis=0, tiled=True),
    )
    key_rows = lax.all_gather(got_rows, "mp", axis=1, tiled=True)
    unit = normalize_rows(key_rows)
    query_start = mp_index * quarter_len
    queries = lax.dynamic_slice_in_dim(unit, query_start, quarter_len, 0)
    query_ids = lax.dynamic_slice_in_dim(got_ids, query_start, quarter_len, 0)
    best_score = best_match(queries, query_ids, query_start, unit, got_ids)
    all_scores = lax.all_gather(best_score, "mp", axis=0, tiled=True)
    returned = lax.all_to_all(all_scores, "dp", split_axis=0, concat_axis=0, tiled=True)
    return returned[slot_index]


def local(embeddings, cluster_ids):
    gathered_bytes = embeddings.size * 2 * lax.axis_size("dp")
    if gathered_bytes <= GATHER_LIMIT:
        return local_gathered(embeddings, cluster_ids)
    return local_routed(embeddings, cluster_ids)


def solution(mesh):
    in_specs = (P("dp", None), P("dp"))
    out_specs = P("dp")
    return jax.shard_map(local, mesh=mesh, in_specs=in_specs, out_specs=out_specs, check_vma=False)
```

```python
import functools
import jax
import jax.numpy as jnp
from jax import lax
from jax.experimental import pallas as pl
from jax.experimental.pallas import tpu as pltpu
from jax.sharding import PartitionSpec as P

CPO = 4
GATHER_LIMIT = 8 * 1024 * 1024
BLK = 128
SUB = 8
PANEL = 256
HI = lax.Precision.HIGHEST


def invert_factor(block):
    shape = (SUB, BLK)
    lane = lax.broadcasted_iota(jnp.int32, shape, 1)
    sub = lax.broadcasted_iota(jnp.int32, shape, 0)
    count = BLK // SUB
    rows = [block[SUB * i : SUB * (i + 1), :] for i in range(count)]
    done = []
    for t in range(count):
        first = SUB * t
        here = (lane >= first) & (lane < first + SUB)
        cols = {
            i: [jnp.broadcast_to(rows[i][:, first + q : first + q + 1], shape) for q in range(SUB)]
            for i in range(t, count)
        }
        for i in range(t, count):
            rows[i] = jnp.where(here, (lane - first == sub).astype(jnp.float32) if i == t else 0.0, rows[i])
        pivots = jnp.ones(shape, jnp.float32)
        for p in range(SUB):
            pivot = jnp.broadcast_to(cols[t][p][p : p + 1, :], shape)
            guess = pl.reciprocal(pivot, approx=True)
            inverse = guess * (2.0 - pivot * guess)
            pivots = jnp.where(sub == p, pivot, pivots)
            pivot_row = jnp.broadcast_to(rows[t][p : p + 1, :], shape)
            tops = {q: jnp.broadcast_to(cols[t][q][p : p + 1, :], shape) for q in range(p + 1, SUB)}
            for i in range(t, count):
                if i == t and p == SUB - 1:
                    continue
                factor = cols[i][p] * inverse
                if i == t:
                    factor = jnp.where(sub > p, factor, 0.0)
                for q in range(p + 1, SUB):
                    cols[i][q] = cols[i][q] - factor * tops[q]
                rows[i] = rows[i] - factor * pivot_row
        done.append(jnp.where(lane <= first + sub, rows[t] * lax.rsqrt(pivots), 0.0))
    return jnp.concatenate(done, axis=0)


def dot_nn(a, b, precision=None):
    return lax.dot_general(a, b, (((1,), (0,)), ((), ())), precision=precision, preferred_element_type=jnp.float32)


def dot_nt(a, b, precision=None):
    return lax.dot_general(a, b, (((1,), (1,)), ((), ())), precision=precision, preferred_element_type=jnp.float32)


def score_kernel(sizes, *refs):
    pieces = refs[: len(sizes)]
    ids_ref, own_ids_ref, out_ref, rows, work, white, unit, sems = refs[len(sizes) :]
    row_total, width = rows.shape
    own = sizes[0]
    copies = []
    at = 0
    for n, (size, source) in enumerate(zip(sizes, pieces)):
        copies.append(pltpu.make_async_copy(source, rows.at[pl.ds(at, size), :], sems.at[n]))
        at += size
    for copy in copies:
        copy.start()
    for copy in copies:
        copy.wait()
    for at in range(0, width, PANEL):
        panel = slice(at, at + PANEL)
        sums = lax.dot_general(
            rows[:, panel], rows[...], (((0,), (0,)), ((), ())), preferred_element_type=jnp.float32
        )
        row_i = at + lax.broadcasted_iota(jnp.int32, (PANEL, width), 0)
        col_i = lax.broadcasted_iota(jnp.int32, (PANEL, width), 1)
        work[panel, :] = sums * (1.0 / row_total) + jnp.where(row_i == col_i, 0.001, 0.0)
    eye = (lax.broadcasted_iota(jnp.int32, (BLK, BLK), 0) == lax.broadcasted_iota(jnp.int32, (BLK, BLK), 1)).astype(jnp.float32)

    @pl.loop(0, width // BLK)
    def _(k):
        at = pl.multiple_of(k * BLK, BLK)
        here = pl.ds(at, BLK)
        inv = invert_factor(work[here, here])
        later = lax.broadcasted_iota(jnp.int32, (width, BLK), 0) >= at + BLK
        left = jnp.where(later, dot_nt(work[:, here], inv, HI), 0.0)
        work[:, here] = jnp.zeros((width, BLK), jnp.float32)
        work[here, here] = eye
        right = dot_nn(inv, work[here, :], HI)
        work[here, :] = right
        work[...] -= dot_nn(left, right, HI)

    white[...] = work[...].astype(jnp.bfloat16)

    @pl.loop(0, row_total // own)
    def _(c):
        chunk = pl.ds(pl.multiple_of(c * own, own), own)
        whitened = dot_nt(rows[chunk, :], white[...]).astype(jnp.bfloat16).astype(jnp.float32)
        square_sum = jnp.sum(whitened * whitened, axis=1, keepdims=True)
        unit[chunk, :] = (whitened * lax.rsqrt(square_sum + 1e-06)).astype(jnp.bfloat16)

    queries = unit[0:own, :]
    flipped = jnp.broadcast_to(own_ids_ref[...], (BLK, own)).T
    own_col = flipped[:, 0:1]
    own_pos = lax.broadcasted_iota(jnp.int32, (own, BLK), 0)
    best = jnp.full((own, BLK), -1.0, jnp.float32)
    for c in range(row_total // BLK):
        keys = unit[c * BLK : (c + 1) * BLK, :]
        sims = dot_nt(queries, keys)
        same = own_col == ids_ref[:, c * BLK : (c + 1) * BLK]
        if c * BLK < own:
            pos = c * BLK + lax.broadcasted_iota(jnp.int32, (own, BLK), 1)
            same = same & (own_pos != pos)
        best = jnp.maximum(best, jnp.where(same, sims, -1.0))
    top = jnp.max(best, axis=1, keepdims=True)
    out_ref[...] = jnp.broadcast_to(top, (own, BLK)).T[0:1, :]


def scores_of(pieces, ids):
    sizes = tuple(piece.shape[0] for piece in pieces)
    row_total, width, own = sum(sizes), pieces[0].shape[1], sizes[0]
    vmem = pl.BlockSpec(memory_space=pltpu.VMEM)
    out = pl.pallas_call(
        functools.partial(score_kernel, sizes),
        out_shape=jax.ShapeDtypeStruct((1, own), jnp.float32),
        in_specs=[pl.BlockSpec(memory_space=pl.ANY)] * len(sizes) + [vmem, vmem],
        out_specs=vmem,
        scratch_shapes=[
            pltpu.VMEM((row_total, width), jnp.bfloat16),
            pltpu.VMEM((width, width), jnp.float32),
            pltpu.VMEM((width, width), jnp.bfloat16),
            pltpu.VMEM((row_total, width), jnp.bfloat16),
            pltpu.SemaphoreType.DMA((len(sizes),)),
        ],
        compiler_params=pltpu.CompilerParams(vmem_limit_bytes=48 * 1024 * 1024),
    )(*pieces, ids.reshape(1, -1), ids[:own].reshape(1, -1))
    return out.reshape(own)


def contract_rows(left_rows, right_rows):
    return lax.dot_general(
        left_rows, right_rows, (((0,), (0,)), ((), ())), preferred_element_type=jnp.float32
    )


def normalize_rows(values):
    widened = values.astype(jnp.float32)
    square_sum = jnp.sum(widened * widened, axis=1, keepdims=True)
    inverse_norm = lax.rsqrt(square_sum + 1e-06)
    return (widened * inverse_norm).astype(jnp.bfloat16)


def best_match(queries, query_ids, query_start, key_units, key_ids):
    similarity = lax.dot_general(
        queries, key_units, (((1,), (1,)), ((), ())), preferred_element_type=jnp.float32
    )
    query_pos = query_start + jnp.arange(queries.shape[0], dtype=jnp.int32)
    key_pos = jnp.arange(key_units.shape[0], dtype=jnp.int32)
    same_cluster = (
        (query_ids[:, None] == key_ids[None, :])
        & (query_ids[:, None] >= 0)
        & (query_pos[:, None] != key_pos[None, :])
    )
    return jnp.max(jnp.where(same_cluster, similarity, -1.0), axis=1)


def whitening_of(moments, row_total):
    identity = jnp.eye(moments.shape[0], dtype=jnp.float32)
    chol_factor = jnp.linalg.cholesky(moments / float(row_total) + 0.001 * identity)
    return jax.scipy.linalg.solve_triangular(chol_factor, identity, lower=True).astype(
        jnp.bfloat16
    )


def exchange(value, axis, flip):
    return lax.ppermute(value, axis, [(i, i ^ flip) for i in range(lax.axis_size(axis))])


def local_gathered(embeddings, cluster_ids):
    row_count = embeddings.shape[0]
    far = range(2, lax.axis_size("dp"), 2)
    mp_index = lax.axis_index("mp")
    half, quarter = row_count // 2, row_count // 4

    def cut(values, size, index):
        return lax.dynamic_slice_in_dim(values, index * size, size, 0)

    own = cut(embeddings, quarter, mp_index)
    along_z = jnp.concatenate([exchange(own, "dp", flip) for flip in far], axis=0)
    near = exchange(cut(embeddings, half, mp_index % 2), "dp", 1)
    along_y = exchange(along_z, "dp", 1)
    held = [along_z, along_y, exchange(along_z, "mp", 2), exchange(along_y, "mp", 2)]
    held = held + [exchange(value, "mp", 1) for value in held]
    pieces = [embeddings, near, exchange(near, "mp", 1)] + held

    ids_z = [exchange(cluster_ids, "dp", flip) for flip in far]
    ids_near = exchange(jnp.stack([cluster_ids] + ids_z), "dp", 1)
    ids = [cluster_ids, cut(ids_near[0], half, mp_index % 2), cut(ids_near[0], half, 1 - mp_index % 2)]
    for flip in (0, 2, 1, 3):
        ids += [cut(value, quarter, mp_index ^ flip) for value in ids_z]
        ids += [cut(ids_near[n], quarter, mp_index ^ flip) for n in range(1, ids_near.shape[0])]
    return scores_of(pieces, jnp.concatenate(ids))


def local_routed(embeddings, cluster_ids):
    row_count, feat_width = embeddings.shape
    dp_count = lax.axis_size("dp")
    mp_count = lax.axis_size("mp")
    mp_index = lax.axis_index("mp")
    pair_cap = 2 * row_count // dp_count
    slot_count = dp_count * pair_cap
    quarter_len = slot_count // mp_count
    col_share = feat_width // mp_count
    own_cols = lax.dynamic_slice_in_dim(embeddings, mp_index * col_share, col_share, 1)
    column_sums = lax.psum(contract_rows(embeddings, own_cols), "dp")
    moments = lax.all_gather(column_sums, "mp", axis=1, tiled=True)
    whitening = whitening_of(moments, row_count * dp_count)
    owner_ids = cluster_ids // CPO
    owner_hits = (owner_ids[:, None] == jnp.arange(dp_count, dtype=jnp.int32)[None, :]).astype(
        jnp.int32
    )
    earlier_hits = jnp.cumsum(owner_hits, axis=0) - owner_hits
    row_rank = jnp.sum(earlier_hits * owner_hits, axis=1)
    whiten_part = lax.dynamic_slice_in_dim(whitening, mp_index * col_share, col_share, 0)
    whitened = lax.dot_general(
        embeddings, whiten_part, (((1,), (1,)), ((), ())), preferred_element_type=jnp.float32
    ).astype(jnp.bfloat16)
    slot_index = owner_ids * pair_cap + row_rank
    send_rows = jnp.zeros((slot_count, col_share), jnp.bfloat16).at[slot_index].set(whitened)
    send_ids = jnp.full((slot_count,), -1, jnp.int32).at[slot_index].set(cluster_ids)
    got_rows, got_ids = (
        lax.all_to_all(send_rows, "dp", split_axis=0, concat_axis=0, tiled=True),
        lax.all_to_all(send_ids, "dp", split_axis=0, concat_axis=0, tiled=True),
    )
    key_rows = lax.all_gather(got_rows, "mp", axis=1, tiled=True)
    unit = normalize_rows(key_rows)
    query_start = mp_index * quarter_len
    queries = lax.dynamic_slice_in_dim(unit, query_start, quarter_len, 0)
    query_ids = lax.dynamic_slice_in_dim(got_ids, query_start, quarter_len, 0)
    best_score = best_match(queries, query_ids, query_start, unit, got_ids)
    all_scores = lax.all_gather(best_score, "mp", axis=0, tiled=True)
    returned = lax.all_to_all(all_scores, "dp", split_axis=0, concat_axis=0, tiled=True)
    return returned[slot_index]


def local(embeddings, cluster_ids):
    gathered_bytes = embeddings.size * 2 * lax.axis_size("dp")
    if gathered_bytes <= GATHER_LIMIT and lax.axis_size("mp") == 4:
        return local_gathered(embeddings, cluster_ids)
    return local_routed(embeddings, cluster_ids)


def solution(mesh):
    in_specs = (P("dp", None), P("dp"))
    out_specs = P("dp")
    return jax.shard_map(local, mesh=mesh, in_specs=in_specs, out_specs=out_specs, check_vma=False)
```

```python
import functools
import jax
import jax.numpy as jnp
from jax import lax
from jax.experimental import pallas as pl
from jax.experimental.pallas import tpu as pltpu
from jax.sharding import PartitionSpec as P

CPO = 4
GATHER_LIMIT = 8 * 1024 * 1024
BLK = 128
SUB = 8
PANEL = 256


def invert_factor(block, jobs):
    shape = (SUB, BLK)
    lane = lax.broadcasted_iota(jnp.int32, shape, 1)
    sub = lax.broadcasted_iota(jnp.int32, shape, 0)
    count = BLK // SUB
    rows = [block[SUB * i : SUB * (i + 1), :] for i in range(count)]
    done = []
    for t in range(count):
        first = SUB * t
        here = (lane >= first) & (lane < first + SUB)
        cols = {
            i: [jnp.broadcast_to(rows[i][:, first + q : first + q + 1], shape) for q in range(SUB)]
            for i in range(t, count)
        }
        for i in range(t, count):
            rows[i] = jnp.where(here, (lane - first == sub).astype(jnp.float32) if i == t else 0.0, rows[i])
        pivots = jnp.ones(shape, jnp.float32)
        for p in range(SUB):
            pivot = jnp.broadcast_to(cols[t][p][p : p + 1, :], shape)
            guess = pl.reciprocal(pivot, approx=True)
            inverse = guess * (2.0 - pivot * guess)
            pivots = jnp.where(sub == p, pivot, pivots)
            pivot_row = jnp.broadcast_to(rows[t][p : p + 1, :], shape)
            tops = {q: jnp.broadcast_to(cols[t][q][p : p + 1, :], shape) for q in range(p + 1, SUB)}
            for i in range(t, count):
                if i == t and p == SUB - 1:
                    continue
                factor = cols[i][p] * inverse
                if i == t:
                    factor = jnp.where(sub > p, factor, 0.0)
                for q in range(p + 1, SUB):
                    cols[i][q] = cols[i][q] - factor * tops[q]
                rows[i] = rows[i] - factor * pivot_row
        done.append(jnp.where(lane <= first + sub, rows[t] * lax.rsqrt(pivots), 0.0))
        for job in jobs[len(jobs) * t // count : len(jobs) * (t + 1) // count]:
            job()
    return jnp.concatenate(done, axis=0)


def dot_nn(a, b):
    return lax.dot_general(a, b, (((1,), (0,)), ((), ())), preferred_element_type=jnp.float32)


def dot_nt(a, b):
    return lax.dot_general(a, b, (((1,), (1,)), ((), ())), preferred_element_type=jnp.float32)


def split(value):
    high = value.astype(jnp.bfloat16)
    rest = value - high.astype(jnp.float32)
    mid = rest.astype(jnp.bfloat16)
    return high, mid, (rest - mid.astype(jnp.float32)).astype(jnp.bfloat16)


def as_left(value):
    a, b, c = split(value)
    return jnp.concatenate([a, a, b, b, a, c], axis=1)


def as_right(value, axis):
    a, b, c = split(value)
    return jnp.concatenate([a, b, a, b, c, a], axis=axis)


def score_kernel(sizes, *refs):
    pieces = refs[: len(sizes)]
    ids_ref, own_ids_ref, out_ref = refs[len(sizes) : len(sizes) + 3]
    rows, flipped, work, left, right, below, white, own_white, sims, sums = refs[len(sizes) + 3 :]
    row_total, width = rows.shape
    own = sizes[0]
    count = width // BLK
    blocks = [slice(BLK * n, BLK * (n + 1)) for n in range(count)]
    chunks = [slice(n, n + own) for n in range(0, row_total, own)]

    at = 0
    for size, source in zip(sizes, pieces):
        rows[at : at + size, :] = source[...]
        at += size

    def flip_panel(at):
        flipped[at : at + PANEL, :] = rows[:, at : at + PANEL].T

    def moments_of(at, to):
        sums_of = dot_nn(flipped[at : at + PANEL, :], rows[:, to : to + PANEL])
        if at == to:
            shape = (PANEL, PANEL)
            on_diagonal = lax.broadcasted_iota(jnp.int32, shape, 0) == lax.broadcasted_iota(jnp.int32, shape, 1)
            work[at : at + PANEL, to : to + PANEL] = sums_of * (1.0 / row_total) + jnp.where(on_diagonal, 0.001, 0.0)
        else:
            work[at : at + PANEL, to : to + PANEL] = sums_of * (1.0 / row_total)

    def mask_of(at):
        own_col = jnp.broadcast_to(own_ids_ref[...], (BLK, own)).T[:, 0:1]
        same = own_col == ids_ref[:, at : at + BLK]
        if at < own:
            own_pos = lax.broadcasted_iota(jnp.int32, (own, BLK), 0)
            same = same & (own_pos != at + lax.broadcasted_iota(jnp.int32, (own, BLK), 1))
        sims[:, at : at + BLK] = jnp.where(same, 0.0, -1e30)

    def first_jobs():
        jobs = []
        for at in range(PANEL, width, PANEL):
            jobs.append(functools.partial(flip_panel, at))
            jobs += [functools.partial(moments_of, at, to) for to in range(0, at + PANEL, PANEL)]
        return jobs + [functools.partial(mask_of, at) for at in range(0, row_total, BLK)]

    def left_of(n, h, inverse_right):
        value = dot_nt(as_left(work[blocks[n], blocks[h]]), inverse_right[...])
        left[blocks[n], :] = as_left(value)
        right[blocks[n], :] = as_right(value, 1)

    def below_of(j, h, inverse_left):
        value = dot_nn(inverse_left[...], as_right(work[blocks[h], blocks[j]], 0))
        below[:, blocks[j]] = as_right(value, 0)
        white[:, blocks[j]] = value.astype(jnp.bfloat16)

    def reduce_right(n, j):
        work[blocks[n], blocks[j]] -= dot_nt(left[blocks[n], :], right[blocks[j], :])

    def reduce_left(n, h):
        if h > 0:
            done = slice(0, BLK * h)
            work[blocks[n], done] -= dot_nn(left[blocks[n], :], below[:, done])
        work[blocks[n], blocks[h]] = -dot_nn(left[blocks[n], :], below[:, blocks[h]])

    def whiten(c, h):
        feats = slice(0, BLK * (h + 1))
        whitened = dot_nt(rows[chunks[c], feats], white[:, feats]).astype(jnp.bfloat16)
        if c == 0:
            own_white[...] = whitened
        sims[:, chunks[c]] += dot_nt(own_white[...], whitened)
        widened = whitened.astype(jnp.float32)
        if h == 0:
            sums[chunks[c], :] = widened * widened
        else:
            sums[chunks[c], :] += widened * widened

    def finish_rows(h, inverse):
        white[:, blocks[h]] = inverse.astype(jnp.bfloat16)
        below[:, blocks[h]] = as_right(inverse, 0)
        inverse_left = as_left(inverse)
        jobs = [functools.partial(below_of, j, h, inverse_left) for j in range(h)]
        return jobs + [functools.partial(whiten, c, h) for c in range(len(chunks))]

    flip_panel(0)
    moments_of(0, 0)
    block = work[blocks[0], blocks[0]]
    jobs = first_jobs()
    for k in range(count):
        inverse = invert_factor(block, jobs)
        jobs = finish_rows(k, inverse)
        if k + 1 < count:
            inverse_right = as_right(inverse, 1)
            nexts = blocks[k + 1]
            value = dot_nt(as_left(work[nexts, blocks[k]]), inverse_right)
            value_left, value_right = as_left(value), as_right(value, 1)
            block = work[nexts, nexts] - dot_nt(value_left, value_right)
            left[nexts, :] = value_left
            right[nexts, :] = value_right
            later = range(k + 2, count)
            jobs += [functools.partial(left_of, n, k, inverse_right) for n in later]
            jobs += [functools.partial(reduce_left, n, k) for n in range(k + 1, count)]
            jobs += [functools.partial(reduce_right, n, j) for n in later for j in range(k + 1, n + 1)]
    for job in jobs:
        job()

    best = jnp.full((own, BLK), -1e30, jnp.float32)
    for at in range(0, row_total, BLK):
        key_sum = jnp.sum(sums[at : at + BLK, :].T, axis=0, keepdims=True)
        best = jnp.maximum(best, sims[:, at : at + BLK] * lax.rsqrt(key_sum + 1e-06))
    top = jnp.max(best, axis=1, keepdims=True)
    own_sum = jnp.sum(sums[0:own, :], axis=1, keepdims=True)
    top = jnp.where(top < -1e20, -1.0, jnp.maximum(top * lax.rsqrt(own_sum + 1e-06), -1.0))
    out_ref[...] = jnp.broadcast_to(top, (own, BLK)).T[0:1, :]


def scores_of(pieces, ids):
    sizes = tuple(piece.shape[0] for piece in pieces)
    row_total, width, own = sum(sizes), pieces[0].shape[1], sizes[0]
    vmem = pl.BlockSpec(memory_space=pltpu.VMEM)
    out = pl.pallas_call(
        functools.partial(score_kernel, sizes),
        out_shape=jax.ShapeDtypeStruct((1, own), jnp.float32),
        in_specs=[vmem] * (len(sizes) + 2),
        out_specs=vmem,
        scratch_shapes=[
            pltpu.VMEM((row_total, width), jnp.bfloat16),
            pltpu.VMEM((width, row_total), jnp.bfloat16),
            pltpu.VMEM((width, width), jnp.float32),
            pltpu.VMEM((width, 6 * BLK), jnp.bfloat16),
            pltpu.VMEM((width, 6 * BLK), jnp.bfloat16),
            pltpu.VMEM((6 * BLK, width), jnp.bfloat16),
            pltpu.VMEM((BLK, width), jnp.bfloat16),
            pltpu.VMEM((own, BLK), jnp.bfloat16),
            pltpu.VMEM((own, row_total), jnp.float32),
            pltpu.VMEM((row_total, BLK), jnp.float32),
        ],
        compiler_params=pltpu.CompilerParams(vmem_limit_bytes=48 * 1024 * 1024),
    )(*pieces, ids.reshape(1, -1), ids[:own].reshape(1, -1))
    return out.reshape(own)


def contract_rows(left_rows, right_rows):
    return lax.dot_general(
        left_rows, right_rows, (((0,), (0,)), ((), ())), preferred_element_type=jnp.float32
    )


def normalize_rows(values):
    widened = values.astype(jnp.float32)
    square_sum = jnp.sum(widened * widened, axis=1, keepdims=True)
    inverse_norm = lax.rsqrt(square_sum + 1e-06)
    return (widened * inverse_norm).astype(jnp.bfloat16)


def best_match(queries, query_ids, query_start, key_units, key_ids):
    similarity = lax.dot_general(
        queries, key_units, (((1,), (1,)), ((), ())), preferred_element_type=jnp.float32
    )
    query_pos = query_start + jnp.arange(queries.shape[0], dtype=jnp.int32)
    key_pos = jnp.arange(key_units.shape[0], dtype=jnp.int32)
    same_cluster = (
        (query_ids[:, None] == key_ids[None, :])
        & (query_ids[:, None] >= 0)
        & (query_pos[:, None] != key_pos[None, :])
    )
    return jnp.max(jnp.where(same_cluster, similarity, -1.0), axis=1)


def whitening_of(moments, row_total):
    identity = jnp.eye(moments.shape[0], dtype=jnp.float32)
    chol_factor = jnp.linalg.cholesky(moments / float(row_total) + 0.001 * identity)
    return jax.scipy.linalg.solve_triangular(chol_factor, identity, lower=True).astype(
        jnp.bfloat16
    )


def exchange(value, axis, flip):
    return lax.ppermute(value, axis, [(i, i ^ flip) for i in range(lax.axis_size(axis))])


def local_gathered(embeddings, cluster_ids):
    row_count = embeddings.shape[0]
    far = range(2, lax.axis_size("dp"), 2)
    mp_index = lax.axis_index("mp")
    half, quarter = row_count // 2, row_count // 4

    def cut(values, size, index):
        return lax.dynamic_slice_in_dim(values, index * size, size, 0)

    own = cut(embeddings, quarter, mp_index)
    along_z = jnp.concatenate([exchange(own, "dp", flip) for flip in far], axis=0)
    near = exchange(cut(embeddings, half, mp_index % 2), "dp", 1)
    along_y = exchange(along_z, "dp", 1)
    held = [along_z, along_y, exchange(along_z, "mp", 2), exchange(along_y, "mp", 2)]
    held = held + [exchange(value, "mp", 1) for value in held]
    pieces = [embeddings, near, exchange(near, "mp", 1)] + held

    ids_z = [exchange(cluster_ids, "dp", flip) for flip in far]
    ids_near = exchange(jnp.stack([cluster_ids] + ids_z), "dp", 1)
    ids = [cluster_ids, cut(ids_near[0], half, mp_index % 2), cut(ids_near[0], half, 1 - mp_index % 2)]
    for flip in (0, 2, 1, 3):
        ids += [cut(value, quarter, mp_index ^ flip) for value in ids_z]
        ids += [cut(ids_near[n], quarter, mp_index ^ flip) for n in range(1, ids_near.shape[0])]
    return scores_of(pieces, jnp.concatenate(ids))


def local_routed(embeddings, cluster_ids):
    row_count, feat_width = embeddings.shape
    dp_count = lax.axis_size("dp")
    mp_count = lax.axis_size("mp")
    mp_index = lax.axis_index("mp")
    pair_cap = 2 * row_count // dp_count
    slot_count = dp_count * pair_cap
    quarter_len = slot_count // mp_count
    col_share = feat_width // mp_count
    own_cols = lax.dynamic_slice_in_dim(embeddings, mp_index * col_share, col_share, 1)
    column_sums = lax.psum(contract_rows(embeddings, own_cols), "dp")
    moments = lax.all_gather(column_sums, "mp", axis=1, tiled=True)
    whitening = whitening_of(moments, row_count * dp_count)
    owner_ids = cluster_ids // CPO
    owner_hits = (owner_ids[:, None] == jnp.arange(dp_count, dtype=jnp.int32)[None, :]).astype(
        jnp.int32
    )
    earlier_hits = jnp.cumsum(owner_hits, axis=0) - owner_hits
    row_rank = jnp.sum(earlier_hits * owner_hits, axis=1)
    whiten_part = lax.dynamic_slice_in_dim(whitening, mp_index * col_share, col_share, 0)
    whitened = lax.dot_general(
        embeddings, whiten_part, (((1,), (1,)), ((), ())), preferred_element_type=jnp.float32
    ).astype(jnp.bfloat16)
    slot_index = owner_ids * pair_cap + row_rank
    send_rows = jnp.zeros((slot_count, col_share), jnp.bfloat16).at[slot_index].set(whitened)
    send_ids = jnp.full((slot_count,), -1, jnp.int32).at[slot_index].set(cluster_ids)
    got_rows, got_ids = (
        lax.all_to_all(send_rows, "dp", split_axis=0, concat_axis=0, tiled=True),
        lax.all_to_all(send_ids, "dp", split_axis=0, concat_axis=0, tiled=True),
    )
    key_rows = lax.all_gather(got_rows, "mp", axis=1, tiled=True)
    unit = normalize_rows(key_rows)
    query_start = mp_index * quarter_len
    queries = lax.dynamic_slice_in_dim(unit, query_start, quarter_len, 0)
    query_ids = lax.dynamic_slice_in_dim(got_ids, query_start, quarter_len, 0)
    best_score = best_match(queries, query_ids, query_start, unit, got_ids)
    all_scores = lax.all_gather(best_score, "mp", axis=0, tiled=True)
    returned = lax.all_to_all(all_scores, "dp", split_axis=0, concat_axis=0, tiled=True)
    return returned[slot_index]


def local(embeddings, cluster_ids):
    gathered_bytes = embeddings.size * 2 * lax.axis_size("dp")
    if gathered_bytes <= GATHER_LIMIT and lax.axis_size("mp") == 4:
        return local_gathered(embeddings, cluster_ids)
    return local_routed(embeddings, cluster_ids)


def solution(mesh):
    in_specs = (P("dp", None), P("dp"))
    out_specs = P("dp")
    return jax.shard_map(local, mesh=mesh, in_specs=in_specs, out_specs=out_specs, check_vma=False)
```

```python
import functools
import jax
import jax.numpy as jnp
from jax import lax
from jax.experimental import pallas as pl
from jax.experimental.pallas import tpu as pltpu
from jax.sharding import PartitionSpec as P

CPO = 4
GATHER_LIMIT = 8 * 1024 * 1024
BLK = 128
SUB = 8
PANEL = 256


def refine(value):
    guess = pl.reciprocal(value, approx=True)
    return guess * (2.0 - value * guess)


def invert_factor(block, jobs):
    shape = (SUB, BLK)
    lane = lax.broadcasted_iota(jnp.int32, shape, 1)
    sub = lax.broadcasted_iota(jnp.int32, shape, 0)
    count = BLK // SUB
    slots = count * SUB // 2
    jobs = list(jobs)
    total = len(jobs)
    rows = [block[SUB * i : SUB * (i + 1), :] for i in range(count)]

    def spread(i, at):
        return [jnp.broadcast_to(rows[i][:, at + q : at + q + 1], shape) for q in range(SUB)]

    def line(value, p):
        return jnp.broadcast_to(value[p : p + 1, :], shape)

    def follow(i, first, steps):
        cols = spread(i, first)
        value = jnp.where((lane >= first) & (lane < first + SUB), 0.0, rows[i])
        for p, (inverse, tops, pivot_row) in enumerate(steps):
            factor = cols[p] * inverse
            for q in range(p + 1, SUB):
                cols[q] = cols[q] - factor * tops[q]
            value = value - factor * pivot_row
        rows[i] = value

    def follow_far(i, first, flipped, lines):
        value = jnp.where((lane >= first) & (lane < first + SUB), 0.0, rows[i])
        for p in range(SUB):
            factor = jnp.broadcast_to(flipped[SUB * i : SUB * (i + 1), p : p + 1], shape)
            value = value - factor * lines[p]
        rows[i] = value

    done = []
    late = []
    cols = spread(0, 0)
    for t in range(count):
        first = SUB * t
        here = (lane >= first) & (lane < first + SUB)
        close = [i for i in (t + 1, t + 2) if i < count]
        close_cols = {i: spread(i, first) for i in close}
        if close:
            ahead = spread(t, first + SUB)
            next_cols = spread(t + 1, first + SUB)
        rows[t] = jnp.where(here, (lane - first == sub).astype(jnp.float32), rows[t])
        for i in close:
            rows[i] = jnp.where(here, 0.0, rows[i])
        pivots = jnp.ones(shape, jnp.float32)
        steps = []
        late_total = len(late)
        for p in range(0, SUB, 2):
            first_pivot, cross = line(cols[p], p), line(cols[p + 1], p)
            cross_low, corner = line(cols[p], p + 1), line(cols[p + 1], p + 1)
            det = first_pivot * corner - cross * cross_low
            inv1 = refine(first_pivot)
            guess = pl.reciprocal(det, approx=True)
            inv2 = (first_pivot * guess) * (2.0 - det * guess)
            below1 = jnp.where(sub > p, cols[p], 0.0)
            factor1 = below1 * inv1
            factor2 = jnp.where(sub > p + 1, cols[p + 1] - (below1 * cross) * inv1, 0.0) * inv2
            top1 = {q: line(cols[q], p) for q in range(p + 2, SUB)}
            top2 = {q: line(cols[q], p + 1) - (cross_low * top1[q]) * inv1 for q in range(p + 2, SUB)}
            for q in range(p + 2, SUB):
                cols[q] = (cols[q] - factor1 * top1[q]) - factor2 * top2[q]
            low = cross_low * inv1
            row1 = line(rows[t], p)
            row2 = line(rows[t], p + 1) - low * row1
            rows[t] = (rows[t] - factor1 * row1) - factor2 * row2
            pivots = jnp.where(sub == p, first_pivot, jnp.where(sub == p + 1, det * inv1, pivots))
            top1[p + 1] = cross
            steps += [(inv1, top1, row1), (inv2, top2, row2)]
            if close:
                ahead1 = [line(value, p) for value in ahead]
                ahead2 = [line(value, p + 1) - low * one for value, one in zip(ahead, ahead1)]
                ahead = [(v - factor1 * one) - factor2 * two for v, one, two in zip(ahead, ahead1, ahead2)]
            for i in close:
                values = close_cols[i]
                near1 = values[p] * inv1
                near2 = (values[p + 1] - near1 * cross) * inv2
                for q in range(p + 2, SUB):
                    values[q] = (values[q] - near1 * top1[q]) - near2 * top2[q]
                rows[i] = (rows[i] - near1 * row1) - near2 * row2
                if i == t + 1:
                    next_cols = [
                        (v - near1 * one) - near2 * two for v, one, two in zip(next_cols, ahead1, ahead2)
                    ]
            for _ in range(late_total * (p + 2) // SUB - late_total * p // SUB):
                late.pop(0)()
            slot = (t * SUB + p) // 2
            for job in jobs[total * slot // slots : total * (slot + 1) // slots]:
                job()
        scale = lax.rsqrt(pivots)
        scale = scale * (1.5 - 0.5 * pivots * scale * scale)
        scaled = rows[t] * scale
        done.append(jnp.where(lane <= first + sub, scaled, 0.0))
        if close:
            cols = next_cols
        if t + 3 < count:
            follow(t + 3, first, steps)
        if t + 4 < count:
            late.append(functools.partial(follow, t + 4, first, steps))
        if t + 5 < count:
            flipped = scaled.T
            lines = [line(scaled, p) for p in range(SUB)]
            late += [functools.partial(follow_far, i, first, flipped, lines) for i in range(t + 5, count)]
    return jnp.concatenate(done, axis=0)


def dot_nn(a, b):
    return lax.dot_general(a, b, (((1,), (0,)), ((), ())), preferred_element_type=jnp.float32)


def dot_nt(a, b):
    return lax.dot_general(a, b, (((1,), (1,)), ((), ())), preferred_element_type=jnp.float32)


def split(value):
    high = value.astype(jnp.bfloat16)
    rest = value - high.astype(jnp.float32)
    mid = rest.astype(jnp.bfloat16)
    return high, mid, (rest - mid.astype(jnp.float32)).astype(jnp.bfloat16)


def as_left(value):
    a, b, c = split(value)
    return jnp.concatenate([a, a, b, b, a, c], axis=1)


def as_right(value, axis):
    a, b, c = split(value)
    return jnp.concatenate([a, b, a, b, c, a], axis=axis)


def score_kernel(sizes, *refs):
    pieces = refs[: len(sizes)]
    ids_ref, own_ids_ref, out_ref = refs[len(sizes) : len(sizes) + 3]
    rows, flipped, work, left, right, below, white, own_white, sims, sums = refs[len(sizes) + 3 :]
    row_total, width = rows.shape
    own = sizes[0]
    count = width // BLK
    blocks = [slice(BLK * n, BLK * (n + 1)) for n in range(count)]
    chunks = [slice(n, n + own) for n in range(0, row_total, own)]

    at = 0
    for size, source in zip(sizes, pieces):
        rows[at : at + size, :] = source[...]
        at += size

    def flip_panel(at):
        flipped[at : at + PANEL, :] = rows[:, at : at + PANEL].T

    def moments_of(at, to):
        sums_of = dot_nn(flipped[at : at + PANEL, :], rows[:, to : to + PANEL])
        if at == to:
            shape = (PANEL, PANEL)
            on_diagonal = lax.broadcasted_iota(jnp.int32, shape, 0) == lax.broadcasted_iota(jnp.int32, shape, 1)
            work[at : at + PANEL, to : to + PANEL] = sums_of * (1.0 / row_total) + jnp.where(on_diagonal, 0.001, 0.0)
        else:
            work[at : at + PANEL, to : to + PANEL] = sums_of * (1.0 / row_total)

    def mask_of(at):
        own_col = jnp.broadcast_to(own_ids_ref[...], (BLK, own)).T[:, 0:1]
        same = own_col == ids_ref[:, at : at + BLK]
        if at < own:
            own_pos = lax.broadcasted_iota(jnp.int32, (own, BLK), 0)
            same = same & (own_pos != at + lax.broadcasted_iota(jnp.int32, (own, BLK), 1))
        sims[:, at : at + BLK] = jnp.where(same, 0.0, -1e30)

    def first_jobs():
        jobs = []
        for at in range(PANEL, width, PANEL):
            jobs.append(functools.partial(flip_panel, at))
            jobs += [functools.partial(moments_of, at, to) for to in range(0, at + PANEL, PANEL)]
        return jobs + [functools.partial(mask_of, at) for at in range(0, row_total, BLK)]

    def left_of(n, h, inverse_right):
        value = dot_nt(as_left(work[blocks[n], blocks[h]]), inverse_right[...])
        left[blocks[n], :] = as_left(value)
        right[blocks[n], :] = as_right(value, 1)

    def below_of(j, h, inverse_left):
        value = dot_nn(inverse_left[...], as_right(work[blocks[h], blocks[j]], 0))
        below[:, blocks[j]] = as_right(value, 0)
        white[:, blocks[j]] = value.astype(jnp.bfloat16)

    def reduce_right(n, j):
        work[blocks[n], blocks[j]] -= dot_nt(left[blocks[n], :], right[blocks[j], :])

    def reduce_left(n, h):
        if h > 0:
            done = slice(0, BLK * h)
            work[blocks[n], done] -= dot_nn(left[blocks[n], :], below[:, done])
        work[blocks[n], blocks[h]] = -dot_nn(left[blocks[n], :], below[:, blocks[h]])

    def whiten(c, h):
        feats = slice(0, BLK * (h + 1))
        whitened = dot_nt(rows[chunks[c], feats], white[:, feats]).astype(jnp.bfloat16)
        if c == 0:
            own_white[...] = whitened
        sims[:, chunks[c]] += dot_nt(own_white[...], whitened)
        widened = whitened.astype(jnp.float32)
        if h == 0:
            sums[chunks[c], :] = widened * widened
        else:
            sums[chunks[c], :] += widened * widened

    def finish_rows(h, inverse):
        white[:, blocks[h]] = inverse.astype(jnp.bfloat16)
        below[:, blocks[h]] = as_right(inverse, 0)
        inverse_left = as_left(inverse)
        jobs = [functools.partial(below_of, j, h, inverse_left) for j in range(h)]
        return jobs + [functools.partial(whiten, c, h) for c in range(len(chunks))]

    flip_panel(0)
    moments_of(0, 0)
    block = work[blocks[0], blocks[0]]
    jobs = first_jobs()
    for k in range(count):
        inverse = invert_factor(block, jobs)
        jobs = finish_rows(k, inverse)
        if k + 1 < count:
            inverse_right = as_right(inverse, 1)
            nexts = blocks[k + 1]
            value = dot_nt(as_left(work[nexts, blocks[k]]), inverse_right)
            value_left, value_right = as_left(value), as_right(value, 1)
            block = work[nexts, nexts] - dot_nt(value_left, value_right)
            left[nexts, :] = value_left
            right[nexts, :] = value_right
            later = range(k + 2, count)
            jobs += [functools.partial(left_of, n, k, inverse_right) for n in later]
            jobs += [functools.partial(reduce_left, n, k) for n in range(k + 1, count)]
            jobs += [functools.partial(reduce_right, n, j) for n in later for j in range(k + 1, n + 1)]
    for job in jobs:
        job()

    best = jnp.full((own, BLK), -1e30, jnp.float32)
    for at in range(0, row_total, BLK):
        key_sum = jnp.sum(sums[at : at + BLK, :].T, axis=0, keepdims=True)
        best = jnp.maximum(best, sims[:, at : at + BLK] * lax.rsqrt(key_sum + 1e-06))
    top = jnp.max(best, axis=1, keepdims=True)
    own_sum = jnp.sum(sums[0:own, :], axis=1, keepdims=True)
    top = jnp.where(top < -1e20, -1.0, jnp.maximum(top * lax.rsqrt(own_sum + 1e-06), -1.0))
    out_ref[...] = jnp.broadcast_to(top, (own, BLK)).T[0:1, :]


def scores_of(pieces, ids):
    sizes = tuple(piece.shape[0] for piece in pieces)
    row_total, width, own = sum(sizes), pieces[0].shape[1], sizes[0]
    vmem = pl.BlockSpec(memory_space=pltpu.VMEM)
    out = pl.pallas_call(
        functools.partial(score_kernel, sizes),
        out_shape=jax.ShapeDtypeStruct((1, own), jnp.float32),
        in_specs=[vmem] * (len(sizes) + 2),
        out_specs=vmem,
        scratch_shapes=[
            pltpu.VMEM((row_total, width), jnp.bfloat16),
            pltpu.VMEM((width, row_total), jnp.bfloat16),
            pltpu.VMEM((width, width), jnp.float32),
            pltpu.VMEM((width, 6 * BLK), jnp.bfloat16),
            pltpu.VMEM((width, 6 * BLK), jnp.bfloat16),
            pltpu.VMEM((6 * BLK, width), jnp.bfloat16),
            pltpu.VMEM((BLK, width), jnp.bfloat16),
            pltpu.VMEM((own, BLK), jnp.bfloat16),
            pltpu.VMEM((own, row_total), jnp.float32),
            pltpu.VMEM((row_total, BLK), jnp.float32),
        ],
        compiler_params=pltpu.CompilerParams(vmem_limit_bytes=48 * 1024 * 1024),
    )(*pieces, ids.reshape(1, -1), ids[:own].reshape(1, -1))
    return out.reshape(own)


def contract_rows(left_rows, right_rows):
    return lax.dot_general(
        left_rows, right_rows, (((0,), (0,)), ((), ())), preferred_element_type=jnp.float32
    )


def normalize_rows(values):
    widened = values.astype(jnp.float32)
    square_sum = jnp.sum(widened * widened, axis=1, keepdims=True)
    inverse_norm = lax.rsqrt(square_sum + 1e-06)
    return (widened * inverse_norm).astype(jnp.bfloat16)


def best_match(queries, query_ids, query_start, key_units, key_ids):
    similarity = lax.dot_general(
        queries, key_units, (((1,), (1,)), ((), ())), preferred_element_type=jnp.float32
    )
    query_pos = query_start + jnp.arange(queries.shape[0], dtype=jnp.int32)
    key_pos = jnp.arange(key_units.shape[0], dtype=jnp.int32)
    same_cluster = (
        (query_ids[:, None] == key_ids[None, :])
        & (query_ids[:, None] >= 0)
        & (query_pos[:, None] != key_pos[None, :])
    )
    return jnp.max(jnp.where(same_cluster, similarity, -1.0), axis=1)


def whitening_of(moments, row_total):
    identity = jnp.eye(moments.shape[0], dtype=jnp.float32)
    chol_factor = jnp.linalg.cholesky(moments / float(row_total) + 0.001 * identity)
    return jax.scipy.linalg.solve_triangular(chol_factor, identity, lower=True).astype(
        jnp.bfloat16
    )


def exchange(value, axis, flip):
    return lax.ppermute(value, axis, [(i, i ^ flip) for i in range(lax.axis_size(axis))])


def local_gathered(embeddings, cluster_ids):
    row_count = embeddings.shape[0]
    dp_count = lax.axis_size("dp")
    mp_index = lax.axis_index("mp")
    core, side = mp_index % 2, mp_index // 2
    half, quarter = row_count // 2, row_count // 4

    own_half = lax.dynamic_slice_in_dim(embeddings, core * half, half, 0)
    own_quarter = lax.dynamic_slice_in_dim(own_half, side * quarter, quarter, 0)
    zone = exchange(own_half, "dp", 2)
    near = exchange(own_half, "dp", 1)
    zone_near = exchange(zone, "dp", 1)
    far = jnp.concatenate([exchange(own_quarter, "dp", flip) for flip in range(4, dp_count, 2)], axis=0)
    far_near = exchange(far, "dp", 1)
    held = [near, zone, zone_near, far, exchange(far, "mp", 2), far_near, exchange(far_near, "mp", 2)]
    pieces = [embeddings] + held + [exchange(value, "mp", 1) for value in held]

    ids = cluster_ids[None]
    flip = 1
    while flip < dp_count:
        ids = jnp.concatenate([ids, exchange(ids, "dp", flip)], axis=0)
        flip *= 2

    def ids_of(sources, start, size):
        return [lax.dynamic_slice_in_dim(ids[n], start, size, 0) for n in sources]

    orders = [cluster_ids]
    for c in (core, 1 - core):
        orders += ids_of((1, 2, 3), c * half, half)
        for first in (4, 5):
            for s in (side, 1 - side):
                orders += ids_of(range(first, dp_count, 2), c * half + s * quarter, quarter)
    return scores_of(pieces, jnp.concatenate(orders))


def local_routed(embeddings, cluster_ids):
    row_count, feat_width = embeddings.shape
    dp_count = lax.axis_size("dp")
    mp_count = lax.axis_size("mp")
    mp_index = lax.axis_index("mp")
    pair_cap = 2 * row_count // dp_count
    slot_count = dp_count * pair_cap
    quarter_len = slot_count // mp_count
    col_share = feat_width // mp_count
    own_cols = lax.dynamic_slice_in_dim(embeddings, mp_index * col_share, col_share, 1)
    column_sums = lax.psum(contract_rows(embeddings, own_cols), "dp")
    moments = lax.all_gather(column_sums, "mp", axis=1, tiled=True)
    whitening = whitening_of(moments, row_count * dp_count)
    owner_ids = cluster_ids // CPO
    owner_hits = (owner_ids[:, None] == jnp.arange(dp_count, dtype=jnp.int32)[None, :]).astype(
        jnp.int32
    )
    earlier_hits = jnp.cumsum(owner_hits, axis=0) - owner_hits
    row_rank = jnp.sum(earlier_hits * owner_hits, axis=1)
    whiten_part = lax.dynamic_slice_in_dim(whitening, mp_index * col_share, col_share, 0)
    whitened = lax.dot_general(
        embeddings, whiten_part, (((1,), (1,)), ((), ())), preferred_element_type=jnp.float32
    ).astype(jnp.bfloat16)
    slot_index = owner_ids * pair_cap + row_rank
    send_rows = jnp.zeros((slot_count, col_share), jnp.bfloat16).at[slot_index].set(whitened)
    send_ids = jnp.full((slot_count,), -1, jnp.int32).at[slot_index].set(cluster_ids)
    got_rows, got_ids = (
        lax.all_to_all(send_rows, "dp", split_axis=0, concat_axis=0, tiled=True),
        lax.all_to_all(send_ids, "dp", split_axis=0, concat_axis=0, tiled=True),
    )
    key_rows = lax.all_gather(got_rows, "mp", axis=1, tiled=True)
    unit = normalize_rows(key_rows)
    query_start = mp_index * quarter_len
    queries = lax.dynamic_slice_in_dim(unit, query_start, quarter_len, 0)
    query_ids = lax.dynamic_slice_in_dim(got_ids, query_start, quarter_len, 0)
    best_score = best_match(queries, query_ids, query_start, unit, got_ids)
    all_scores = lax.all_gather(best_score, "mp", axis=0, tiled=True)
    returned = lax.all_to_all(all_scores, "dp", split_axis=0, concat_axis=0, tiled=True)
    return returned[slot_index]


def local(embeddings, cluster_ids):
    gathered_bytes = embeddings.size * 2 * lax.axis_size("dp")
    if gathered_bytes <= GATHER_LIMIT and lax.axis_size("mp") == 4:
        return local_gathered(embeddings, cluster_ids)
    return local_routed(embeddings, cluster_ids)


def solution(mesh):
    in_specs = (P("dp", None), P("dp"))
    out_specs = P("dp")
    return jax.shard_map(local, mesh=mesh, in_specs=in_specs, out_specs=out_specs, check_vma=False)
```

```python
import functools
import jax
import jax.numpy as jnp
from jax import lax
from jax.experimental import pallas as pl
from jax.experimental.pallas import tpu as pltpu
from jax.sharding import PartitionSpec as P

CPO = 4
GATHER_LIMIT = 8 * 1024 * 1024
EXACT_IDS = 256
BLK = 128
SUB = 8
PANEL = 256


def refine(value):
    guess = pl.reciprocal(value, approx=True)
    return guess * (2.0 - value * guess)


def invert_factor(block, jobs):
    shape = (SUB, BLK)
    lane = lax.broadcasted_iota(jnp.int32, shape, 1)
    sub = lax.broadcasted_iota(jnp.int32, shape, 0)
    count = BLK // SUB
    slots = count * SUB // 2
    jobs = list(jobs)
    total = len(jobs)
    rows = [block[SUB * i : SUB * (i + 1), :] for i in range(count)]

    def spread(i, at):
        return [jnp.broadcast_to(rows[i][:, at + q : at + q + 1], shape) for q in range(SUB)]

    def line(value, p):
        return jnp.broadcast_to(value[p : p + 1, :], shape)

    def follow(i, first, steps):
        cols = spread(i, first)
        value = jnp.where((lane >= first) & (lane < first + SUB), 0.0, rows[i])
        for p, (inverse, tops, pivot_row) in enumerate(steps):
            factor = cols[p] * inverse
            for q in range(p + 1, SUB):
                cols[q] = cols[q] - factor * tops[q]
            value = value - factor * pivot_row
        rows[i] = value

    def follow_far(i, first, flipped, lines):
        value = jnp.where((lane >= first) & (lane < first + SUB), 0.0, rows[i])
        for p in range(SUB):
            factor = jnp.broadcast_to(flipped[SUB * i : SUB * (i + 1), p : p + 1], shape)
            value = value - factor * lines[p]
        rows[i] = value

    done = []
    late = []
    cols = spread(0, 0)
    for t in range(count):
        first = SUB * t
        here = (lane >= first) & (lane < first + SUB)
        close = [i for i in (t + 1,) if i < count]
        close_cols = {i: spread(i, first) for i in close}
        rows[t] = jnp.where(here, (lane - first == sub).astype(jnp.float32), rows[t])
        for i in close:
            rows[i] = jnp.where(here, 0.0, rows[i])
        pivots = jnp.ones(shape, jnp.float32)
        steps = []
        late_total = len(late)
        for p in range(0, SUB, 2):
            first_pivot, cross = line(cols[p], p), line(cols[p + 1], p)
            cross_low, corner = line(cols[p], p + 1), line(cols[p + 1], p + 1)
            det = first_pivot * corner - cross * cross_low
            inv1 = refine(first_pivot)
            guess = pl.reciprocal(det, approx=True)
            inv2 = (first_pivot * guess) * (2.0 - det * guess)
            below1 = jnp.where(sub > p, cols[p], 0.0)
            factor1 = below1 * inv1
            factor2 = jnp.where(sub > p + 1, cols[p + 1] - (below1 * cross) * inv1, 0.0) * inv2
            top1 = {q: line(cols[q], p) for q in range(p + 2, SUB)}
            top2 = {q: line(cols[q], p + 1) - (cross_low * top1[q]) * inv1 for q in range(p + 2, SUB)}
            for q in range(p + 2, SUB):
                cols[q] = (cols[q] - factor1 * top1[q]) - factor2 * top2[q]
            low = cross_low * inv1
            row1 = line(rows[t], p)
            row2 = line(rows[t], p + 1) - low * row1
            rows[t] = (rows[t] - factor1 * row1) - factor2 * row2
            pivots = jnp.where(sub == p, first_pivot, jnp.where(sub == p + 1, det * inv1, pivots))
            top1[p + 1] = cross
            steps += [(inv1, top1, row1), (inv2, top2, row2)]
            for i in close:
                values = close_cols[i]
                near1 = values[p] * inv1
                near2 = (values[p + 1] - near1 * cross) * inv2
                for q in range(p + 2, SUB):
                    values[q] = (values[q] - near1 * top1[q]) - near2 * top2[q]
                rows[i] = (rows[i] - near1 * row1) - near2 * row2
            for _ in range(late_total * (p + 2) // SUB - late_total * p // SUB):
                late.pop(0)()
            slot = (t * SUB + p) // 2
            for job in jobs[total * slot // slots : total * (slot + 1) // slots]:
                job()
        scale = lax.rsqrt(pivots)
        scale = scale * (1.5 - 0.5 * pivots * scale * scale)
        scaled = rows[t] * scale
        done.append(jnp.where(lane <= first + sub, scaled, 0.0))
        if close:
            cols = spread(t + 1, first + SUB)
        if t + 2 < count:
            follow(t + 2, first, steps)
        if t + 3 < count:
            flipped = scaled.T
            lines = [line(scaled, p) for p in range(SUB)]
            late += [functools.partial(follow_far, i, first, flipped, lines) for i in range(t + 3, count)]
    return jnp.concatenate(done, axis=0)


def dot_nn(a, b):
    return lax.dot_general(a, b, (((1,), (0,)), ((), ())), preferred_element_type=jnp.float32)


def dot_nt(a, b):
    return lax.dot_general(a, b, (((1,), (1,)), ((), ())), preferred_element_type=jnp.float32)


def split(value):
    high = value.astype(jnp.bfloat16)
    rest = value - high.astype(jnp.float32)
    mid = rest.astype(jnp.bfloat16)
    return high, mid, (rest - mid.astype(jnp.float32)).astype(jnp.bfloat16)


def as_left(terms):
    a, b, c = terms
    return jnp.concatenate([a, a, b, b, a, c], axis=1)


def as_right(terms, axis):
    a, b, c = terms
    return jnp.concatenate([a, b, a, b, c, a], axis=axis)


def score_kernel(own, rows, ids_ref, out_ref, flipped, work, left, right, below, white, own_white, sims, sums):
    row_total, width = rows.shape
    count = width // BLK
    blocks = [slice(BLK * n, BLK * (n + 1)) for n in range(count)]
    chunks = [slice(n, n + own) for n in range(0, row_total, own)]

    def flip_columns(at, size):
        flipped[at : at + size, :] = rows[:, at : at + size].T

    def moments_of(at, size, to, to_size):
        mean = dot_nn(flipped[at : at + size, :], rows[:, to : to + to_size]) * (1.0 / row_total)
        if at < to + to_size:
            shape = (size, to_size)
            row_i = at + lax.broadcasted_iota(jnp.int32, shape, 0)
            col_i = to + lax.broadcasted_iota(jnp.int32, shape, 1)
            mean = mean + jnp.where(row_i == col_i, 0.001, 0.0)
        work[at : at + size, to : to + to_size] = mean

    def mask_of(at):
        own_col = jnp.broadcast_to(ids_ref[:, 0:own], (BLK, own)).T[:, 0:1]
        same = own_col == ids_ref[:, at : at + BLK]
        if at < own:
            own_pos = lax.broadcasted_iota(jnp.int32, (own, BLK), 0)
            same = same & (own_pos != at + lax.broadcasted_iota(jnp.int32, (own, BLK), 1))
        sims[:, at : at + BLK] = jnp.where(same, 0.0, -1e30)

    def first_jobs():
        jobs = [functools.partial(flip_columns, BLK, PANEL - BLK)]
        jobs.append(functools.partial(moments_of, BLK, PANEL - BLK, 0, PANEL))
        for at in range(PANEL, width, PANEL):
            jobs.append(functools.partial(flip_columns, at, PANEL))
            jobs += [functools.partial(moments_of, at, PANEL, to, PANEL) for to in range(0, at + PANEL, PANEL)]
        return jobs + [functools.partial(mask_of, at) for at in range(0, row_total, BLK)]

    def left_of(n, h, inverse_right):
        terms = split(dot_nt(as_left(split(work[blocks[n], blocks[h]])), inverse_right))
        left[blocks[n], :] = as_left(terms)
        right[blocks[n], :] = as_right(terms, 1)

    def below_of(j, h, inverse_left):
        value = dot_nn(inverse_left, as_right(split(work[blocks[h], blocks[j]]), 0))
        below[:, blocks[j]] = as_right(split(value), 0)
        white[blocks[h % 4], blocks[j]] = value.astype(jnp.bfloat16)

    def reduce_right(n, j):
        work[blocks[n], blocks[j]] -= dot_nt(left[blocks[n], :], right[blocks[j], :])

    def reduce_left(n, h):
        if h > 0:
            done = slice(0, BLK * h)
            work[blocks[n], done] -= dot_nn(left[blocks[n], :], below[:, done])
        work[blocks[n], blocks[h]] = -dot_nn(left[blocks[n], :], below[:, blocks[h]])

    def whiten(c, h, begin, size):
        feats = slice(0, BLK * (h + 1))
        whitened = dot_nt(rows[chunks[c], feats], white[begin : begin + size, feats]).astype(jnp.bfloat16)
        if c == 0:
            own_white[:, 0:size] = whitened
        sims[:, chunks[c]] += dot_nt(own_white[:, 0:size], whitened)
        squares = whitened.astype(jnp.float32)
        squares = squares * squares
        squares = sum(squares[:, n : n + BLK] for n in range(0, size, BLK))
        sums[chunks[c], :] = squares if h < 2 else sums[chunks[c], :] + squares

    def finish_rows(h, inverse):
        white[blocks[h % 4], blocks[h]] = inverse.astype(jnp.bfloat16)
        terms = split(inverse)
        below[:, blocks[h]] = as_right(terms, 0)
        jobs = [functools.partial(below_of, j, h, as_left(terms)) for j in range(h)]
        if h >= count - 2:
            return jobs, [functools.partial(whiten, c, h, BLK * (h % 4), BLK) for c in range(len(chunks))]
        if h % 2 == 0:
            white[blocks[h % 4], blocks[h + 1]] = jnp.zeros((BLK, BLK), jnp.bfloat16)
            return jobs, []
        return jobs, [functools.partial(whiten, c, h, BLK * (h % 4 - 1), 2 * BLK) for c in range(len(chunks))]

    flip_columns(0, BLK)
    moments_of(0, BLK, 0, BLK)
    block = work[blocks[0], blocks[0]]
    jobs = first_jobs()
    waiting = []
    for k in range(count):
        inverse = invert_factor(block, jobs)
        jobs, white_jobs = finish_rows(k, inverse)
        if k + 1 == count:
            break
        terms = split(inverse)
        inverse_right = as_right(terms, 1)
        nexts = blocks[k + 1]
        terms = split(dot_nt(as_left(split(work[nexts, blocks[k]])), inverse_right))
        value_left, value_right = as_left(terms), as_right(terms, 1)
        block = work[nexts, nexts] - dot_nt(value_left, value_right)
        left[nexts, :] = value_left
        right[nexts, :] = value_right
        later = range(k + 2, count)
        jobs += [functools.partial(left_of, n, k, inverse_right) for n in later]
        jobs += [functools.partial(reduce_left, n, k) for n in range(k + 1, count)]
        jobs += [functools.partial(reduce_right, n, j) for n in later for j in range(k + 1, n + 1)]
        if k % 2 == 1 and white_jobs:
            waiting = white_jobs[len(white_jobs) // 2 :]
            jobs += white_jobs[: len(white_jobs) // 2]
        else:
            jobs += waiting + white_jobs
            waiting = []
    for job in jobs + white_jobs:
        job()

    best = jnp.full((own, BLK), -1e30, jnp.float32)
    for at in range(0, row_total, BLK):
        key_sum = jnp.sum(sums[at : at + BLK, :].T, axis=0, keepdims=True)
        best = jnp.maximum(best, sims[:, at : at + BLK] * lax.rsqrt(key_sum + 1e-06))
    top = jnp.max(best, axis=1, keepdims=True)
    own_sum = jnp.sum(sums[0:own, :], axis=1, keepdims=True)
    top = jnp.where(top < -1e20, -1.0, jnp.maximum(top * lax.rsqrt(own_sum + 1e-06), -1.0))
    out_ref[...] = jnp.broadcast_to(top, (own, BLK)).T[0:1, :]


def scores_of(rows, ids, own):
    row_total, width = rows.shape
    vmem = pl.BlockSpec(memory_space=pltpu.VMEM)
    out = pl.pallas_call(
        functools.partial(score_kernel, own),
        out_shape=jax.ShapeDtypeStruct((1, own), jnp.float32),
        in_specs=[vmem, vmem],
        out_specs=vmem,
        scratch_shapes=[
            pltpu.VMEM((width, row_total), jnp.bfloat16),
            pltpu.VMEM((width, width), jnp.float32),
            pltpu.VMEM((width, 6 * BLK), jnp.bfloat16),
            pltpu.VMEM((width, 6 * BLK), jnp.bfloat16),
            pltpu.VMEM((6 * BLK, width), jnp.bfloat16),
            pltpu.VMEM((4 * BLK, width), jnp.bfloat16),
            pltpu.VMEM((own, 2 * BLK), jnp.bfloat16),
            pltpu.VMEM((own, row_total), jnp.float32),
            pltpu.VMEM((row_total, BLK), jnp.float32),
        ],
        compiler_params=pltpu.CompilerParams(vmem_limit_bytes=40 * 1024 * 1024),
    )(rows, ids.reshape(1, -1))
    return out.reshape(own)


def contract_rows(left_rows, right_rows):
    return lax.dot_general(
        left_rows, right_rows, (((0,), (0,)), ((), ())), preferred_element_type=jnp.float32
    )


def normalize_rows(values):
    widened = values.astype(jnp.float32)
    square_sum = jnp.sum(widened * widened, axis=1, keepdims=True)
    inverse_norm = lax.rsqrt(square_sum + 1e-06)
    return (widened * inverse_norm).astype(jnp.bfloat16)


def best_match(queries, query_ids, query_start, key_units, key_ids):
    similarity = lax.dot_general(
        queries, key_units, (((1,), (1,)), ((), ())), preferred_element_type=jnp.float32
    )
    query_pos = query_start + jnp.arange(queries.shape[0], dtype=jnp.int32)
    key_pos = jnp.arange(key_units.shape[0], dtype=jnp.int32)
    same_cluster = (
        (query_ids[:, None] == key_ids[None, :])
        & (query_ids[:, None] >= 0)
        & (query_pos[:, None] != key_pos[None, :])
    )
    return jnp.max(jnp.where(same_cluster, similarity, -1.0), axis=1)


def whitening_of(moments, row_total):
    identity = jnp.eye(moments.shape[0], dtype=jnp.float32)
    chol_factor = jnp.linalg.cholesky(moments / float(row_total) + 0.001 * identity)
    return jax.scipy.linalg.solve_triangular(chol_factor, identity, lower=True).astype(
        jnp.bfloat16
    )


def exchange(value, axis, flip):
    return lax.ppermute(value, axis, [(i, i ^ flip) for i in range(lax.axis_size(axis))])


def local_gathered(embeddings, cluster_ids):
    row_count, width = embeddings.shape
    dp_count = lax.axis_size("dp")
    mp_index = lax.axis_index("mp")
    core, side = mp_index % 2, mp_index // 2
    half, quarter = row_count // 2, row_count // 4

    tag = jnp.pad(cluster_ids.astype(jnp.bfloat16)[None], ((0, SUB - 1), (0, width - row_count)))
    own_half = lax.optimization_barrier(lax.dynamic_slice_in_dim(embeddings, core * half, half, 0))
    own_quarter = lax.dynamic_slice_in_dim(own_half, side * quarter, quarter, 0)
    tagged_quarter = jnp.concatenate([own_quarter, tag], axis=0)
    tagged_half = jnp.concatenate([own_half, tag], axis=0)
    far_flips = range(4, dp_count, 2)
    far = jnp.concatenate([exchange(tagged_quarter, "dp", flip) for flip in far_flips], axis=0)
    near = exchange(tagged_half, "dp", 1)
    zone = exchange(tagged_half, "dp", 2)
    far_near = exchange(far, "dp", 1)
    zone_near = exchange(zone, "dp", 1)

    step = quarter + SUB
    cut = lambda value: jnp.concatenate([value[n : n + quarter] for n in range(0, value.shape[0], step)], axis=0)
    far_rows, far_near_rows = cut(far), cut(far_near)
    first = jnp.concatenate([near[:half], zone[:half], far_rows], axis=0)
    second = jnp.concatenate([zone_near[:half], exchange(far_rows, "mp", 2), far_near_rows], axis=0)
    third = exchange(far_near_rows, "mp", 2)
    held = [first, second, third]
    rows = jnp.concatenate([embeddings] + held + [exchange(value, "mp", 1) for value in held], axis=0)

    def ids_in(value, at):
        return value[at, :row_count].astype(jnp.int32)

    near_ids, zone_ids, zone_near_ids = (ids_in(value, half) for value in (near, zone, zone_near))
    far_ids = [ids_in(far, n + quarter) for n in range(0, far.shape[0], step)]
    far_near_ids = [ids_in(far_near, n + quarter) for n in range(0, far.shape[0], step)]

    def of_half(value, c):
        return [lax.dynamic_slice_in_dim(value, c * half, half, 0)]

    def of_quarter(values, c, s):
        return [lax.dynamic_slice_in_dim(value, c * half + s * quarter, quarter, 0) for value in values]

    ids = [cluster_ids]
    for c in (core, 1 - core):
        ids += of_half(near_ids, c) + of_half(zone_ids, c) + of_quarter(far_ids, c, side)
        ids += of_half(zone_near_ids, c) + of_quarter(far_ids, c, 1 - side) + of_quarter(far_near_ids, c, side)
        ids += of_quarter(far_near_ids, c, 1 - side)
    return scores_of(rows, jnp.concatenate(ids), row_count)


def local_routed(embeddings, cluster_ids):
    row_count, feat_width = embeddings.shape
    dp_count = lax.axis_size("dp")
    mp_count = lax.axis_size("mp")
    mp_index = lax.axis_index("mp")
    pair_cap = 2 * row_count // dp_count
    slot_count = dp_count * pair_cap
    quarter_len = slot_count // mp_count
    col_share = feat_width // mp_count
    own_cols = lax.dynamic_slice_in_dim(embeddings, mp_index * col_share, col_share, 1)
    column_sums = lax.psum(contract_rows(embeddings, own_cols), "dp")
    moments = lax.all_gather(column_sums, "mp", axis=1, tiled=True)
    whitening = whitening_of(moments, row_count * dp_count)
    owner_ids = cluster_ids // CPO
    owner_hits = (owner_ids[:, None] == jnp.arange(dp_count, dtype=jnp.int32)[None, :]).astype(
        jnp.int32
    )
    earlier_hits = jnp.cumsum(owner_hits, axis=0) - owner_hits
    row_rank = jnp.sum(earlier_hits * owner_hits, axis=1)
    whiten_part = lax.dynamic_slice_in_dim(whitening, mp_index * col_share, col_share, 0)
    whitened = lax.dot_general(
        embeddings, whiten_part, (((1,), (1,)), ((), ())), preferred_element_type=jnp.float32
    ).astype(jnp.bfloat16)
    slot_index = owner_ids * pair_cap + row_rank
    send_rows = jnp.zeros((slot_count, col_share), jnp.bfloat16).at[slot_index].set(whitened)
    send_ids = jnp.full((slot_count,), -1, jnp.int32).at[slot_index].set(cluster_ids)
    got_rows, got_ids = (
        lax.all_to_all(send_rows, "dp", split_axis=0, concat_axis=0, tiled=True),
        lax.all_to_all(send_ids, "dp", split_axis=0, concat_axis=0, tiled=True),
    )
    key_rows = lax.all_gather(got_rows, "mp", axis=1, tiled=True)
    unit = normalize_rows(key_rows)
    query_start = mp_index * quarter_len
    queries = lax.dynamic_slice_in_dim(unit, query_start, quarter_len, 0)
    query_ids = lax.dynamic_slice_in_dim(got_ids, query_start, quarter_len, 0)
    best_score = best_match(queries, query_ids, query_start, unit, got_ids)
    all_scores = lax.all_gather(best_score, "mp", axis=0, tiled=True)
    returned = lax.all_to_all(all_scores, "dp", split_axis=0, concat_axis=0, tiled=True)
    return returned[slot_index]


def local(embeddings, cluster_ids):
    row_count, feat_width = embeddings.shape
    owners = lax.axis_size("dp")
    fits = embeddings.size * 2 * owners <= GATHER_LIMIT and row_count <= feat_width
    if fits and lax.axis_size("mp") == 4 and owners * CPO <= EXACT_IDS:
        return local_gathered(embeddings, cluster_ids)
    return local_routed(embeddings, cluster_ids)


def solution(mesh):
    in_specs = (P("dp", None), P("dp"))
    out_specs = P("dp")
    return jax.shard_map(local, mesh=mesh, in_specs=in_specs, out_specs=out_specs, check_vma=False)
```

```python
import functools
import jax
import jax.numpy as jnp
from jax import lax
from jax.experimental import pallas as pl
from jax.experimental.pallas import tpu as pltpu
from jax.sharding import PartitionSpec as P

CPO = 4
GATHER_LIMIT = 8 * 1024 * 1024
BLK = 128
SUB = 8
PANEL = 256


def refine(value):
    guess = pl.reciprocal(value, approx=True)
    return guess * (2.0 - value * guess)


def invert_factor(block, jobs):
    shape = (SUB, BLK)
    lane = lax.broadcasted_iota(jnp.int32, shape, 1)
    sub = lax.broadcasted_iota(jnp.int32, shape, 0)
    count = BLK // SUB
    slots = count * SUB // 2
    jobs = list(jobs)
    total = len(jobs)
    rows = [block[SUB * i : SUB * (i + 1), :] for i in range(count)]

    def spread(i, at):
        return [jnp.broadcast_to(rows[i][:, at + q : at + q + 1], shape) for q in range(SUB)]

    def line(value, p):
        return jnp.broadcast_to(value[p : p + 1, :], shape)

    def follow(i, first, steps):
        cols = spread(i, first)
        value = jnp.where((lane >= first) & (lane < first + SUB), 0.0, rows[i])
        for p, (inverse, tops, pivot_row) in enumerate(steps):
            factor = cols[p] * inverse
            for q in range(p + 1, SUB):
                cols[q] = cols[q] - factor * tops[q]
            value = value - factor * pivot_row
        rows[i] = value

    def follow_far(i, first, flipped, lines):
        value = jnp.where((lane >= first) & (lane < first + SUB), 0.0, rows[i])
        for p in range(SUB):
            factor = jnp.broadcast_to(flipped[SUB * i : SUB * (i + 1), p : p + 1], shape)
            value = value - factor * lines[p]
        rows[i] = value

    done = []
    late = []
    cols = spread(0, 0)
    for t in range(count):
        first = SUB * t
        here = (lane >= first) & (lane < first + SUB)
        close = [i for i in (t + 1,) if i < count]
        close_cols = {i: spread(i, first) for i in close}
        rows[t] = jnp.where(here, (lane - first == sub).astype(jnp.float32), rows[t])
        for i in close:
            rows[i] = jnp.where(here, 0.0, rows[i])
        pivots = jnp.ones(shape, jnp.float32)
        steps = []
        late_total = len(late)
        for p in range(0, SUB, 2):
            first_pivot, cross = line(cols[p], p), line(cols[p + 1], p)
            cross_low, corner = line(cols[p], p + 1), line(cols[p + 1], p + 1)
            det = first_pivot * corner - cross * cross_low
            inv1 = refine(first_pivot)
            guess = pl.reciprocal(det, approx=True)
            inv2 = (first_pivot * guess) * (2.0 - det * guess)
            below1 = jnp.where(sub > p, cols[p], 0.0)
            factor1 = below1 * inv1
            factor2 = jnp.where(sub > p + 1, cols[p + 1] - (below1 * cross) * inv1, 0.0) * inv2
            top1 = {q: line(cols[q], p) for q in range(p + 2, SUB)}
            top2 = {q: line(cols[q], p + 1) - (cross_low * top1[q]) * inv1 for q in range(p + 2, SUB)}
            for q in range(p + 2, SUB):
                cols[q] = (cols[q] - factor1 * top1[q]) - factor2 * top2[q]
            low = cross_low * inv1
            row1 = line(rows[t], p)
            row2 = line(rows[t], p + 1) - low * row1
            rows[t] = (rows[t] - factor1 * row1) - factor2 * row2
            pivots = jnp.where(sub == p, first_pivot, jnp.where(sub == p + 1, det * inv1, pivots))
            top1[p + 1] = cross
            steps += [(inv1, top1, row1), (inv2, top2, row2)]
            for i in close:
                values = close_cols[i]
                near1 = values[p] * inv1
                near2 = (values[p + 1] - near1 * cross) * inv2
                for q in range(p + 2, SUB):
                    values[q] = (values[q] - near1 * top1[q]) - near2 * top2[q]
                rows[i] = (rows[i] - near1 * row1) - near2 * row2
            for _ in range(late_total * (p + 2) // SUB - late_total * p // SUB):
                late.pop(0)()
            slot = (t * SUB + p) // 2
            for job in jobs[total * slot // slots : total * (slot + 1) // slots]:
                job()
        scale = lax.rsqrt(pivots)
        scale = scale * (1.5 - 0.5 * pivots * scale * scale)
        scaled = rows[t] * scale
        done.append(jnp.where(lane <= first + sub, scaled, 0.0))
        if close:
            cols = spread(t + 1, first + SUB)
        if t + 2 < count:
            follow(t + 2, first, steps)
        if t + 3 < count:
            flipped = scaled.T
            lines = [line(scaled, p) for p in range(SUB)]
            late += [functools.partial(follow_far, i, first, flipped, lines) for i in range(t + 3, count)]
    return jnp.concatenate(done, axis=0)


def dot_nn(a, b):
    return lax.dot_general(a, b, (((1,), (0,)), ((), ())), preferred_element_type=jnp.float32)


def dot_nt(a, b):
    return lax.dot_general(a, b, (((1,), (1,)), ((), ())), preferred_element_type=jnp.float32)


def split(value):
    high = value.astype(jnp.bfloat16)
    rest = value - high.astype(jnp.float32)
    mid = rest.astype(jnp.bfloat16)
    return high, mid, (rest - mid.astype(jnp.float32)).astype(jnp.bfloat16)


def as_left(terms):
    a, b, c = terms
    return jnp.concatenate([a, a, b, b, a, c], axis=1)


def as_right(terms, axis):
    a, b, c = terms
    return jnp.concatenate([a, b, a, b, c, a], axis=axis)


def score_kernel(sizes, *refs):
    pieces = refs[: len(sizes)]
    ids_ref, out_ref = refs[len(sizes) : len(sizes) + 2]
    rows, flipped, work, left, right, below, white, own_white, sims, sums = refs[len(sizes) + 2 :]
    row_total, width = rows.shape
    own = sizes[0]
    count = width // BLK
    blocks = [slice(BLK * n, BLK * (n + 1)) for n in range(count)]
    chunks = [slice(n, n + 2 * own) for n in range(0, row_total, 2 * own)]

    at = 0
    for size, source in zip(sizes, pieces):
        rows[at : at + size, :] = source[...]
        at += size

    def flip_columns(at, size):
        flipped[at : at + size, :] = rows[:, at : at + size].T

    def moments_of(at, size, to, to_size):
        mean = dot_nn(flipped[at : at + size, :], rows[:, to : to + to_size]) * (1.0 / row_total)
        if at < to + to_size:
            shape = (size, to_size)
            row_i = at + lax.broadcasted_iota(jnp.int32, shape, 0)
            col_i = to + lax.broadcasted_iota(jnp.int32, shape, 1)
            mean = mean + jnp.where(row_i == col_i, 0.001, 0.0)
        work[at : at + size, to : to + to_size] = mean

    def mask_of(at):
        own_col = jnp.broadcast_to(ids_ref[:, 0:own], (BLK, own)).T[:, 0:1]
        same = own_col == ids_ref[:, at : at + BLK]
        if at < own:
            own_pos = lax.broadcasted_iota(jnp.int32, (own, BLK), 0)
            same = same & (own_pos != at + lax.broadcasted_iota(jnp.int32, (own, BLK), 1))
        sims[:, at : at + BLK] = jnp.where(same, 0.0, -1e30)

    def first_jobs():
        jobs = [functools.partial(flip_columns, BLK, PANEL - BLK)]
        jobs.append(functools.partial(moments_of, BLK, PANEL - BLK, 0, PANEL))
        jobs += [functools.partial(flip_columns, at, PANEL) for at in range(PANEL, width, PANEL)]
        for to in range(0, width, PANEL):
            at = max(to, PANEL)
            jobs.append(functools.partial(moments_of, at, width - at, to, PANEL))
        return jobs + [functools.partial(mask_of, at) for at in range(0, row_total, BLK)]

    def left_of(begin, h, inverse_right):
        terms = split(dot_nt(as_left(split(work[begin:width, blocks[h]])), inverse_right))
        left[begin:width, :] = as_left(terms)
        right[begin:width, :] = as_right(terms, 1)

    def below_of(h, inverse_left):
        known = slice(0, BLK * h)
        value = dot_nn(inverse_left, as_right(split(work[blocks[h], known]), 0))
        below[:, known] = as_right(split(value), 0)
        white[blocks[h % 4], known] = value.astype(jnp.bfloat16)

    def reduce_left(begin, h):
        known = slice(0, BLK * (h + 1))
        work[begin:width, blocks[h]] = jnp.zeros((width - begin, BLK), jnp.float32)
        work[begin:width, known] -= dot_nn(left[begin:width, :], below[:, known])

    def reduce_right(begin, size):
        work[begin:width, begin : begin + size] -= dot_nt(left[begin:width, :], right[begin : begin + size, :])

    def whiten(c, h, begin, size):
        feats = slice(0, BLK * (h + 1))
        whitened = dot_nt(rows[chunks[c], feats], white[begin : begin + size, feats]).astype(jnp.bfloat16)
        if c == 0:
            own_white[:, 0:size] = whitened[0:own, :]
        sims[:, chunks[c]] += dot_nt(own_white[:, 0:size], whitened)
        squares = whitened.astype(jnp.float32)
        squares = squares * squares
        squares = sum(squares[:, n : n + BLK] for n in range(0, size, BLK))
        sums[chunks[c], :] = squares if h < 2 else sums[chunks[c], :] + squares

    def finish_rows(h, inverse):
        white[blocks[h % 4], blocks[h]] = inverse.astype(jnp.bfloat16)
        terms = split(inverse)
        below[:, blocks[h]] = as_right(terms, 0)
        jobs = [functools.partial(below_of, h, as_left(terms))] if h else []
        if h >= count - 2:
            return jobs, [functools.partial(whiten, c, h, BLK * (h % 4), BLK) for c in range(len(chunks))]
        if h % 2 == 0:
            white[blocks[h % 4], blocks[h + 1]] = jnp.zeros((BLK, BLK), jnp.bfloat16)
            return jobs, []
        return jobs, [functools.partial(whiten, c, h, BLK * (h % 4 - 1), 2 * BLK) for c in range(len(chunks))]

    flip_columns(0, BLK)
    moments_of(0, BLK, 0, BLK)
    block = work[blocks[0], blocks[0]]
    jobs = first_jobs()
    waiting = []
    for k in range(count):
        inverse = invert_factor(block, jobs)
        jobs, white_jobs = finish_rows(k, inverse)
        if k + 1 == count:
            break
        terms = split(inverse)
        inverse_right = as_right(terms, 1)
        nexts = blocks[k + 1]
        terms = split(dot_nt(as_left(split(work[nexts, blocks[k]])), inverse_right))
        value_left, value_right = as_left(terms), as_right(terms, 1)
        block = work[nexts, nexts] - dot_nt(value_left, value_right)
        left[nexts, :] = value_left
        right[nexts, :] = value_right
        begin = BLK * (k + 1)
        if begin + BLK < width:
            jobs.append(functools.partial(left_of, begin + BLK, k, inverse_right))
            for at in range(begin, width, PANEL):
                jobs.append(functools.partial(reduce_right, at, min(PANEL, width - at)))
        jobs.append(functools.partial(reduce_left, begin, k))
        if k % 2 == 1 and white_jobs:
            waiting = white_jobs[len(white_jobs) // 2 :]
            jobs += white_jobs[: len(white_jobs) // 2]
        else:
            jobs += waiting + white_jobs
            waiting = []
    for job in jobs + white_jobs:
        job()

    best = jnp.full((own, BLK), -1e30, jnp.float32)
    for at in range(0, row_total, BLK):
        key_sum = jnp.sum(sums[at : at + BLK, :].T, axis=0, keepdims=True)
        best = jnp.maximum(best, sims[:, at : at + BLK] * lax.rsqrt(key_sum + 1e-06))
    top = jnp.max(best, axis=1, keepdims=True)
    own_sum = jnp.sum(sums[0:own, :], axis=1, keepdims=True)
    top = jnp.where(top < -1e20, -1.0, jnp.maximum(top * lax.rsqrt(own_sum + 1e-06), -1.0))
    out_ref[...] = jnp.broadcast_to(top, (own, BLK)).T[0:1, :]


def scores_of(pieces, ids):
    sizes = tuple(piece.shape[0] for piece in pieces)
    row_total, width, own = sum(sizes), pieces[0].shape[1], sizes[0]
    vmem = pl.BlockSpec(memory_space=pltpu.VMEM)
    out = pl.pallas_call(
        functools.partial(score_kernel, sizes),
        out_shape=jax.ShapeDtypeStruct((1, own), jnp.float32),
        in_specs=[vmem] * (len(sizes) + 1),
        out_specs=vmem,
        scratch_shapes=[
            pltpu.VMEM((row_total, width), jnp.bfloat16),
            pltpu.VMEM((width, row_total), jnp.bfloat16),
            pltpu.VMEM((width, width), jnp.float32),
            pltpu.VMEM((width, 6 * BLK), jnp.bfloat16),
            pltpu.VMEM((width, 6 * BLK), jnp.bfloat16),
            pltpu.VMEM((6 * BLK, width), jnp.bfloat16),
            pltpu.VMEM((4 * BLK, width), jnp.bfloat16),
            pltpu.VMEM((own, 2 * BLK), jnp.bfloat16),
            pltpu.VMEM((own, row_total), jnp.float32),
            pltpu.VMEM((row_total, BLK), jnp.float32),
        ],
        compiler_params=pltpu.CompilerParams(vmem_limit_bytes=32 * 1024 * 1024),
    )(*pieces, ids.reshape(1, -1))
    return out.reshape(own)


def contract_rows(left_rows, right_rows):
    return lax.dot_general(
        left_rows, right_rows, (((0,), (0,)), ((), ())), preferred_element_type=jnp.float32
    )


def normalize_rows(values):
    widened = values.astype(jnp.float32)
    square_sum = jnp.sum(widened * widened, axis=1, keepdims=True)
    inverse_norm = lax.rsqrt(square_sum + 1e-06)
    return (widened * inverse_norm).astype(jnp.bfloat16)


def best_match(queries, query_ids, query_start, key_units, key_ids):
    similarity = lax.dot_general(
        queries, key_units, (((1,), (1,)), ((), ())), preferred_element_type=jnp.float32
    )
    query_pos = query_start + jnp.arange(queries.shape[0], dtype=jnp.int32)
    key_pos = jnp.arange(key_units.shape[0], dtype=jnp.int32)
    same_cluster = (
        (query_ids[:, None] == key_ids[None, :])
        & (query_ids[:, None] >= 0)
        & (query_pos[:, None] != key_pos[None, :])
    )
    return jnp.max(jnp.where(same_cluster, similarity, -1.0), axis=1)


def whitening_of(moments, row_total):
    identity = jnp.eye(moments.shape[0], dtype=jnp.float32)
    chol_factor = jnp.linalg.cholesky(moments / float(row_total) + 0.001 * identity)
    return jax.scipy.linalg.solve_triangular(chol_factor, identity, lower=True).astype(
        jnp.bfloat16
    )


def exchange(value, axis, flip):
    return lax.ppermute(value, axis, [(i, i ^ flip) for i in range(lax.axis_size(axis))])


def local_gathered(embeddings, cluster_ids):
    row_count = embeddings.shape[0]
    dp_count = lax.axis_size("dp")
    mp_index = lax.axis_index("mp")
    core, side = mp_index % 2, mp_index // 2
    half, quarter = row_count // 2, row_count // 4

    own_half = lax.dynamic_slice_in_dim(embeddings, core * half, half, 0)
    own_quarter = lax.dynamic_slice_in_dim(own_half, side * quarter, quarter, 0)
    zone = exchange(own_half, "dp", 2)
    near = exchange(own_half, "dp", 1)
    zone_near = exchange(zone, "dp", 1)
    far = jnp.concatenate([exchange(own_quarter, "dp", flip) for flip in range(4, dp_count, 2)], axis=0)
    far_near = exchange(far, "dp", 1)
    held = [near, zone, zone_near, far, exchange(far, "mp", 2), far_near, exchange(far_near, "mp", 2)]
    pieces = [embeddings] + held + [exchange(value, "mp", 1) for value in held]

    def arrived(value):
        return (value[0, 0] != value[0, 0]).astype(jnp.int32)

    ids = cluster_ids[None]
    for flip, stage in ((2, None), (4, far), (1, far_near)):
        if stage is not None:
            ids = ids + arrived(stage)
        ids = jnp.concatenate([ids, exchange(ids, "dp", flip)], axis=0)
    place = {0: 0, 2: 1, 4: 2, 6: 3, 1: 4, 3: 5, 5: 6, 7: 7}

    def ids_of(sources, start, size):
        return [lax.dynamic_slice_in_dim(ids[place[n]], start, size, 0) for n in sources]

    orders = [cluster_ids]
    for c in (core, 1 - core):
        orders += ids_of((1, 2, 3), c * half, half)
        for first in (4, 5):
            for s in (side, 1 - side):
                orders += ids_of(range(first, dp_count, 2), c * half + s * quarter, quarter)
    return scores_of(pieces, jnp.concatenate(orders))


def local_routed(embeddings, cluster_ids):
    row_count, feat_width = embeddings.shape
    dp_count = lax.axis_size("dp")
    mp_count = lax.axis_size("mp")
    mp_index = lax.axis_index("mp")
    pair_cap = 2 * row_count // dp_count
    slot_count = dp_count * pair_cap
    quarter_len = slot_count // mp_count
    col_share = feat_width // mp_count
    own_cols = lax.dynamic_slice_in_dim(embeddings, mp_index * col_share, col_share, 1)
    column_sums = lax.psum(contract_rows(embeddings, own_cols), "dp")
    moments = lax.all_gather(column_sums, "mp", axis=1, tiled=True)
    whitening = whitening_of(moments, row_count * dp_count)
    owner_ids = cluster_ids // CPO
    owner_hits = (owner_ids[:, None] == jnp.arange(dp_count, dtype=jnp.int32)[None, :]).astype(
        jnp.int32
    )
    earlier_hits = jnp.cumsum(owner_hits, axis=0) - owner_hits
    row_rank = jnp.sum(earlier_hits * owner_hits, axis=1)
    whiten_part = lax.dynamic_slice_in_dim(whitening, mp_index * col_share, col_share, 0)
    whitened = lax.dot_general(
        embeddings, whiten_part, (((1,), (1,)), ((), ())), preferred_element_type=jnp.float32
    ).astype(jnp.bfloat16)
    slot_index = owner_ids * pair_cap + row_rank
    send_rows = jnp.zeros((slot_count, col_share), jnp.bfloat16).at[slot_index].set(whitened)
    send_ids = jnp.full((slot_count,), -1, jnp.int32).at[slot_index].set(cluster_ids)
    got_rows, got_ids = (
        lax.all_to_all(send_rows, "dp", split_axis=0, concat_axis=0, tiled=True),
        lax.all_to_all(send_ids, "dp", split_axis=0, concat_axis=0, tiled=True),
    )
    key_rows = lax.all_gather(got_rows, "mp", axis=1, tiled=True)
    unit = normalize_rows(key_rows)
    query_start = mp_index * quarter_len
    queries = lax.dynamic_slice_in_dim(unit, query_start, quarter_len, 0)
    query_ids = lax.dynamic_slice_in_dim(got_ids, query_start, quarter_len, 0)
    best_score = best_match(queries, query_ids, query_start, unit, got_ids)
    all_scores = lax.all_gather(best_score, "mp", axis=0, tiled=True)
    returned = lax.all_to_all(all_scores, "dp", split_axis=0, concat_axis=0, tiled=True)
    return returned[slot_index]


def local(embeddings, cluster_ids):
    owners = lax.axis_size("dp")
    fits = embeddings.size * 2 * owners <= GATHER_LIMIT
    if fits and lax.axis_size("mp") == 4 and owners == 8:
        return local_gathered(embeddings, cluster_ids)
    return local_routed(embeddings, cluster_ids)


def solution(mesh):
    in_specs = (P("dp", None), P("dp"))
    out_specs = P("dp")
    return jax.shard_map(local, mesh=mesh, in_specs=in_specs, out_specs=out_specs, check_vma=False)
```

```python
import functools
import jax
import jax.numpy as jnp
from jax import lax
from jax.experimental import pallas as pl
from jax.experimental.pallas import tpu as pltpu
from jax.sharding import PartitionSpec as P

CPO = 4
GATHER_LIMIT = 8 * 1024 * 1024
BLK = 128
SUB = 8
PANEL = 256


def refine(value):
    guess = pl.reciprocal(value, approx=True)
    return guess * (2.0 - value * guess)


def invert_factor(block, jobs):
    shape = (SUB, BLK)
    lane = lax.broadcasted_iota(jnp.int32, shape, 1)
    sub = lax.broadcasted_iota(jnp.int32, shape, 0)
    count = BLK // SUB
    slots = count * SUB // 2
    jobs = list(jobs)
    total = len(jobs)
    rows = [block[SUB * i : SUB * (i + 1), :] for i in range(count)]

    def spread(i, at):
        return [jnp.broadcast_to(rows[i][:, at + q : at + q + 1], shape) for q in range(SUB)]

    def line(value, p):
        return jnp.broadcast_to(value[p : p + 1, :], shape)

    done = []
    for t in range(count):
        first = SUB * t
        here = (lane >= first) & (lane < first + SUB)
        every = {i: spread(i, first) for i in range(t, count)}
        cols = every.pop(t)
        rows[t] = jnp.where(here, (lane - first == sub).astype(jnp.float32), rows[t])
        for i in every:
            rows[i] = jnp.where(here, 0.0, rows[i])
        pivots = jnp.ones(shape, jnp.float32)
        for p in range(0, SUB, 2):
            first_pivot, cross = line(cols[p], p), line(cols[p + 1], p)
            cross_low, corner = line(cols[p], p + 1), line(cols[p + 1], p + 1)
            det = first_pivot * corner - cross * cross_low
            inv1 = refine(first_pivot)
            guess = pl.reciprocal(det, approx=True)
            inv2 = (first_pivot * guess) * (2.0 - det * guess)
            below1 = jnp.where(sub > p, cols[p], 0.0)
            factor1 = below1 * inv1
            factor2 = jnp.where(sub > p + 1, cols[p + 1] - (below1 * cross) * inv1, 0.0) * inv2
            top1 = {q: line(cols[q], p) for q in range(p + 2, SUB)}
            top2 = {q: line(cols[q], p + 1) - (cross_low * top1[q]) * inv1 for q in range(p + 2, SUB)}
            for q in range(p + 2, SUB):
                cols[q] = (cols[q] - factor1 * top1[q]) - factor2 * top2[q]
            low = cross_low * inv1
            row1 = line(rows[t], p)
            row2 = line(rows[t], p + 1) - low * row1
            rows[t] = (rows[t] - factor1 * row1) - factor2 * row2
            pivots = jnp.where(sub == p, first_pivot, jnp.where(sub == p + 1, det * inv1, pivots))
            for i, values in every.items():
                near1 = values[p] * inv1
                near2 = (values[p + 1] - near1 * cross) * inv2
                for q in range(p + 2, SUB):
                    values[q] = (values[q] - near1 * top1[q]) - near2 * top2[q]
                rows[i] = (rows[i] - near1 * row1) - near2 * row2
            slot = (t * SUB + p) // 2
            for job in jobs[total * slot // slots : total * (slot + 1) // slots]:
                job()
        scale = lax.rsqrt(pivots)
        scale = scale * (1.5 - 0.5 * pivots * scale * scale)
        scaled = rows[t] * scale
        done.append(jnp.where(lane <= first + sub, scaled, 0.0))
    return jnp.concatenate(done, axis=0)


def dot_nn(a, b):
    return lax.dot_general(a, b, (((1,), (0,)), ((), ())), preferred_element_type=jnp.float32)


def dot_nt(a, b):
    return lax.dot_general(a, b, (((1,), (1,)), ((), ())), preferred_element_type=jnp.float32)


def split(value):
    high = value.astype(jnp.bfloat16)
    rest = value - high.astype(jnp.float32)
    mid = rest.astype(jnp.bfloat16)
    return high, mid, (rest - mid.astype(jnp.float32)).astype(jnp.bfloat16)


def as_left(terms):
    a, b, c = terms
    return jnp.concatenate([a, a, b, b, a, c], axis=1)


def as_right(terms, axis):
    a, b, c = terms
    return jnp.concatenate([a, b, a, b, c, a], axis=axis)


def score_kernel(sizes, *refs):
    pieces = refs[: len(sizes)]
    ids_ref, out_ref = refs[len(sizes) : len(sizes) + 2]
    rows, flipped, work, left, right, below, white, own_white, sims, sums = refs[len(sizes) + 2 :]
    row_total, width = rows.shape
    own = sizes[0]
    count = width // BLK
    blocks = [slice(BLK * n, BLK * (n + 1)) for n in range(count)]
    chunks = [slice(n, n + 2 * own) for n in range(0, row_total, 2 * own)]

    at = 0
    for size, source in zip(sizes, pieces):
        rows[at : at + size, :] = source[...]
        at += size

    def flip_columns(at, size):
        flipped[at : at + size, :] = rows[:, at : at + size].T

    def moments_of(at, size, to, to_size):
        mean = dot_nn(flipped[at : at + size, :], rows[:, to : to + to_size]) * (1.0 / row_total)
        if at < to + to_size:
            shape = (size, to_size)
            row_i = at + lax.broadcasted_iota(jnp.int32, shape, 0)
            col_i = to + lax.broadcasted_iota(jnp.int32, shape, 1)
            mean = mean + jnp.where(row_i == col_i, 0.001, 0.0)
        work[at : at + size, to : to + to_size] = mean

    def mask_of(at):
        own_col = jnp.broadcast_to(ids_ref[:, 0:own], (BLK, own)).T[:, 0:1]
        same = own_col == ids_ref[:, at : at + BLK]
        if at < own:
            own_pos = lax.broadcasted_iota(jnp.int32, (own, BLK), 0)
            same = same & (own_pos != at + lax.broadcasted_iota(jnp.int32, (own, BLK), 1))
        sims[:, at : at + BLK] = jnp.where(same, 0.0, -1e30)

    def first_jobs():
        jobs = [functools.partial(flip_columns, BLK, PANEL - BLK)]
        jobs.append(functools.partial(moments_of, BLK, PANEL - BLK, 0, PANEL))
        jobs += [functools.partial(flip_columns, at, PANEL) for at in range(PANEL, width, PANEL)]
        for to in range(0, width, PANEL):
            at = max(to, PANEL)
            jobs.append(functools.partial(moments_of, at, width - at, to, PANEL))
        return jobs + [functools.partial(mask_of, at) for at in range(0, row_total, BLK)]

    def left_of(begin, h, inverse_right):
        terms = split(dot_nt(as_left(split(work[begin:width, blocks[h]])), inverse_right))
        left[begin:width, :] = as_left(terms)
        right[begin:width, :] = as_right(terms, 1)

    def below_of(h, inverse_left):
        known = slice(0, BLK * h)
        value = dot_nn(inverse_left, as_right(split(work[blocks[h], known]), 0))
        below[:, known] = as_right(split(value), 0)
        white[blocks[h % 4], known] = value.astype(jnp.bfloat16)

    def reduce_left(begin, h):
        known = slice(0, BLK * (h + 1))
        work[begin:width, blocks[h]] = jnp.zeros((width - begin, BLK), jnp.float32)
        work[begin:width, known] -= dot_nn(left[begin:width, :], below[:, known])

    def reduce_right(begin, size):
        work[begin:width, begin : begin + size] -= dot_nt(left[begin:width, :], right[begin : begin + size, :])

    def whiten(c, h, begin, size):
        feats = slice(0, BLK * (h + 1))
        whitened = dot_nt(rows[chunks[c], feats], white[begin : begin + size, feats]).astype(jnp.bfloat16)
        if c == 0:
            own_white[:, 0:size] = whitened[0:own, :]
        sims[:, chunks[c]] += dot_nt(own_white[:, 0:size], whitened)
        squares = whitened.astype(jnp.float32)
        squares = squares * squares
        squares = sum(squares[:, n : n + BLK] for n in range(0, size, BLK))
        sums[chunks[c], :] = squares if h < 2 else sums[chunks[c], :] + squares

    def finish_rows(h, inverse):
        white[blocks[h % 4], blocks[h]] = inverse.astype(jnp.bfloat16)
        terms = split(inverse)
        below[:, blocks[h]] = as_right(terms, 0)
        jobs = [functools.partial(below_of, h, as_left(terms))] if h else []
        if h >= count - 2:
            return jobs, [functools.partial(whiten, c, h, BLK * (h % 4), BLK) for c in range(len(chunks))]
        if h % 2 == 0:
            white[blocks[h % 4], blocks[h + 1]] = jnp.zeros((BLK, BLK), jnp.bfloat16)
            return jobs, []
        return jobs, [functools.partial(whiten, c, h, BLK * (h % 4 - 1), 2 * BLK) for c in range(len(chunks))]

    flip_columns(0, BLK)
    moments_of(0, BLK, 0, BLK)
    block = work[blocks[0], blocks[0]]
    jobs = first_jobs()
    waiting = []
    for k in range(count):
        inverse = invert_factor(block, jobs)
        jobs, white_jobs = finish_rows(k, inverse)
        if k + 1 == count:
            break
        terms = split(inverse)
        inverse_right = as_right(terms, 1)
        nexts = blocks[k + 1]
        terms = split(dot_nt(as_left(split(work[nexts, blocks[k]])), inverse_right))
        value_left, value_right = as_left(terms), as_right(terms, 1)
        block = work[nexts, nexts] - dot_nt(value_left, value_right)
        left[nexts, :] = value_left
        right[nexts, :] = value_right
        begin = BLK * (k + 1)
        if begin + BLK < width:
            jobs.append(functools.partial(left_of, begin + BLK, k, inverse_right))
            for at in range(begin, width, PANEL):
                jobs.append(functools.partial(reduce_right, at, min(PANEL, width - at)))
        jobs.append(functools.partial(reduce_left, begin, k))
        if k % 2 == 1 and white_jobs:
            waiting = white_jobs[len(white_jobs) // 2 :]
            jobs += white_jobs[: len(white_jobs) // 2]
        else:
            jobs += waiting + white_jobs
            waiting = []
    for job in jobs + white_jobs:
        job()

    best = jnp.full((own, BLK), -1e30, jnp.float32)
    for at in range(0, row_total, BLK):
        key_sum = jnp.sum(sums[at : at + BLK, :].T, axis=0, keepdims=True)
        best = jnp.maximum(best, sims[:, at : at + BLK] * lax.rsqrt(key_sum + 1e-06))
    top = jnp.max(best, axis=1, keepdims=True)
    own_sum = jnp.sum(sums[0:own, :], axis=1, keepdims=True)
    top = jnp.where(top < -1e20, -1.0, jnp.maximum(top * lax.rsqrt(own_sum + 1e-06), -1.0))
    out_ref[...] = jnp.broadcast_to(top, (own, BLK)).T[0:1, :]


def scores_of(pieces, ids):
    sizes = tuple(piece.shape[0] for piece in pieces)
    row_total, width, own = sum(sizes), pieces[0].shape[1], sizes[0]
    vmem = pl.BlockSpec(memory_space=pltpu.VMEM)
    out = pl.pallas_call(
        functools.partial(score_kernel, sizes),
        out_shape=jax.ShapeDtypeStruct((1, own), jnp.float32),
        in_specs=[vmem] * (len(sizes) + 1),
        out_specs=vmem,
        scratch_shapes=[
            pltpu.VMEM((row_total, width), jnp.bfloat16),
            pltpu.VMEM((width, row_total), jnp.bfloat16),
            pltpu.VMEM((width, width), jnp.float32),
            pltpu.VMEM((width, 6 * BLK), jnp.bfloat16),
            pltpu.VMEM((width, 6 * BLK), jnp.bfloat16),
            pltpu.VMEM((6 * BLK, width), jnp.bfloat16),
            pltpu.VMEM((4 * BLK, width), jnp.bfloat16),
            pltpu.VMEM((own, 2 * BLK), jnp.bfloat16),
            pltpu.VMEM((own, row_total), jnp.float32),
            pltpu.VMEM((row_total, BLK), jnp.float32),
        ],
        compiler_params=pltpu.CompilerParams(vmem_limit_bytes=32 * 1024 * 1024),
    )(*pieces, ids.reshape(1, -1))
    return out.reshape(own)


def contract_rows(left_rows, right_rows):
    return lax.dot_general(
        left_rows, right_rows, (((0,), (0,)), ((), ())), preferred_element_type=jnp.float32
    )


def normalize_rows(values):
    widened = values.astype(jnp.float32)
    square_sum = jnp.sum(widened * widened, axis=1, keepdims=True)
    inverse_norm = lax.rsqrt(square_sum + 1e-06)
    return (widened * inverse_norm).astype(jnp.bfloat16)


def best_match(queries, query_ids, query_start, key_units, key_ids):
    similarity = lax.dot_general(
        queries, key_units, (((1,), (1,)), ((), ())), preferred_element_type=jnp.float32
    )
    query_pos = query_start + jnp.arange(queries.shape[0], dtype=jnp.int32)
    key_pos = jnp.arange(key_units.shape[0], dtype=jnp.int32)
    same_cluster = (
        (query_ids[:, None] == key_ids[None, :])
        & (query_ids[:, None] >= 0)
        & (query_pos[:, None] != key_pos[None, :])
    )
    return jnp.max(jnp.where(same_cluster, similarity, -1.0), axis=1)


def whitening_of(moments, row_total):
    identity = jnp.eye(moments.shape[0], dtype=jnp.float32)
    chol_factor = jnp.linalg.cholesky(moments / float(row_total) + 0.001 * identity)
    return jax.scipy.linalg.solve_triangular(chol_factor, identity, lower=True).astype(
        jnp.bfloat16
    )


def exchange(value, axis, flip):
    return lax.ppermute(value, axis, [(i, i ^ flip) for i in range(lax.axis_size(axis))])


def local_gathered(embeddings, cluster_ids):
    row_count = embeddings.shape[0]
    dp_count = lax.axis_size("dp")
    mp_index = lax.axis_index("mp")
    core, side = mp_index % 2, mp_index // 2
    half, quarter = row_count // 2, row_count // 4

    own_half = lax.dynamic_slice_in_dim(embeddings, core * half, half, 0)
    own_quarter = lax.dynamic_slice_in_dim(own_half, side * quarter, quarter, 0)
    zone = exchange(own_half, "dp", 2)
    near = exchange(own_half, "dp", 1)
    zone_near = exchange(zone, "dp", 1)
    far = jnp.concatenate([exchange(own_quarter, "dp", flip) for flip in range(4, dp_count, 2)], axis=0)
    far_near = exchange(far, "dp", 1)
    held = [near, zone, zone_near, far, exchange(far, "mp", 2), far_near, exchange(far_near, "mp", 2)]
    pieces = [embeddings] + held + [exchange(value, "mp", 1) for value in held]

    dp_index = lax.axis_index("dp")
    copies = jnp.broadcast_to(cluster_ids[None], (dp_count, row_count))
    ids = lax.all_to_all(copies, "dp", split_axis=0, concat_axis=0, tiled=True)

    def ids_of(sources, start, size):
        return [lax.dynamic_slice(ids, (dp_index ^ n, start), (1, size))[0] for n in sources]

    orders = [cluster_ids]
    for c in (core, 1 - core):
        orders += ids_of((1, 2, 3), c * half, half)
        for first in (4, 5):
            for s in (side, 1 - side):
                orders += ids_of(range(first, dp_count, 2), c * half + s * quarter, quarter)
    return scores_of(pieces, jnp.concatenate(orders))


def local_routed(embeddings, cluster_ids):
    row_count, feat_width = embeddings.shape
    dp_count = lax.axis_size("dp")
    mp_count = lax.axis_size("mp")
    mp_index = lax.axis_index("mp")
    pair_cap = 2 * row_count // dp_count
    slot_count = dp_count * pair_cap
    quarter_len = slot_count // mp_count
    col_share = feat_width // mp_count
    own_cols = lax.dynamic_slice_in_dim(embeddings, mp_index * col_share, col_share, 1)
    column_sums = lax.psum(contract_rows(embeddings, own_cols), "dp")
    moments = lax.all_gather(column_sums, "mp", axis=1, tiled=True)
    whitening = whitening_of(moments, row_count * dp_count)
    owner_ids = cluster_ids // CPO
    owner_hits = (owner_ids[:, None] == jnp.arange(dp_count, dtype=jnp.int32)[None, :]).astype(
        jnp.int32
    )
    earlier_hits = jnp.cumsum(owner_hits, axis=0) - owner_hits
    row_rank = jnp.sum(earlier_hits * owner_hits, axis=1)
    whiten_part = lax.dynamic_slice_in_dim(whitening, mp_index * col_share, col_share, 0)
    whitened = lax.dot_general(
        embeddings, whiten_part, (((1,), (1,)), ((), ())), preferred_element_type=jnp.float32
    ).astype(jnp.bfloat16)
    slot_index = owner_ids * pair_cap + row_rank
    send_rows = jnp.zeros((slot_count, col_share), jnp.bfloat16).at[slot_index].set(whitened)
    send_ids = jnp.full((slot_count,), -1, jnp.int32).at[slot_index].set(cluster_ids)
    got_rows, got_ids = (
        lax.all_to_all(send_rows, "dp", split_axis=0, concat_axis=0, tiled=True),
        lax.all_to_all(send_ids, "dp", split_axis=0, concat_axis=0, tiled=True),
    )
    key_rows = lax.all_gather(got_rows, "mp", axis=1, tiled=True)
    unit = normalize_rows(key_rows)
    query_start = mp_index * quarter_len
    queries = lax.dynamic_slice_in_dim(unit, query_start, quarter_len, 0)
    query_ids = lax.dynamic_slice_in_dim(got_ids, query_start, quarter_len, 0)
    best_score = best_match(queries, query_ids, query_start, unit, got_ids)
    all_scores = lax.all_gather(best_score, "mp", axis=0, tiled=True)
    returned = lax.all_to_all(all_scores, "dp", split_axis=0, concat_axis=0, tiled=True)
    return returned[slot_index]


def local(embeddings, cluster_ids):
    owners = lax.axis_size("dp")
    fits = embeddings.size * 2 * owners <= GATHER_LIMIT
    if fits and lax.axis_size("mp") == 4 and owners == 8:
        return local_gathered(embeddings, cluster_ids)
    return local_routed(embeddings, cluster_ids)


def solution(mesh):
    in_specs = (P("dp", None), P("dp"))
    out_specs = P("dp")
    return jax.shard_map(local, mesh=mesh, in_specs=in_specs, out_specs=out_specs, check_vma=False)
```

```python
import functools
import jax
import jax.numpy as jnp
from jax import lax
from jax.experimental import pallas as pl
from jax.experimental.pallas import tpu as pltpu
from jax.sharding import PartitionSpec as P

CPO = 4
GATHER_LIMIT = 8 * 1024 * 1024
BLK = 128
SUB = 8
PANEL = 256


def refine(value):
    guess = pl.reciprocal(value, approx=True)
    return guess * (2.0 - value * guess)


def invert_factor(block, jobs):
    shape = (SUB, BLK)
    lane = lax.broadcasted_iota(jnp.int32, shape, 1)
    sub = lax.broadcasted_iota(jnp.int32, shape, 0)
    count = BLK // SUB
    slots = count * SUB // 2
    jobs = list(jobs)
    total = len(jobs)
    rows = [block[SUB * i : SUB * (i + 1), :] for i in range(count)]

    def spread(i, at):
        return [jnp.broadcast_to(rows[i][:, at + q : at + q + 1], shape) for q in range(SUB)]

    def line(value, p):
        return jnp.broadcast_to(value[p : p + 1, :], shape)

    done = []
    for t in range(count):
        first = SUB * t
        here = (lane >= first) & (lane < first + SUB)
        every = {i: spread(i, first) for i in range(t, count)}
        cols = every.pop(t)
        rows[t] = jnp.where(here, (lane - first == sub).astype(jnp.float32), rows[t])
        for i in every:
            rows[i] = jnp.where(here, 0.0, rows[i])
        pivots = jnp.ones(shape, jnp.float32)
        for p in range(0, SUB, 2):
            first_pivot, cross = line(cols[p], p), line(cols[p + 1], p)
            cross_low, corner = line(cols[p], p + 1), line(cols[p + 1], p + 1)
            det = first_pivot * corner - cross * cross_low
            inv1 = refine(first_pivot)
            guess = pl.reciprocal(det, approx=True)
            inv2 = (first_pivot * guess) * (2.0 - det * guess)
            below1 = jnp.where(sub > p, cols[p], 0.0)
            factor1 = below1 * inv1
            factor2 = jnp.where(sub > p + 1, cols[p + 1] - (below1 * cross) * inv1, 0.0) * inv2
            top1 = {q: line(cols[q], p) for q in range(p + 2, SUB)}
            top2 = {q: line(cols[q], p + 1) - (cross_low * top1[q]) * inv1 for q in range(p + 2, SUB)}
            for q in range(p + 2, SUB):
                cols[q] = (cols[q] - factor1 * top1[q]) - factor2 * top2[q]
            low = cross_low * inv1
            row1 = line(rows[t], p)
            row2 = line(rows[t], p + 1) - low * row1
            rows[t] = (rows[t] - factor1 * row1) - factor2 * row2
            pivots = jnp.where(sub == p, first_pivot, jnp.where(sub == p + 1, det * inv1, pivots))
            for i, values in every.items():
                near1 = values[p] * inv1
                near2 = (values[p + 1] - near1 * cross) * inv2
                for q in range(p + 2, SUB):
                    values[q] = (values[q] - near1 * top1[q]) - near2 * top2[q]
                rows[i] = (rows[i] - near1 * row1) - near2 * row2
            slot = (t * SUB + p) // 2
            for job in jobs[total * slot // slots : total * (slot + 1) // slots]:
                job()
        scale = lax.rsqrt(pivots)
        scale = scale * (1.5 - 0.5 * pivots * scale * scale)
        scaled = rows[t] * scale
        done.append(jnp.where(lane <= first + sub, scaled, 0.0))
    return jnp.concatenate(done, axis=0)


def dot_nn(a, b):
    return lax.dot_general(a, b, (((1,), (0,)), ((), ())), preferred_element_type=jnp.float32)


def dot_nt(a, b):
    return lax.dot_general(a, b, (((1,), (1,)), ((), ())), preferred_element_type=jnp.float32)


def split(value):
    high = value.astype(jnp.bfloat16)
    rest = value - high.astype(jnp.float32)
    mid = rest.astype(jnp.bfloat16)
    return high, mid, (rest - mid.astype(jnp.float32)).astype(jnp.bfloat16)


def as_left(terms):
    a, b, c = terms
    return jnp.concatenate([a, a, b, b, a, c], axis=1)


def as_right(terms, axis):
    a, b, c = terms
    return jnp.concatenate([a, b, a, b, c, a], axis=axis)


def score_kernel(sizes, *refs):
    pieces = refs[: len(sizes)]
    ids_ref, out_ref = refs[len(sizes) : len(sizes) + 2]
    rows, flipped, work, left, right, below, white, own_white, sims, sums = refs[len(sizes) + 2 :]
    row_total, width = rows.shape
    own = sizes[0]
    count = width // BLK
    blocks = [slice(BLK * n, BLK * (n + 1)) for n in range(count)]
    chunks = [slice(n, n + 2 * own) for n in range(0, row_total, 2 * own)]

    at = 0
    for size, source in zip(sizes, pieces):
        rows[at : at + size, :] = source[...]
        at += size

    def flip_columns(at, size):
        flipped[at : at + size, :] = rows[:, at : at + size].T

    def moments_of(at, size, to, to_size):
        mean = dot_nn(flipped[at : at + size, :], rows[:, to : to + to_size]) * (1.0 / row_total)
        if at < to + to_size:
            shape = (size, to_size)
            row_i = at + lax.broadcasted_iota(jnp.int32, shape, 0)
            col_i = to + lax.broadcasted_iota(jnp.int32, shape, 1)
            mean = mean + jnp.where(row_i == col_i, 0.001, 0.0)
        work[at : at + size, to : to + to_size] = mean

    def mask_of(at):
        own_col = jnp.broadcast_to(ids_ref[:, 0:own], (BLK, own)).T[:, 0:1]
        same = own_col == ids_ref[:, at : at + BLK]
        if at < own:
            own_pos = lax.broadcasted_iota(jnp.int32, (own, BLK), 0)
            same = same & (own_pos != at + lax.broadcasted_iota(jnp.int32, (own, BLK), 1))
        sims[:, at : at + BLK] = jnp.where(same, 0.0, -1e30)

    def first_jobs():
        jobs = [functools.partial(flip_columns, BLK, PANEL - BLK)]
        jobs.append(functools.partial(moments_of, BLK, PANEL - BLK, 0, PANEL))
        jobs += [functools.partial(flip_columns, at, PANEL) for at in range(PANEL, width, PANEL)]
        for to in range(0, width, PANEL):
            at = max(to, PANEL)
            jobs.append(functools.partial(moments_of, at, width - at, to, PANEL))
        return jobs + [functools.partial(mask_of, at) for at in range(0, row_total, BLK)]

    def left_of(begin, h, inverse_right):
        terms = split(dot_nt(as_left(split(work[begin:width, blocks[h]])), inverse_right))
        left[begin:width, :] = as_left(terms)
        right[begin:width, :] = as_right(terms, 1)

    def below_of(h, inverse_left):
        known = slice(0, BLK * h)
        value = dot_nn(inverse_left, as_right(split(work[blocks[h], known]), 0))
        below[:, known] = as_right(split(value), 0)
        white[blocks[h % 4], known] = value.astype(jnp.bfloat16)

    def reduce_left(begin, h):
        known = slice(0, BLK * (h + 1))
        work[begin:width, blocks[h]] = jnp.zeros((width - begin, BLK), jnp.float32)
        work[begin:width, known] -= dot_nn(left[begin:width, :], below[:, known])

    def reduce_right(begin, size):
        work[begin:width, begin : begin + size] -= dot_nt(left[begin:width, :], right[begin : begin + size, :])

    def whiten_own(h, begin, size):
        feats = slice(0, BLK * (h + 1))
        own_white[:, 0:size] = dot_nt(rows[0:own, feats], white[begin : begin + size, feats]).astype(jnp.bfloat16)

    def whiten(c, h, begin, size):
        feats = slice(0, BLK * (h + 1))
        whitened = dot_nt(white[begin : begin + size, feats], rows[chunks[c], feats]).astype(jnp.bfloat16)
        sims[:, chunks[c]] += dot_nn(own_white[:, 0:size], whitened)
        widened = whitened.astype(jnp.float32)
        squares = sum(widened[n : n + SUB, :] * widened[n : n + SUB, :] for n in range(0, size, SUB))
        sums[:, chunks[c]] = squares if h < 2 else sums[:, chunks[c]] + squares

    def whiten_jobs(h, begin, size):
        jobs = [functools.partial(whiten_own, h, begin, size)]
        return jobs + [functools.partial(whiten, c, h, begin, size) for c in range(len(chunks))]

    def finish_rows(h, inverse):
        white[blocks[h % 4], blocks[h]] = inverse.astype(jnp.bfloat16)
        terms = split(inverse)
        below[:, blocks[h]] = as_right(terms, 0)
        jobs = [functools.partial(below_of, h, as_left(terms))] if h else []
        if h >= count - 2:
            return jobs, whiten_jobs(h, BLK * (h % 4), BLK)
        if h % 2 == 0:
            white[blocks[h % 4], blocks[h + 1]] = jnp.zeros((BLK, BLK), jnp.bfloat16)
            return jobs, []
        return jobs, whiten_jobs(h, BLK * (h % 4 - 1), 2 * BLK)

    flip_columns(0, BLK)
    moments_of(0, BLK, 0, BLK)
    block = work[blocks[0], blocks[0]]
    jobs = first_jobs()
    waiting = []
    for k in range(count):
        inverse = invert_factor(block, jobs)
        jobs, white_jobs = finish_rows(k, inverse)
        if k + 1 == count:
            break
        terms = split(inverse)
        inverse_right = as_right(terms, 1)
        nexts = blocks[k + 1]
        terms = split(dot_nt(as_left(split(work[nexts, blocks[k]])), inverse_right))
        value_left, value_right = as_left(terms), as_right(terms, 1)
        block = work[nexts, nexts] - dot_nt(value_left, value_right)
        left[nexts, :] = value_left
        right[nexts, :] = value_right
        begin = BLK * (k + 1)
        if begin + BLK < width:
            jobs.append(functools.partial(left_of, begin + BLK, k, inverse_right))
            for at in range(begin, width, PANEL):
                jobs.append(functools.partial(reduce_right, at, min(PANEL, width - at)))
        jobs.append(functools.partial(reduce_left, begin, k))
        if k % 2 == 1 and white_jobs:
            waiting = white_jobs[len(white_jobs) // 2 :]
            jobs += white_jobs[: len(white_jobs) // 2]
        else:
            jobs += waiting + white_jobs
            waiting = []
    for job in jobs + white_jobs:
        job()

    key_sums = jnp.sum(sums[...], axis=0, keepdims=True)
    scales = lax.rsqrt(key_sums + 1e-06)
    best = jnp.full((own, BLK), -1e30, jnp.float32)
    for at in range(0, row_total, BLK):
        best = jnp.maximum(best, sims[:, at : at + BLK] * scales[:, at : at + BLK])
    top = jnp.max(best, axis=1, keepdims=True)
    own_scale = jnp.broadcast_to(scales[:, 0:own], (BLK, own)).T[:, 0:1]
    top = jnp.where(top < -1e20, -1.0, jnp.maximum(top * own_scale, -1.0))
    out_ref[...] = jnp.broadcast_to(top, (own, BLK)).T[0:1, :]


def scores_of(pieces, ids):
    sizes = tuple(piece.shape[0] for piece in pieces)
    row_total, width, own = sum(sizes), pieces[0].shape[1], sizes[0]
    vmem = pl.BlockSpec(memory_space=pltpu.VMEM)
    out = pl.pallas_call(
        functools.partial(score_kernel, sizes),
        out_shape=jax.ShapeDtypeStruct((1, own), jnp.float32),
        in_specs=[vmem] * (len(sizes) + 1),
        out_specs=vmem,
        scratch_shapes=[
            pltpu.VMEM((row_total, width), jnp.bfloat16),
            pltpu.VMEM((width, row_total), jnp.bfloat16),
            pltpu.VMEM((width, width), jnp.float32),
            pltpu.VMEM((width, 6 * BLK), jnp.bfloat16),
            pltpu.VMEM((width, 6 * BLK), jnp.bfloat16),
            pltpu.VMEM((6 * BLK, width), jnp.bfloat16),
            pltpu.VMEM((4 * BLK, width), jnp.bfloat16),
            pltpu.VMEM((own, 2 * BLK), jnp.bfloat16),
            pltpu.VMEM((own, row_total), jnp.float32),
            pltpu.VMEM((SUB, row_total), jnp.float32),
        ],
        compiler_params=pltpu.CompilerParams(vmem_limit_bytes=32 * 1024 * 1024),
    )(*pieces, ids.reshape(1, -1))
    return out.reshape(own)


def contract_rows(left_rows, right_rows):
    return lax.dot_general(
        left_rows, right_rows, (((0,), (0,)), ((), ())), preferred_element_type=jnp.float32
    )


def normalize_rows(values):
    widened = values.astype(jnp.float32)
    square_sum = jnp.sum(widened * widened, axis=1, keepdims=True)
    inverse_norm = lax.rsqrt(square_sum + 1e-06)
    return (widened * inverse_norm).astype(jnp.bfloat16)


def best_match(queries, query_ids, query_start, key_units, key_ids):
    similarity = lax.dot_general(
        queries, key_units, (((1,), (1,)), ((), ())), preferred_element_type=jnp.float32
    )
    query_pos = query_start + jnp.arange(queries.shape[0], dtype=jnp.int32)
    key_pos = jnp.arange(key_units.shape[0], dtype=jnp.int32)
    same_cluster = (
        (query_ids[:, None] == key_ids[None, :])
        & (query_ids[:, None] >= 0)
        & (query_pos[:, None] != key_pos[None, :])
    )
    return jnp.max(jnp.where(same_cluster, similarity, -1.0), axis=1)


def whitening_of(moments, row_total):
    identity = jnp.eye(moments.shape[0], dtype=jnp.float32)
    chol_factor = jnp.linalg.cholesky(moments / float(row_total) + 0.001 * identity)
    return jax.scipy.linalg.solve_triangular(chol_factor, identity, lower=True).astype(
        jnp.bfloat16
    )


def exchange(value, axis, flip):
    return lax.ppermute(value, axis, [(i, i ^ flip) for i in range(lax.axis_size(axis))])


def local_gathered(embeddings, cluster_ids):
    row_count = embeddings.shape[0]
    dp_count = lax.axis_size("dp")
    mp_index = lax.axis_index("mp")
    core, side = mp_index % 2, mp_index // 2
    half, quarter = row_count // 2, row_count // 4

    own_half = lax.dynamic_slice_in_dim(embeddings, core * half, half, 0)
    own_quarter = lax.dynamic_slice_in_dim(own_half, side * quarter, quarter, 0)
    far = jnp.concatenate([exchange(own_quarter, "dp", flip) for flip in range(4, dp_count, 2)], axis=0)
    zone = exchange(own_half, "dp", 2)
    near = exchange(own_half, "dp", 1)
    ids = cluster_ids[None]
    ids = jnp.concatenate([ids, exchange(ids, "dp", 2)], axis=0)

    far, near = lax.optimization_barrier((far, near))
    far_near = exchange(far, "dp", 1)
    far_side = exchange(far, "mp", 2)
    zone_near = exchange(zone, "dp", 1)
    far_near_side = exchange(far_near, "mp", 2)

    far_side, ids = lax.optimization_barrier((far_side, ids))
    for flip in (4, 1):
        ids = jnp.concatenate([ids, exchange(ids, "dp", flip)], axis=0)
    place = {0: 0, 2: 1, 4: 2, 6: 3, 1: 4, 3: 5, 5: 6, 7: 7}

    near, zone, far, far_side = lax.optimization_barrier((near, zone, far, far_side))
    held = [near, zone, zone_near, far, far_side, far_near, far_near_side]
    pieces = [embeddings] + held + [exchange(value, "mp", 1) for value in held]

    def ids_of(sources, start, size):
        return [lax.dynamic_slice_in_dim(ids[place[n]], start, size, 0) for n in sources]

    orders = [cluster_ids]
    for c in (core, 1 - core):
        orders += ids_of((1, 2, 3), c * half, half)
        for first in (4, 5):
            for s in (side, 1 - side):
                orders += ids_of(range(first, dp_count, 2), c * half + s * quarter, quarter)
    return scores_of(pieces, jnp.concatenate(orders))


def local_routed(embeddings, cluster_ids):
    row_count, feat_width = embeddings.shape
    dp_count = lax.axis_size("dp")
    mp_count = lax.axis_size("mp")
    mp_index = lax.axis_index("mp")
    pair_cap = 2 * row_count // dp_count
    slot_count = dp_count * pair_cap
    quarter_len = slot_count // mp_count
    col_share = feat_width // mp_count
    own_cols = lax.dynamic_slice_in_dim(embeddings, mp_index * col_share, col_share, 1)
    column_sums = lax.psum(contract_rows(embeddings, own_cols), "dp")
    moments = lax.all_gather(column_sums, "mp", axis=1, tiled=True)
    whitening = whitening_of(moments, row_count * dp_count)
    owner_ids = cluster_ids // CPO
    owner_hits = (owner_ids[:, None] == jnp.arange(dp_count, dtype=jnp.int32)[None, :]).astype(
        jnp.int32
    )
    earlier_hits = jnp.cumsum(owner_hits, axis=0) - owner_hits
    row_rank = jnp.sum(earlier_hits * owner_hits, axis=1)
    whiten_part = lax.dynamic_slice_in_dim(whitening, mp_index * col_share, col_share, 0)
    whitened = lax.dot_general(
        embeddings, whiten_part, (((1,), (1,)), ((), ())), preferred_element_type=jnp.float32
    ).astype(jnp.bfloat16)
    slot_index = owner_ids * pair_cap + row_rank
    send_rows = jnp.zeros((slot_count, col_share), jnp.bfloat16).at[slot_index].set(whitened)
    send_ids = jnp.full((slot_count,), -1, jnp.int32).at[slot_index].set(cluster_ids)
    got_rows, got_ids = (
        lax.all_to_all(send_rows, "dp", split_axis=0, concat_axis=0, tiled=True),
        lax.all_to_all(send_ids, "dp", split_axis=0, concat_axis=0, tiled=True),
    )
    key_rows = lax.all_gather(got_rows, "mp", axis=1, tiled=True)
    unit = normalize_rows(key_rows)
    query_start = mp_index * quarter_len
    queries = lax.dynamic_slice_in_dim(unit, query_start, quarter_len, 0)
    query_ids = lax.dynamic_slice_in_dim(got_ids, query_start, quarter_len, 0)
    best_score = best_match(queries, query_ids, query_start, unit, got_ids)
    all_scores = lax.all_gather(best_score, "mp", axis=0, tiled=True)
    returned = lax.all_to_all(all_scores, "dp", split_axis=0, concat_axis=0, tiled=True)
    return returned[slot_index]


def local(embeddings, cluster_ids):
    owners = lax.axis_size("dp")
    fits = embeddings.size * 2 * owners <= GATHER_LIMIT
    if fits and lax.axis_size("mp") == 4 and owners == 8:
        return local_gathered(embeddings, cluster_ids)
    return local_routed(embeddings, cluster_ids)


def solution(mesh):
    in_specs = (P("dp", None), P("dp"))
    out_specs = P("dp")
    return jax.shard_map(local, mesh=mesh, in_specs=in_specs, out_specs=out_specs, check_vma=False)
```

```python
import functools
import jax
import jax.numpy as jnp
from jax import lax
from jax.experimental import pallas as pl
from jax.experimental.pallas import tpu as pltpu
from jax.sharding import PartitionSpec as P

CPO = 4
GATHER_LIMIT = 8 * 1024 * 1024
BLK = 128
SUB = 8
GROUP = 4
PANEL = 256


def refine(value):
    guess = pl.reciprocal(value, approx=True)
    return guess * (2.0 - value * guess)


def invert_factor(block, jobs):
    shape = (SUB, BLK)
    lane = lax.broadcasted_iota(jnp.int32, shape, 1)
    sub = lax.broadcasted_iota(jnp.int32, shape, 0)
    count = BLK // SUB
    slots = count * SUB // 2
    jobs = list(jobs)
    total = len(jobs)
    rows = [block[SUB * i : SUB * (i + 1), :] for i in range(count)]

    def spread(i, at):
        return [jnp.broadcast_to(rows[i][:, at + q : at + q + 1], shape) for q in range(SUB)]

    def line(value, p):
        return jnp.broadcast_to(value[p : p + 1, :], shape)

    def follow(i, first, steps):
        cols = spread(i, first)
        value = jnp.where((lane >= first) & (lane < first + SUB), 0.0, rows[i])
        for p, (inverse, tops, pivot_row) in enumerate(steps):
            factor = cols[p] * inverse
            for q in range(p + 1, SUB):
                cols[q] = cols[q] - factor * tops[q]
            value = value - factor * pivot_row
        rows[i] = value

    def follow_group(end, members):
        start = end - SUB * GROUP
        factors = as_right(split(jnp.concatenate(members, axis=0)), 0)
        lines = [
            jnp.where((lane >= start + SUB * (n + 1)) & (lane < end), 0.0, member) for n, member in enumerate(members)
        ]
        a, b, c = split(jnp.concatenate(lines, axis=0))
        change = lax.dot_general(
            factors,
            jnp.concatenate([a, a, b, b, a, c], axis=0),
            (((0,), (0,)), ((), ())),
            preferred_element_type=jnp.float32,
        )
        for i in range(end // SUB + GROUP, count):
            kept = jnp.where((lane >= start) & (lane < end), 0.0, rows[i])
            rows[i] = kept - change[SUB * i : SUB * (i + 1), :]

    done = []
    late = []
    members = []
    cols = spread(0, 0)
    for t in range(count):
        first = SUB * t
        here = (lane >= first) & (lane < first + SUB)
        window = min((t // GROUP + 2) * GROUP, count)
        every = {i: spread(i, first) for i in range(t + 1, min(t + 2, count))}
        late_total = len(late)
        steps = []
        rows[t] = jnp.where(here, (lane - first == sub).astype(jnp.float32), rows[t])
        for i in every:
            rows[i] = jnp.where(here, 0.0, rows[i])
        pivots = jnp.ones(shape, jnp.float32)
        for p in range(0, SUB, 2):
            first_pivot, cross = line(cols[p], p), line(cols[p + 1], p)
            cross_low, corner = line(cols[p], p + 1), line(cols[p + 1], p + 1)
            det = first_pivot * corner - cross * cross_low
            inv1 = refine(first_pivot)
            guess = pl.reciprocal(det, approx=True)
            inv2 = (first_pivot * guess) * (2.0 - det * guess)
            below1 = jnp.where(sub > p, cols[p], 0.0)
            factor1 = below1 * inv1
            factor2 = jnp.where(sub > p + 1, cols[p + 1] - (below1 * cross) * inv1, 0.0) * inv2
            top1 = {q: line(cols[q], p) for q in range(p + 2, SUB)}
            top2 = {q: line(cols[q], p + 1) - (cross_low * top1[q]) * inv1 for q in range(p + 2, SUB)}
            for q in range(p + 2, SUB):
                cols[q] = (cols[q] - factor1 * top1[q]) - factor2 * top2[q]
            low = cross_low * inv1
            row1 = line(rows[t], p)
            row2 = line(rows[t], p + 1) - low * row1
            rows[t] = (rows[t] - factor1 * row1) - factor2 * row2
            pivots = jnp.where(sub == p, first_pivot, jnp.where(sub == p + 1, det * inv1, pivots))
            top1[p + 1] = cross
            steps += [(inv1, top1, row1), (inv2, top2, row2)]
            for i, values in every.items():
                near1 = values[p] * inv1
                near2 = (values[p + 1] - near1 * cross) * inv2
                for q in range(p + 2, SUB):
                    values[q] = (values[q] - near1 * top1[q]) - near2 * top2[q]
                rows[i] = (rows[i] - near1 * row1) - near2 * row2
            for _ in range(late_total * (p + 2) // SUB - late_total * p // SUB):
                late.pop(0)()
            slot = (t * SUB + p) // 2
            for job in jobs[total * slot // slots : total * (slot + 1) // slots]:
                job()
        scale = lax.rsqrt(pivots)
        scale = scale * (1.5 - 0.5 * pivots * scale * scale)
        scaled = rows[t] * scale
        done.append(jnp.where(lane <= first + sub, scaled, 0.0))
        if t + 1 < count:
            cols = spread(t + 1, first + SUB)
        if t + 2 < window:
            follow(t + 2, first, steps)
        late += [functools.partial(follow, i, first, steps) for i in range(t + 3, window)]
        members.append(scaled)
        if len(members) == GROUP:
            if window < count:
                follow_group(first + SUB, members)
            members = []
    return jnp.concatenate(done, axis=0)


def dot_nn(a, b):
    return lax.dot_general(a, b, (((1,), (0,)), ((), ())), preferred_element_type=jnp.float32)


def dot_nt(a, b):
    return lax.dot_general(a, b, (((1,), (1,)), ((), ())), preferred_element_type=jnp.float32)


def split(value):
    high = value.astype(jnp.bfloat16)
    rest = value - high.astype(jnp.float32)
    mid = rest.astype(jnp.bfloat16)
    return high, mid, (rest - mid.astype(jnp.float32)).astype(jnp.bfloat16)


def as_left(terms):
    a, b, c = terms
    return jnp.concatenate([a, a, b, b, a, c], axis=1)


def as_right(terms, axis):
    a, b, c = terms
    return jnp.concatenate([a, b, a, b, c, a], axis=axis)


def score_kernel(sizes, *refs):
    pieces = refs[: len(sizes)]
    ids_ref, out_ref = refs[len(sizes) : len(sizes) + 2]
    rows, flipped, work, left, right, below, white, own_white, sims, sums = refs[len(sizes) + 2 :]
    row_total, width = rows.shape
    own = sizes[0]
    count = width // BLK
    blocks = [slice(BLK * n, BLK * (n + 1)) for n in range(count)]
    chunks = [slice(n, n + 2 * own) for n in range(0, row_total, 2 * own)]

    at = 0
    for size, source in zip(sizes, pieces):
        rows[at : at + size, :] = source[...]
        at += size

    def flip_columns(at, size):
        flipped[at : at + size, :] = rows[:, at : at + size].T

    def moments_of(at, size, to, to_size):
        mean = dot_nn(flipped[at : at + size, :], rows[:, to : to + to_size]) * (1.0 / row_total)
        if at < to + to_size:
            shape = (size, to_size)
            row_i = at + lax.broadcasted_iota(jnp.int32, shape, 0)
            col_i = to + lax.broadcasted_iota(jnp.int32, shape, 1)
            mean = mean + jnp.where(row_i == col_i, 0.001, 0.0)
        work[at : at + size, to : to + to_size] = mean

    def mask_of(at):
        own_col = jnp.broadcast_to(ids_ref[:, 0:own], (BLK, own)).T[:, 0:1]
        same = own_col == ids_ref[:, at : at + BLK]
        if at < own:
            own_pos = lax.broadcasted_iota(jnp.int32, (own, BLK), 0)
            same = same & (own_pos != at + lax.broadcasted_iota(jnp.int32, (own, BLK), 1))
        sims[:, at : at + BLK] = jnp.where(same, 0.0, -1e30)

    def first_jobs():
        jobs = [functools.partial(flip_columns, BLK, PANEL - BLK)]
        jobs.append(functools.partial(moments_of, BLK, PANEL - BLK, 0, PANEL))
        jobs += [functools.partial(flip_columns, at, PANEL) for at in range(PANEL, width, PANEL)]
        for to in range(0, width, PANEL):
            at = max(to, PANEL)
            jobs.append(functools.partial(moments_of, at, width - at, to, PANEL))
        return jobs + [functools.partial(mask_of, at) for at in range(0, row_total, BLK)]

    def left_of(begin, h, inverse_right):
        terms = split(dot_nt(as_left(split(work[begin:width, blocks[h]])), inverse_right))
        left[begin:width, :] = as_left(terms)
        right[begin:width, :] = as_right(terms, 1)

    def below_of(h, inverse_left):
        known = slice(0, BLK * h)
        value = dot_nn(inverse_left, as_right(split(work[blocks[h], known]), 0))
        below[:, known] = as_right(split(value), 0)
        white[blocks[h % 4], known] = value.astype(jnp.bfloat16)

    def reduce_left(begin, h):
        known = slice(0, BLK * (h + 1))
        work[begin:width, blocks[h]] = jnp.zeros((width - begin, BLK), jnp.float32)
        work[begin:width, known] -= dot_nn(left[begin:width, :], below[:, known])

    def reduce_right(begin, size):
        work[begin:width, begin : begin + size] -= dot_nt(left[begin:width, :], right[begin : begin + size, :])

    def whiten_own(h, begin, size):
        feats = slice(0, BLK * (h + 1))
        own_white[:, 0:size] = dot_nt(rows[0:own, feats], white[begin : begin + size, feats]).astype(jnp.bfloat16)

    def whiten(c, h, begin, size):
        feats = slice(0, BLK * (h + 1))
        whitened = dot_nt(white[begin : begin + size, feats], rows[chunks[c], feats]).astype(jnp.bfloat16)
        sims[:, chunks[c]] += dot_nn(own_white[:, 0:size], whitened)
        widened = whitened.astype(jnp.float32)
        squares = sum(widened[n : n + SUB, :] * widened[n : n + SUB, :] for n in range(0, size, SUB))
        sums[:, chunks[c]] = squares if h < 2 else sums[:, chunks[c]] + squares

    def whiten_jobs(h, begin, size):
        jobs = [functools.partial(whiten_own, h, begin, size)]
        return jobs + [functools.partial(whiten, c, h, begin, size) for c in range(len(chunks))]

    def finish_rows(h, inverse):
        white[blocks[h % 4], blocks[h]] = inverse.astype(jnp.bfloat16)
        terms = split(inverse)
        below[:, blocks[h]] = as_right(terms, 0)
        jobs = [functools.partial(below_of, h, as_left(terms))] if h else []
        if h >= count - 2:
            return jobs, whiten_jobs(h, BLK * (h % 4), BLK)
        if h % 2 == 0:
            white[blocks[h % 4], blocks[h + 1]] = jnp.zeros((BLK, BLK), jnp.bfloat16)
            return jobs, []
        return jobs, whiten_jobs(h, BLK * (h % 4 - 1), 2 * BLK)

    flip_columns(0, BLK)
    moments_of(0, BLK, 0, BLK)
    block = work[blocks[0], blocks[0]]
    jobs = first_jobs()
    waiting = []
    for k in range(count):
        inverse = invert_factor(block, jobs)
        jobs, white_jobs = finish_rows(k, inverse)
        if k + 1 == count:
            break
        terms = split(inverse)
        inverse_right = as_right(terms, 1)
        nexts = blocks[k + 1]
        terms = split(dot_nt(as_left(split(work[nexts, blocks[k]])), inverse_right))
        value_left, value_right = as_left(terms), as_right(terms, 1)
        block = work[nexts, nexts] - dot_nt(value_left, value_right)
        left[nexts, :] = value_left
        right[nexts, :] = value_right
        begin = BLK * (k + 1)
        if begin + BLK < width:
            jobs.append(functools.partial(left_of, begin + BLK, k, inverse_right))
            for at in range(begin, width, PANEL):
                jobs.append(functools.partial(reduce_right, at, min(PANEL, width - at)))
        jobs.append(functools.partial(reduce_left, begin, k))
        if k % 2 == 1 and white_jobs:
            waiting = white_jobs[len(white_jobs) // 2 :]
            jobs += white_jobs[: len(white_jobs) // 2]
        else:
            jobs += waiting + white_jobs
            waiting = []
    for job in jobs + white_jobs:
        job()

    key_sums = jnp.sum(sums[...], axis=0, keepdims=True)
    scales = lax.rsqrt(key_sums + 1e-06)
    best = jnp.full((own, BLK), -1e30, jnp.float32)
    for at in range(0, row_total, BLK):
        best = jnp.maximum(best, sims[:, at : at + BLK] * scales[:, at : at + BLK])
    top = jnp.max(best, axis=1, keepdims=True)
    own_scale = jnp.broadcast_to(scales[:, 0:own], (BLK, own)).T[:, 0:1]
    top = jnp.where(top < -1e20, -1.0, jnp.maximum(top * own_scale, -1.0))
    out_ref[...] = jnp.broadcast_to(top, (own, BLK)).T[0:1, :]


def scores_of(pieces, ids):
    sizes = tuple(piece.shape[0] for piece in pieces)
    row_total, width, own = sum(sizes), pieces[0].shape[1], sizes[0]
    vmem = pl.BlockSpec(memory_space=pltpu.VMEM)
    out = pl.pallas_call(
        functools.partial(score_kernel, sizes),
        out_shape=jax.ShapeDtypeStruct((1, own), jnp.float32),
        in_specs=[vmem] * (len(sizes) + 1),
        out_specs=vmem,
        scratch_shapes=[
            pltpu.VMEM((row_total, width), jnp.bfloat16),
            pltpu.VMEM((width, row_total), jnp.bfloat16),
            pltpu.VMEM((width, width), jnp.float32),
            pltpu.VMEM((width, 6 * BLK), jnp.bfloat16),
            pltpu.VMEM((width, 6 * BLK), jnp.bfloat16),
            pltpu.VMEM((6 * BLK, width), jnp.bfloat16),
            pltpu.VMEM((4 * BLK, width), jnp.bfloat16),
            pltpu.VMEM((own, 2 * BLK), jnp.bfloat16),
            pltpu.VMEM((own, row_total), jnp.float32),
            pltpu.VMEM((SUB, row_total), jnp.float32),
        ],
        compiler_params=pltpu.CompilerParams(vmem_limit_bytes=32 * 1024 * 1024),
    )(*pieces, ids.reshape(1, -1))
    return out.reshape(own)


def contract_rows(left_rows, right_rows):
    return lax.dot_general(
        left_rows, right_rows, (((0,), (0,)), ((), ())), preferred_element_type=jnp.float32
    )


def normalize_rows(values):
    widened = values.astype(jnp.float32)
    square_sum = jnp.sum(widened * widened, axis=1, keepdims=True)
    inverse_norm = lax.rsqrt(square_sum + 1e-06)
    return (widened * inverse_norm).astype(jnp.bfloat16)


def best_match(queries, query_ids, query_start, key_units, key_ids):
    similarity = lax.dot_general(
        queries, key_units, (((1,), (1,)), ((), ())), preferred_element_type=jnp.float32
    )
    query_pos = query_start + jnp.arange(queries.shape[0], dtype=jnp.int32)
    key_pos = jnp.arange(key_units.shape[0], dtype=jnp.int32)
    same_cluster = (
        (query_ids[:, None] == key_ids[None, :])
        & (query_ids[:, None] >= 0)
        & (query_pos[:, None] != key_pos[None, :])
    )
    return jnp.max(jnp.where(same_cluster, similarity, -1.0), axis=1)


def whitening_of(moments, row_total):
    identity = jnp.eye(moments.shape[0], dtype=jnp.float32)
    chol_factor = jnp.linalg.cholesky(moments / float(row_total) + 0.001 * identity)
    return jax.scipy.linalg.solve_triangular(chol_factor, identity, lower=True).astype(
        jnp.bfloat16
    )


def exchange(value, axis, flip):
    return lax.ppermute(value, axis, [(i, i ^ flip) for i in range(lax.axis_size(axis))])


def local_gathered(embeddings, cluster_ids):
    row_count = embeddings.shape[0]
    dp_count = lax.axis_size("dp")
    mp_index = lax.axis_index("mp")
    core, side = mp_index % 2, mp_index // 2
    half, quarter = row_count // 2, row_count // 4

    own_half = lax.dynamic_slice_in_dim(embeddings, core * half, half, 0)
    own_quarter = lax.dynamic_slice_in_dim(own_half, side * quarter, quarter, 0)
    far = jnp.concatenate([exchange(own_quarter, "dp", flip) for flip in range(4, dp_count, 2)], axis=0)
    zone = exchange(own_half, "dp", 2)
    near = exchange(own_half, "dp", 1)
    ids = cluster_ids[None]
    ids = jnp.concatenate([ids, exchange(ids, "dp", 2)], axis=0)

    far, near = lax.optimization_barrier((far, near))
    far_near = exchange(far, "dp", 1)
    far_side = exchange(far, "mp", 2)
    zone_near = exchange(zone, "dp", 1)
    far_near_side = exchange(far_near, "mp", 2)

    far_side, ids = lax.optimization_barrier((far_side, ids))
    for flip in (4, 1):
        ids = jnp.concatenate([ids, exchange(ids, "dp", flip)], axis=0)
    place = {0: 0, 2: 1, 4: 2, 6: 3, 1: 4, 3: 5, 5: 6, 7: 7}

    near, zone, far, far_side = lax.optimization_barrier((near, zone, far, far_side))
    held = [near, zone, zone_near, far, far_side, far_near, far_near_side]
    pieces = [embeddings] + held + [exchange(value, "mp", 1) for value in held]

    def ids_of(sources, start, size):
        return [lax.dynamic_slice_in_dim(ids[place[n]], start, size, 0) for n in sources]

    orders = [cluster_ids]
    for c in (core, 1 - core):
        orders += ids_of((1, 2, 3), c * half, half)
        for first in (4, 5):
            for s in (side, 1 - side):
                orders += ids_of(range(first, dp_count, 2), c * half + s * quarter, quarter)
    return scores_of(pieces, jnp.concatenate(orders))


def local_routed(embeddings, cluster_ids):
    row_count, feat_width = embeddings.shape
    dp_count = lax.axis_size("dp")
    mp_count = lax.axis_size("mp")
    mp_index = lax.axis_index("mp")
    pair_cap = 2 * row_count // dp_count
    slot_count = dp_count * pair_cap
    quarter_len = slot_count // mp_count
    col_share = feat_width // mp_count
    own_cols = lax.dynamic_slice_in_dim(embeddings, mp_index * col_share, col_share, 1)
    column_sums = lax.psum(contract_rows(embeddings, own_cols), "dp")
    moments = lax.all_gather(column_sums, "mp", axis=1, tiled=True)
    whitening = whitening_of(moments, row_count * dp_count)
    owner_ids = cluster_ids // CPO
    owner_hits = (owner_ids[:, None] == jnp.arange(dp_count, dtype=jnp.int32)[None, :]).astype(
        jnp.int32
    )
    earlier_hits = jnp.cumsum(owner_hits, axis=0) - owner_hits
    row_rank = jnp.sum(earlier_hits * owner_hits, axis=1)
    whiten_part = lax.dynamic_slice_in_dim(whitening, mp_index * col_share, col_share, 0)
    whitened = lax.dot_general(
        embeddings, whiten_part, (((1,), (1,)), ((), ())), preferred_element_type=jnp.float32
    ).astype(jnp.bfloat16)
    slot_index = owner_ids * pair_cap + row_rank
    send_rows = jnp.zeros((slot_count, col_share), jnp.bfloat16).at[slot_index].set(whitened)
    send_ids = jnp.full((slot_count,), -1, jnp.int32).at[slot_index].set(cluster_ids)
    got_rows, got_ids = (
        lax.all_to_all(send_rows, "dp", split_axis=0, concat_axis=0, tiled=True),
        lax.all_to_all(send_ids, "dp", split_axis=0, concat_axis=0, tiled=True),
    )
    key_rows = lax.all_gather(got_rows, "mp", axis=1, tiled=True)
    unit = normalize_rows(key_rows)
    query_start = mp_index * quarter_len
    queries = lax.dynamic_slice_in_dim(unit, query_start, quarter_len, 0)
    query_ids = lax.dynamic_slice_in_dim(got_ids, query_start, quarter_len, 0)
    best_score = best_match(queries, query_ids, query_start, unit, got_ids)
    all_scores = lax.all_gather(best_score, "mp", axis=0, tiled=True)
    returned = lax.all_to_all(all_scores, "dp", split_axis=0, concat_axis=0, tiled=True)
    return returned[slot_index]


def local(embeddings, cluster_ids):
    owners = lax.axis_size("dp")
    fits = embeddings.size * 2 * owners <= GATHER_LIMIT
    if fits and lax.axis_size("mp") == 4 and owners == 8:
        return local_gathered(embeddings, cluster_ids)
    return local_routed(embeddings, cluster_ids)


def solution(mesh):
    in_specs = (P("dp", None), P("dp"))
    out_specs = P("dp")
    return jax.shard_map(local, mesh=mesh, in_specs=in_specs, out_specs=out_specs, check_vma=False)
```

```python
import functools
import jax
import jax.numpy as jnp
from jax import lax
from jax.experimental import pallas as pl
from jax.experimental.pallas import tpu as pltpu
from jax.sharding import PartitionSpec as P

CPO = 4
GATHER_LIMIT = 8 * 1024 * 1024
BLK = 128
SUB = 8
GROUP = 4
PANEL = 256


def refine(value):
    guess = pl.reciprocal(value, approx=True)
    return guess * (2.0 - value * guess)


def invert_factor(block, jobs):
    shape = (SUB, BLK)
    lane = lax.broadcasted_iota(jnp.int32, shape, 1)
    sub = lax.broadcasted_iota(jnp.int32, shape, 0)
    count = BLK // SUB
    slots = count * SUB // 2
    jobs = list(jobs)
    total = len(jobs)
    rows = [block[SUB * i : SUB * (i + 1), :] for i in range(count)]

    def spread(i, at):
        return [jnp.broadcast_to(rows[i][:, at + q : at + q + 1], shape) for q in range(SUB)]

    def line(value, p):
        return jnp.broadcast_to(value[p : p + 1, :], shape)

    def follow(i, first, steps):
        cols = spread(i, first)
        value = jnp.where((lane >= first) & (lane < first + SUB), 0.0, rows[i])
        for p, (inverse, tops, pivot_row) in enumerate(steps):
            factor = cols[p] * inverse
            for q in range(p + 1, SUB):
                cols[q] = cols[q] - factor * tops[q]
            value = value - factor * pivot_row
        rows[i] = value

    def follow_group(end, members):
        start = end - SUB * GROUP
        factors = as_right(split(jnp.concatenate(members, axis=0)), 0)
        lines = [
            jnp.where((lane >= start + SUB * (n + 1)) & (lane < end), 0.0, member) for n, member in enumerate(members)
        ]
        a, b, c = split(jnp.concatenate(lines, axis=0))
        change = lax.dot_general(
            factors,
            jnp.concatenate([a, a, b, b, a, c], axis=0),
            (((0,), (0,)), ((), ())),
            preferred_element_type=jnp.float32,
        )
        for i in range(end // SUB + GROUP, count):
            kept = jnp.where((lane >= start) & (lane < end), 0.0, rows[i])
            rows[i] = kept - change[SUB * i : SUB * (i + 1), :]

    done = []
    late = []
    members = []
    cols = spread(0, 0)
    for t in range(count):
        first = SUB * t
        here = (lane >= first) & (lane < first + SUB)
        window = min((t // GROUP + 2) * GROUP, count)
        every = {i: spread(i, first) for i in range(t + 1, min(t + 3, window))}
        if every:
            ahead = spread(t, first + SUB)
            next_cols = spread(t + 1, first + SUB)
        late_total = len(late)
        steps = []
        rows[t] = jnp.where(here, (lane - first == sub).astype(jnp.float32), rows[t])
        for i in every:
            rows[i] = jnp.where(here, 0.0, rows[i])
        pivots = jnp.ones(shape, jnp.float32)
        for p in range(0, SUB, 2):
            first_pivot, cross = line(cols[p], p), line(cols[p + 1], p)
            cross_low, corner = line(cols[p], p + 1), line(cols[p + 1], p + 1)
            det = first_pivot * corner - cross * cross_low
            inv1 = refine(first_pivot)
            guess = pl.reciprocal(det, approx=True)
            inv2 = (first_pivot * guess) * (2.0 - det * guess)
            below1 = jnp.where(sub > p, cols[p], 0.0)
            factor1 = below1 * inv1
            factor2 = jnp.where(sub > p + 1, cols[p + 1] - (below1 * cross) * inv1, 0.0) * inv2
            top1 = {q: line(cols[q], p) for q in range(p + 2, SUB)}
            top2 = {q: line(cols[q], p + 1) - (cross_low * top1[q]) * inv1 for q in range(p + 2, SUB)}
            for q in range(p + 2, SUB):
                cols[q] = (cols[q] - factor1 * top1[q]) - factor2 * top2[q]
            low = cross_low * inv1
            row1 = line(rows[t], p)
            row2 = line(rows[t], p + 1) - low * row1
            rows[t] = (rows[t] - factor1 * row1) - factor2 * row2
            pivots = jnp.where(sub == p, first_pivot, jnp.where(sub == p + 1, det * inv1, pivots))
            top1[p + 1] = cross
            steps += [(inv1, top1, row1), (inv2, top2, row2)]
            if every:
                ahead1 = [line(value, p) for value in ahead]
                ahead2 = [line(value, p + 1) - low * one for value, one in zip(ahead, ahead1)]
                ahead = [(v - factor1 * one) - factor2 * two for v, one, two in zip(ahead, ahead1, ahead2)]
            for i, values in every.items():
                near1 = values[p] * inv1
                near2 = (values[p + 1] - near1 * cross) * inv2
                for q in range(p + 2, SUB):
                    values[q] = (values[q] - near1 * top1[q]) - near2 * top2[q]
                rows[i] = (rows[i] - near1 * row1) - near2 * row2
                if i == t + 1:
                    next_cols = [
                        (v - near1 * one) - near2 * two for v, one, two in zip(next_cols, ahead1, ahead2)
                    ]
            for _ in range(late_total * (p + 2) // SUB - late_total * p // SUB):
                late.pop(0)()
            slot = (t * SUB + p) // 2
            for job in jobs[total * slot // slots : total * (slot + 1) // slots]:
                job()
        scale = lax.rsqrt(pivots)
        scale = scale * (1.5 - 0.5 * pivots * scale * scale)
        scaled = rows[t] * scale
        done.append(jnp.where(lane <= first + sub, scaled, 0.0))
        if every:
            cols = next_cols
        if t + 3 < window:
            follow(t + 3, first, steps)
        late += [functools.partial(follow, i, first, steps) for i in range(t + 4, window)]
        members.append(scaled)
        if len(members) == GROUP:
            if window < count:
                follow_group(first + SUB, members)
            members = []
    return jnp.concatenate(done, axis=0)


def dot_nn(a, b):
    return lax.dot_general(a, b, (((1,), (0,)), ((), ())), preferred_element_type=jnp.float32)


def dot_nt(a, b):
    return lax.dot_general(a, b, (((1,), (1,)), ((), ())), preferred_element_type=jnp.float32)


def split(value):
    high = value.astype(jnp.bfloat16)
    rest = value - high.astype(jnp.float32)
    mid = rest.astype(jnp.bfloat16)
    return high, mid, (rest - mid.astype(jnp.float32)).astype(jnp.bfloat16)


def as_left(terms):
    a, b, c = terms
    return jnp.concatenate([a, a, b, b, a, c], axis=1)


def as_right(terms, axis):
    a, b, c = terms
    return jnp.concatenate([a, b, a, b, c, a], axis=axis)


def score_kernel(sizes, *refs):
    pieces = refs[: len(sizes)]
    ids_ref, out_ref = refs[len(sizes) : len(sizes) + 2]
    rows, flipped, work, left, right, below, white, own_white, sims, sums = refs[len(sizes) + 2 :]
    row_total, width = rows.shape
    own = sizes[0]
    count = width // BLK
    blocks = [slice(BLK * n, BLK * (n + 1)) for n in range(count)]
    chunks = [slice(n, n + 2 * own) for n in range(0, row_total, 2 * own)]

    at = 0
    for size, source in zip(sizes, pieces):
        rows[at : at + size, :] = source[...]
        at += size

    def flip_columns(at, size):
        flipped[at : at + size, :] = rows[:, at : at + size].T

    def moments_of(at, size, to, to_size):
        mean = dot_nn(flipped[at : at + size, :], rows[:, to : to + to_size]) * (1.0 / row_total)
        if at < to + to_size:
            shape = (size, to_size)
            row_i = at + lax.broadcasted_iota(jnp.int32, shape, 0)
            col_i = to + lax.broadcasted_iota(jnp.int32, shape, 1)
            mean = mean + jnp.where(row_i == col_i, 0.001, 0.0)
        work[at : at + size, to : to + to_size] = mean

    def mask_of(at):
        own_col = jnp.broadcast_to(ids_ref[:, 0:own], (BLK, own)).T[:, 0:1]
        same = own_col == ids_ref[:, at : at + BLK]
        if at < own:
            own_pos = lax.broadcasted_iota(jnp.int32, (own, BLK), 0)
            same = same & (own_pos != at + lax.broadcasted_iota(jnp.int32, (own, BLK), 1))
        sims[:, at : at + BLK] = jnp.where(same, 0.0, -1e30)

    def first_jobs():
        jobs = [functools.partial(flip_columns, BLK, PANEL - BLK)]
        jobs.append(functools.partial(moments_of, BLK, PANEL - BLK, 0, PANEL))
        jobs += [functools.partial(flip_columns, at, PANEL) for at in range(PANEL, width, PANEL)]
        for to in range(0, width, PANEL):
            at = max(to, PANEL)
            jobs.append(functools.partial(moments_of, at, width - at, to, PANEL))
        return jobs + [functools.partial(mask_of, at) for at in range(0, row_total, BLK)]

    def left_of(begin, h, inverse_right):
        terms = split(dot_nt(as_left(split(work[begin:width, blocks[h]])), inverse_right))
        left[begin:width, :] = as_left(terms)
        right[begin:width, :] = as_right(terms, 1)

    def below_of(h, inverse_left):
        known = slice(0, BLK * h)
        value = dot_nn(inverse_left, as_right(split(work[blocks[h], known]), 0))
        below[:, known] = as_right(split(value), 0)
        white[blocks[h % 4], known] = value.astype(jnp.bfloat16)

    def reduce_left(begin, h):
        known = slice(0, BLK * (h + 1))
        work[begin:width, blocks[h]] = jnp.zeros((width - begin, BLK), jnp.float32)
        work[begin:width, known] -= dot_nn(left[begin:width, :], below[:, known])

    def reduce_right(begin, size):
        work[begin:width, begin : begin + size] -= dot_nt(left[begin:width, :], right[begin : begin + size, :])

    def whiten_own(h, begin, size):
        feats = slice(0, BLK * (h + 1))
        own_white[:, 0:size] = dot_nt(rows[0:own, feats], white[begin : begin + size, feats]).astype(jnp.bfloat16)

    def whiten(c, h, begin, size):
        feats = slice(0, BLK * (h + 1))
        whitened = dot_nt(white[begin : begin + size, feats], rows[chunks[c], feats]).astype(jnp.bfloat16)
        sims[:, chunks[c]] += dot_nn(own_white[:, 0:size], whitened)
        widened = whitened.astype(jnp.float32)
        squares = sum(widened[n : n + SUB, :] * widened[n : n + SUB, :] for n in range(0, size, SUB))
        sums[:, chunks[c]] = squares if h < 2 else sums[:, chunks[c]] + squares

    def whiten_jobs(h, begin, size):
        jobs = [functools.partial(whiten_own, h, begin, size)]
        return jobs + [functools.partial(whiten, c, h, begin, size) for c in range(len(chunks))]

    def finish_rows(h, inverse):
        white[blocks[h % 4], blocks[h]] = inverse.astype(jnp.bfloat16)
        terms = split(inverse)
        below[:, blocks[h]] = as_right(terms, 0)
        jobs = [functools.partial(below_of, h, as_left(terms))] if h else []
        if h >= count - 2:
            return jobs, whiten_jobs(h, BLK * (h % 4), BLK)
        if h % 2 == 0:
            white[blocks[h % 4], blocks[h + 1]] = jnp.zeros((BLK, BLK), jnp.bfloat16)
            return jobs, []
        return jobs, whiten_jobs(h, BLK * (h % 4 - 1), 2 * BLK)

    flip_columns(0, BLK)
    moments_of(0, BLK, 0, BLK)
    block = work[blocks[0], blocks[0]]
    jobs = first_jobs()
    waiting = []
    for k in range(count):
        inverse = invert_factor(block, jobs)
        jobs, white_jobs = finish_rows(k, inverse)
        if k + 1 == count:
            break
        terms = split(inverse)
        inverse_right = as_right(terms, 1)
        nexts = blocks[k + 1]
        terms = split(dot_nt(as_left(split(work[nexts, blocks[k]])), inverse_right))
        value_left, value_right = as_left(terms), as_right(terms, 1)
        block = work[nexts, nexts] - dot_nt(value_left, value_right)
        left[nexts, :] = value_left
        right[nexts, :] = value_right
        begin = BLK * (k + 1)
        if begin + BLK < width:
            jobs.append(functools.partial(left_of, begin + BLK, k, inverse_right))
            for at in range(begin, width, PANEL):
                jobs.append(functools.partial(reduce_right, at, min(PANEL, width - at)))
        jobs.append(functools.partial(reduce_left, begin, k))
        if k % 2 == 1 and white_jobs:
            waiting = white_jobs[len(white_jobs) // 2 :]
            jobs += white_jobs[: len(white_jobs) // 2]
        else:
            jobs += waiting + white_jobs
            waiting = []
    for job in jobs + white_jobs:
        job()

    key_sums = jnp.sum(sums[...], axis=0, keepdims=True)
    scales = lax.rsqrt(key_sums + 1e-06)
    best = jnp.full((own, BLK), -1e30, jnp.float32)
    for at in range(0, row_total, BLK):
        best = jnp.maximum(best, sims[:, at : at + BLK] * scales[:, at : at + BLK])
    top = jnp.max(best, axis=1, keepdims=True)
    own_scale = jnp.broadcast_to(scales[:, 0:own], (BLK, own)).T[:, 0:1]
    top = jnp.where(top < -1e20, -1.0, jnp.maximum(top * own_scale, -1.0))
    out_ref[...] = jnp.broadcast_to(top, (own, BLK)).T[0:1, :]


def scores_of(pieces, ids):
    sizes = tuple(piece.shape[0] for piece in pieces)
    row_total, width, own = sum(sizes), pieces[0].shape[1], sizes[0]
    vmem = pl.BlockSpec(memory_space=pltpu.VMEM)
    out = pl.pallas_call(
        functools.partial(score_kernel, sizes),
        out_shape=jax.ShapeDtypeStruct((1, own), jnp.float32),
        in_specs=[vmem] * (len(sizes) + 1),
        out_specs=vmem,
        scratch_shapes=[
            pltpu.VMEM((row_total, width), jnp.bfloat16),
            pltpu.VMEM((width, row_total), jnp.bfloat16),
            pltpu.VMEM((width, width), jnp.float32),
            pltpu.VMEM((width, 6 * BLK), jnp.bfloat16),
            pltpu.VMEM((width, 6 * BLK), jnp.bfloat16),
            pltpu.VMEM((6 * BLK, width), jnp.bfloat16),
            pltpu.VMEM((4 * BLK, width), jnp.bfloat16),
            pltpu.VMEM((own, 2 * BLK), jnp.bfloat16),
            pltpu.VMEM((own, row_total), jnp.float32),
            pltpu.VMEM((SUB, row_total), jnp.float32),
        ],
        compiler_params=pltpu.CompilerParams(vmem_limit_bytes=32 * 1024 * 1024),
    )(*pieces, ids.reshape(1, -1))
    return out.reshape(own)


def contract_rows(left_rows, right_rows):
    return lax.dot_general(
        left_rows, right_rows, (((0,), (0,)), ((), ())), preferred_element_type=jnp.float32
    )


def normalize_rows(values):
    widened = values.astype(jnp.float32)
    square_sum = jnp.sum(widened * widened, axis=1, keepdims=True)
    inverse_norm = lax.rsqrt(square_sum + 1e-06)
    return (widened * inverse_norm).astype(jnp.bfloat16)


def best_match(queries, query_ids, query_start, key_units, key_ids):
    similarity = lax.dot_general(
        queries, key_units, (((1,), (1,)), ((), ())), preferred_element_type=jnp.float32
    )
    query_pos = query_start + jnp.arange(queries.shape[0], dtype=jnp.int32)
    key_pos = jnp.arange(key_units.shape[0], dtype=jnp.int32)
    same_cluster = (
        (query_ids[:, None] == key_ids[None, :])
        & (query_ids[:, None] >= 0)
        & (query_pos[:, None] != key_pos[None, :])
    )
    return jnp.max(jnp.where(same_cluster, similarity, -1.0), axis=1)


def whitening_of(moments, row_total):
    identity = jnp.eye(moments.shape[0], dtype=jnp.float32)
    chol_factor = jnp.linalg.cholesky(moments / float(row_total) + 0.001 * identity)
    return jax.scipy.linalg.solve_triangular(chol_factor, identity, lower=True).astype(
        jnp.bfloat16
    )


def exchange(value, axis, flip):
    return lax.ppermute(value, axis, [(i, i ^ flip) for i in range(lax.axis_size(axis))])


def local_gathered(embeddings, cluster_ids):
    row_count = embeddings.shape[0]
    dp_count = lax.axis_size("dp")
    mp_index = lax.axis_index("mp")
    core, side = mp_index % 2, mp_index // 2
    half, quarter = row_count // 2, row_count // 4

    own_half = lax.dynamic_slice_in_dim(embeddings, core * half, half, 0)
    own_quarter = lax.dynamic_slice_in_dim(own_half, side * quarter, quarter, 0)
    far = jnp.concatenate([exchange(own_quarter, "dp", flip) for flip in range(4, dp_count, 2)], axis=0)
    zone = exchange(own_half, "dp", 2)
    near = exchange(own_half, "dp", 1)
    ids = cluster_ids[None]
    next_ids = exchange(ids, "dp", 2)
    far, near, next_ids = lax.optimization_barrier((far, near, next_ids))

    far_near = exchange(far, "dp", 1)
    far_side = exchange(far, "mp", 2)
    zone_near = exchange(zone, "dp", 1)
    ids = jnp.concatenate([ids, next_ids], axis=0)
    ids = jnp.concatenate([ids, exchange(ids, "dp", 4)], axis=0)
    far_near_side = exchange(far_near, "mp", 2)

    ids = jnp.concatenate([ids, exchange(ids, "dp", 1)], axis=0)
    place = {0: 0, 2: 1, 4: 2, 6: 3, 1: 4, 3: 5, 5: 6, 7: 7}

    held = lax.optimization_barrier([near, zone, zone_near, far, far_side, far_near, far_near_side])
    pieces = [embeddings] + held + [exchange(value, "mp", 1) for value in held]

    def ids_of(sources, start, size):
        return [lax.dynamic_slice_in_dim(ids[place[n]], start, size, 0) for n in sources]

    orders = [cluster_ids]
    for c in (core, 1 - core):
        orders += ids_of((1, 2, 3), c * half, half)
        for first in (4, 5):
            for s in (side, 1 - side):
                orders += ids_of(range(first, dp_count, 2), c * half + s * quarter, quarter)
    return scores_of(pieces, jnp.concatenate(orders))


def local_routed(embeddings, cluster_ids):
    row_count, feat_width = embeddings.shape
    dp_count = lax.axis_size("dp")
    mp_count = lax.axis_size("mp")
    mp_index = lax.axis_index("mp")
    pair_cap = 2 * row_count // dp_count
    slot_count = dp_count * pair_cap
    quarter_len = slot_count // mp_count
    col_share = feat_width // mp_count
    own_cols = lax.dynamic_slice_in_dim(embeddings, mp_index * col_share, col_share, 1)
    column_sums = lax.psum(contract_rows(embeddings, own_cols), "dp")
    moments = lax.all_gather(column_sums, "mp", axis=1, tiled=True)
    whitening = whitening_of(moments, row_count * dp_count)
    owner_ids = cluster_ids // CPO
    owner_hits = (owner_ids[:, None] == jnp.arange(dp_count, dtype=jnp.int32)[None, :]).astype(
        jnp.int32
    )
    earlier_hits = jnp.cumsum(owner_hits, axis=0) - owner_hits
    row_rank = jnp.sum(earlier_hits * owner_hits, axis=1)
    whiten_part = lax.dynamic_slice_in_dim(whitening, mp_index * col_share, col_share, 0)
    whitened = lax.dot_general(
        embeddings, whiten_part, (((1,), (1,)), ((), ())), preferred_element_type=jnp.float32
    ).astype(jnp.bfloat16)
    slot_index = owner_ids * pair_cap + row_rank
    send_rows = jnp.zeros((slot_count, col_share), jnp.bfloat16).at[slot_index].set(whitened)
    send_ids = jnp.full((slot_count,), -1, jnp.int32).at[slot_index].set(cluster_ids)
    got_rows, got_ids = (
        lax.all_to_all(send_rows, "dp", split_axis=0, concat_axis=0, tiled=True),
        lax.all_to_all(send_ids, "dp", split_axis=0, concat_axis=0, tiled=True),
    )
    key_rows = lax.all_gather(got_rows, "mp", axis=1, tiled=True)
    unit = normalize_rows(key_rows)
    query_start = mp_index * quarter_len
    queries = lax.dynamic_slice_in_dim(unit, query_start, quarter_len, 0)
    query_ids = lax.dynamic_slice_in_dim(got_ids, query_start, quarter_len, 0)
    best_score = best_match(queries, query_ids, query_start, unit, got_ids)
    all_scores = lax.all_gather(best_score, "mp", axis=0, tiled=True)
    returned = lax.all_to_all(all_scores, "dp", split_axis=0, concat_axis=0, tiled=True)
    return returned[slot_index]


def local(embeddings, cluster_ids):
    owners = lax.axis_size("dp")
    fits = embeddings.size * 2 * owners <= GATHER_LIMIT
    if fits and lax.axis_size("mp") == 4 and owners == 8:
        return local_gathered(embeddings, cluster_ids)
    return local_routed(embeddings, cluster_ids)


def solution(mesh):
    in_specs = (P("dp", None), P("dp"))
    out_specs = P("dp")
    return jax.shard_map(local, mesh=mesh, in_specs=in_specs, out_specs=out_specs, check_vma=False)
```

```python
import functools
import jax
import jax.numpy as jnp
from jax import lax
from jax.experimental import pallas as pl
from jax.experimental.pallas import tpu as pltpu
from jax.sharding import PartitionSpec as P

CPO = 4
GATHER_LIMIT = 8 * 1024 * 1024
BLK = 128
SUB = 8
GROUP = 4
PANEL = 256


def refine(value):
    guess = pl.reciprocal(value, approx=True)
    return guess * (2.0 - value * guess)


def invert_factor(block, jobs):
    shape = (SUB, BLK)
    lane = lax.broadcasted_iota(jnp.int32, shape, 1)
    sub = lax.broadcasted_iota(jnp.int32, shape, 0)
    count = BLK // SUB
    slots = (count - 1) * SUB // 2
    jobs = list(jobs)
    total = len(jobs)
    rows = [block[SUB * i : SUB * (i + 1), :] for i in range(count)]

    def spread(i, at):
        return [jnp.broadcast_to(rows[i][:, at + q : at + q + 1], shape) for q in range(SUB)]

    def line(value, p):
        return jnp.broadcast_to(value[p : p + 1, :], shape)

    def follow(i, first, steps):
        cols = spread(i, first)
        value = jnp.where((lane >= first) & (lane < first + SUB), 0.0, rows[i])
        for p, (inverse, tops, pivot_row) in enumerate(steps):
            factor = cols[p] * inverse
            for q in range(p + 1, SUB):
                cols[q] = cols[q] - factor * tops[q]
            value = value - factor * pivot_row
        rows[i] = value

    def follow_group(end, members):
        start = end - SUB * GROUP
        factors = as_right(split(jnp.concatenate(members, axis=0)), 0)
        lines = [
            jnp.where((lane >= start + SUB * (n + 1)) & (lane < end), 0.0, member) for n, member in enumerate(members)
        ]
        a, b, c = split(jnp.concatenate(lines, axis=0))
        change = lax.dot_general(
            factors,
            jnp.concatenate([a, a, b, b, a, c], axis=0),
            (((0,), (0,)), ((), ())),
            preferred_element_type=jnp.float32,
        )
        for i in range(end // SUB + GROUP, count):
            kept = jnp.where((lane >= start) & (lane < end), 0.0, rows[i])
            rows[i] = kept - change[SUB * i : SUB * (i + 1), :]

    done = []
    late = []
    members = []
    cols = spread(0, 0)
    for t in range(count):
        first = SUB * t
        here = (lane >= first) & (lane < first + SUB)
        window = min((t // GROUP + 2) * GROUP, count)
        every = {i: spread(i, first) for i in range(t + 1, min(t + 3, window))}
        if every:
            ahead = spread(t, first + SUB)
            next_cols = spread(t + 1, first + SUB)
        late_total = len(late)
        steps = []
        rows[t] = jnp.where(here, (lane - first == sub).astype(jnp.float32), rows[t])
        for i in every:
            rows[i] = jnp.where(here, 0.0, rows[i])
        pivots = jnp.ones(shape, jnp.float32)
        for p in range(0, SUB, 2):
            first_pivot, cross = line(cols[p], p), line(cols[p + 1], p)
            cross_low, corner = line(cols[p], p + 1), line(cols[p + 1], p + 1)
            det = first_pivot * corner - cross * cross_low
            inv1 = refine(first_pivot)
            guess = pl.reciprocal(det, approx=True)
            inv2 = (first_pivot * guess) * (2.0 - det * guess)
            below1 = jnp.where(sub > p, cols[p], 0.0)
            factor1 = below1 * inv1
            factor2 = jnp.where(sub > p + 1, cols[p + 1] - (below1 * cross) * inv1, 0.0) * inv2
            top1 = {q: line(cols[q], p) for q in range(p + 2, SUB)}
            top2 = {q: line(cols[q], p + 1) - (cross_low * top1[q]) * inv1 for q in range(p + 2, SUB)}
            for q in range(p + 2, SUB):
                cols[q] = (cols[q] - factor1 * top1[q]) - factor2 * top2[q]
            low = cross_low * inv1
            row1 = line(rows[t], p)
            row2 = line(rows[t], p + 1) - low * row1
            rows[t] = (rows[t] - factor1 * row1) - factor2 * row2
            pivots = jnp.where(sub == p, first_pivot, jnp.where(sub == p + 1, det * inv1, pivots))
            top1[p + 1] = cross
            steps += [(inv1, top1, row1), (inv2, top2, row2)]
            if every:
                ahead1 = [line(value, p) for value in ahead]
                ahead2 = [line(value, p + 1) - low * one for value, one in zip(ahead, ahead1)]
                ahead = [(v - factor1 * one) - factor2 * two for v, one, two in zip(ahead, ahead1, ahead2)]
            for i, values in every.items():
                near1 = values[p] * inv1
                near2 = (values[p + 1] - near1 * cross) * inv2
                for q in range(p + 2, SUB):
                    values[q] = (values[q] - near1 * top1[q]) - near2 * top2[q]
                rows[i] = (rows[i] - near1 * row1) - near2 * row2
                if i == t + 1:
                    next_cols = [
                        (v - near1 * one) - near2 * two for v, one, two in zip(next_cols, ahead1, ahead2)
                    ]
            for _ in range(late_total * (p + 2) // SUB - late_total * p // SUB):
                late.pop(0)()
            slot = (t * SUB + p) // 2
            for job in jobs[total * slot // slots : total * (slot + 1) // slots]:
                job()
        scale = lax.rsqrt(pivots)
        scale = scale * (1.5 - 0.5 * pivots * scale * scale)
        scaled = rows[t] * scale
        done.append(jnp.where(lane <= first + sub, scaled, 0.0))
        if every:
            cols = next_cols
        if t + 3 < window:
            follow(t + 3, first, steps)
        late += [functools.partial(follow, i, first, steps) for i in range(t + 4, window)]
        members.append(scaled)
        if len(members) == GROUP:
            if window < count:
                follow_group(first + SUB, members)
            members = []
    return jnp.concatenate(done, axis=0)


def dot_nn(a, b):
    return lax.dot_general(a, b, (((1,), (0,)), ((), ())), preferred_element_type=jnp.float32)


def dot_nt(a, b):
    return lax.dot_general(a, b, (((1,), (1,)), ((), ())), preferred_element_type=jnp.float32)


def split(value):
    high = value.astype(jnp.bfloat16)
    rest = value - high.astype(jnp.float32)
    mid = rest.astype(jnp.bfloat16)
    return high, mid, (rest - mid.astype(jnp.float32)).astype(jnp.bfloat16)


def as_left(terms):
    a, b, c = terms
    return jnp.concatenate([a, a, b, b, a, c], axis=1)


def as_right(terms, axis):
    a, b, c = terms
    return jnp.concatenate([a, b, a, b, c, a], axis=axis)


def score_kernel(sizes, *refs):
    pieces = refs[: len(sizes)]
    ids_ref, out_ref = refs[len(sizes) : len(sizes) + 2]
    rows, flipped, work, left, right, below, white, own_white, sims, sums = refs[len(sizes) + 2 :]
    row_total, width = rows.shape
    own = sizes[0]
    count = width // BLK
    blocks = [slice(BLK * n, BLK * (n + 1)) for n in range(count)]
    chunks = [slice(n, n + 2 * own) for n in range(0, row_total, 2 * own)]

    at = 0
    for size, source in zip(sizes, pieces):
        rows[at : at + size, :] = source[...]
        at += size

    def flip_columns(at, size):
        flipped[at : at + size, :] = rows[:, at : at + size].T

    def moments_of(at, size, to, to_size):
        mean = dot_nn(flipped[at : at + size, :], rows[:, to : to + to_size]) * (1.0 / row_total)
        if at < to + to_size:
            shape = (size, to_size)
            row_i = at + lax.broadcasted_iota(jnp.int32, shape, 0)
            col_i = to + lax.broadcasted_iota(jnp.int32, shape, 1)
            mean = mean + jnp.where(row_i == col_i, 0.001, 0.0)
        work[at : at + size, to : to + to_size] = mean

    def mask_of(at):
        own_col = jnp.broadcast_to(ids_ref[:, 0:own], (BLK, own)).T[:, 0:1]
        same = own_col == ids_ref[:, at : at + BLK]
        if at < own:
            own_pos = lax.broadcasted_iota(jnp.int32, (own, BLK), 0)
            same = same & (own_pos != at + lax.broadcasted_iota(jnp.int32, (own, BLK), 1))
        sims[:, at : at + BLK] = jnp.where(same, 0.0, -1e30)

    def first_jobs():
        jobs = [functools.partial(flip_columns, BLK, PANEL - BLK)]
        jobs.append(functools.partial(moments_of, BLK, PANEL - BLK, 0, PANEL))
        jobs += [functools.partial(flip_columns, at, PANEL) for at in range(PANEL, width, PANEL)]
        for to in range(0, width, PANEL):
            at = max(to, PANEL)
            jobs.append(functools.partial(moments_of, at, width - at, to, PANEL))
        return jobs + [functools.partial(mask_of, at) for at in range(0, row_total, BLK)]

    def left_of(begin, h, inverse_right):
        terms = split(dot_nt(as_left(split(work[begin:width, blocks[h]])), inverse_right))
        left[begin:width, :] = as_left(terms)
        right[begin:width, :] = as_right(terms, 1)

    def below_of(h, inverse_left):
        known = slice(0, BLK * h)
        value = dot_nn(inverse_left, as_right(split(work[blocks[h], known]), 0))
        below[:, known] = as_right(split(value), 0)
        white[blocks[h % 4], known] = value.astype(jnp.bfloat16)

    def reduce_left(begin, h):
        known = slice(0, BLK * (h + 1))
        work[begin:width, blocks[h]] = jnp.zeros((width - begin, BLK), jnp.float32)
        work[begin:width, known] -= dot_nn(left[begin:width, :], below[:, known])

    def reduce_right(begin, size):
        work[begin:width, begin : begin + size] -= dot_nt(left[begin:width, :], right[begin : begin + size, :])

    def whiten_own(h, begin, size):
        feats = slice(0, BLK * (h + 1))
        own_white[:, 0:size] = dot_nt(rows[0:own, feats], white[begin : begin + size, feats]).astype(jnp.bfloat16)

    def whiten(c, h, begin, size):
        feats = slice(0, BLK * (h + 1))
        whitened = dot_nt(white[begin : begin + size, feats], rows[chunks[c], feats]).astype(jnp.bfloat16)
        sims[:, chunks[c]] += dot_nn(own_white[:, 0:size], whitened)
        widened = whitened.astype(jnp.float32)
        squares = sum(widened[n : n + SUB, :] * widened[n : n + SUB, :] for n in range(0, size, SUB))
        sums[:, chunks[c]] = squares if h < 2 else sums[:, chunks[c]] + squares

    def whiten_jobs(h, begin, size):
        jobs = [functools.partial(whiten_own, h, begin, size)]
        return jobs + [functools.partial(whiten, c, h, begin, size) for c in range(len(chunks))]

    def finish_rows(h, inverse):
        white[blocks[h % 4], blocks[h]] = inverse.astype(jnp.bfloat16)
        terms = split(inverse)
        below[:, blocks[h]] = as_right(terms, 0)
        jobs = [functools.partial(below_of, h, as_left(terms))] if h else []
        if h >= count - 2:
            return jobs, whiten_jobs(h, BLK * (h % 4), BLK)
        if h % 2 == 0:
            white[blocks[h % 4], blocks[h + 1]] = jnp.zeros((BLK, BLK), jnp.bfloat16)
            return jobs, []
        return jobs, whiten_jobs(h, BLK * (h % 4 - 1), 2 * BLK)

    flip_columns(0, BLK)
    moments_of(0, BLK, 0, BLK)
    block = work[blocks[0], blocks[0]]
    jobs = first_jobs()
    waiting = []
    for k in range(count):
        inverse = invert_factor(block, jobs)
        jobs, white_jobs = finish_rows(k, inverse)
        if k + 1 == count:
            break
        terms = split(inverse)
        inverse_right = as_right(terms, 1)
        nexts = blocks[k + 1]
        terms = split(dot_nt(as_left(split(work[nexts, blocks[k]])), inverse_right))
        value_left, value_right = as_left(terms), as_right(terms, 1)
        block = work[nexts, nexts] - dot_nt(value_left, value_right)
        left[nexts, :] = value_left
        right[nexts, :] = value_right
        begin = BLK * (k + 1)
        if begin + BLK < width:
            jobs.append(functools.partial(left_of, begin + BLK, k, inverse_right))
            for at in range(begin, width, PANEL):
                jobs.append(functools.partial(reduce_right, at, min(PANEL, width - at)))
        jobs.append(functools.partial(reduce_left, begin, k))
        if k % 2 == 1 and white_jobs:
            waiting = white_jobs[len(white_jobs) // 2 :]
            jobs += white_jobs[: len(white_jobs) // 2]
        else:
            jobs += waiting + white_jobs
            waiting = []
    for job in jobs + white_jobs:
        job()

    key_sums = jnp.sum(sums[...], axis=0, keepdims=True)
    scales = lax.rsqrt(key_sums + 1e-06)
    best = jnp.full((own, BLK), -1e30, jnp.float32)
    for at in range(0, row_total, BLK):
        best = jnp.maximum(best, sims[:, at : at + BLK] * scales[:, at : at + BLK])
    top = jnp.max(best, axis=1, keepdims=True)
    own_scale = jnp.broadcast_to(scales[:, 0:own], (BLK, own)).T[:, 0:1]
    top = jnp.where(top < -1e20, -1.0, jnp.maximum(top * own_scale, -1.0))
    out_ref[...] = jnp.broadcast_to(top, (own, BLK)).T[0:1, :]


def scores_of(pieces, ids):
    sizes = tuple(piece.shape[0] for piece in pieces)
    row_total, width, own = sum(sizes), pieces[0].shape[1], sizes[0]
    vmem = pl.BlockSpec(memory_space=pltpu.VMEM)
    out = pl.pallas_call(
        functools.partial(score_kernel, sizes),
        out_shape=jax.ShapeDtypeStruct((1, own), jnp.float32),
        in_specs=[vmem] * (len(sizes) + 1),
        out_specs=vmem,
        scratch_shapes=[
            pltpu.VMEM((row_total, width), jnp.bfloat16),
            pltpu.VMEM((width, row_total), jnp.bfloat16),
            pltpu.VMEM((width, width), jnp.float32),
            pltpu.VMEM((width, 6 * BLK), jnp.bfloat16),
            pltpu.VMEM((width, 6 * BLK), jnp.bfloat16),
            pltpu.VMEM((6 * BLK, width), jnp.bfloat16),
            pltpu.VMEM((4 * BLK, width), jnp.bfloat16),
            pltpu.VMEM((own, 2 * BLK), jnp.bfloat16),
            pltpu.VMEM((own, row_total), jnp.float32),
            pltpu.VMEM((SUB, row_total), jnp.float32),
        ],
        compiler_params=pltpu.CompilerParams(vmem_limit_bytes=32 * 1024 * 1024),
    )(*pieces, ids.reshape(1, -1))
    return out.reshape(own)


def contract_rows(left_rows, right_rows):
    return lax.dot_general(
        left_rows, right_rows, (((0,), (0,)), ((), ())), preferred_element_type=jnp.float32
    )


def normalize_rows(values):
    widened = values.astype(jnp.float32)
    square_sum = jnp.sum(widened * widened, axis=1, keepdims=True)
    inverse_norm = lax.rsqrt(square_sum + 1e-06)
    return (widened * inverse_norm).astype(jnp.bfloat16)


def best_match(queries, query_ids, query_start, key_units, key_ids):
    similarity = lax.dot_general(
        queries, key_units, (((1,), (1,)), ((), ())), preferred_element_type=jnp.float32
    )
    query_pos = query_start + jnp.arange(queries.shape[0], dtype=jnp.int32)
    key_pos = jnp.arange(key_units.shape[0], dtype=jnp.int32)
    same_cluster = (
        (query_ids[:, None] == key_ids[None, :])
        & (query_ids[:, None] >= 0)
        & (query_pos[:, None] != key_pos[None, :])
    )
    return jnp.max(jnp.where(same_cluster, similarity, -1.0), axis=1)


def whitening_of(moments, row_total):
    identity = jnp.eye(moments.shape[0], dtype=jnp.float32)
    chol_factor = jnp.linalg.cholesky(moments / float(row_total) + 0.001 * identity)
    return jax.scipy.linalg.solve_triangular(chol_factor, identity, lower=True).astype(
        jnp.bfloat16
    )


def exchange(value, axis, flip):
    return lax.ppermute(value, axis, [(i, i ^ flip) for i in range(lax.axis_size(axis))])


def local_gathered(embeddings, cluster_ids):
    row_count = embeddings.shape[0]
    dp_count = lax.axis_size("dp")
    mp_index = lax.axis_index("mp")
    core, side = mp_index % 2, mp_index // 2
    half, quarter = row_count // 2, row_count // 4

    own_half = lax.dynamic_slice_in_dim(embeddings, core * half, half, 0)
    own_quarter = lax.dynamic_slice_in_dim(own_half, side * quarter, quarter, 0)
    far = jnp.concatenate([exchange(own_quarter, "dp", flip) for flip in range(4, dp_count, 2)], axis=0)
    zone = exchange(own_half, "dp", 2)
    near = exchange(own_half, "dp", 1)
    ids = cluster_ids[None]
    next_ids = exchange(ids, "dp", 1)
    far, near, next_ids = lax.optimization_barrier((far, near, next_ids))

    far_near = exchange(far, "dp", 1)
    far_side = exchange(far, "mp", 2)
    zone_near = exchange(zone, "dp", 1)
    ids = jnp.concatenate([ids, next_ids], axis=0)
    ids = jnp.concatenate([ids, exchange(ids, "dp", 2)], axis=0)
    far_near_side = exchange(far_near, "mp", 2)

    ids = jnp.concatenate([ids, exchange(ids, "dp", 4)], axis=0)
    held = lax.optimization_barrier([near, zone, zone_near, far, far_side, far_near, far_near_side])
    pieces = [embeddings] + held + [exchange(value, "mp", 1) for value in held]

    def ids_of(sources, start, size):
        return [lax.dynamic_slice_in_dim(ids[n], start, size, 0) for n in sources]

    orders = [cluster_ids]
    for c in (core, 1 - core):
        orders += ids_of((1, 2, 3), c * half, half)
        for first in (4, 5):
            for s in (side, 1 - side):
                orders += ids_of(range(first, dp_count, 2), c * half + s * quarter, quarter)
    return scores_of(pieces, jnp.concatenate(orders))


def local_routed(embeddings, cluster_ids):
    row_count, feat_width = embeddings.shape
    dp_count = lax.axis_size("dp")
    mp_count = lax.axis_size("mp")
    mp_index = lax.axis_index("mp")
    pair_cap = 2 * row_count // dp_count
    slot_count = dp_count * pair_cap
    quarter_len = slot_count // mp_count
    col_share = feat_width // mp_count
    own_cols = lax.dynamic_slice_in_dim(embeddings, mp_index * col_share, col_share, 1)
    column_sums = lax.psum(contract_rows(embeddings, own_cols), "dp")
    moments = lax.all_gather(column_sums, "mp", axis=1, tiled=True)
    whitening = whitening_of(moments, row_count * dp_count)
    owner_ids = cluster_ids // CPO
    owner_hits = (owner_ids[:, None] == jnp.arange(dp_count, dtype=jnp.int32)[None, :]).astype(
        jnp.int32
    )
    earlier_hits = jnp.cumsum(owner_hits, axis=0) - owner_hits
    row_rank = jnp.sum(earlier_hits * owner_hits, axis=1)
    whiten_part = lax.dynamic_slice_in_dim(whitening, mp_index * col_share, col_share, 0)
    whitened = lax.dot_general(
        embeddings, whiten_part, (((1,), (1,)), ((), ())), preferred_element_type=jnp.float32
    ).astype(jnp.bfloat16)
    slot_index = owner_ids * pair_cap + row_rank
    send_rows = jnp.zeros((slot_count, col_share), jnp.bfloat16).at[slot_index].set(whitened)
    send_ids = jnp.full((slot_count,), -1, jnp.int32).at[slot_index].set(cluster_ids)
    got_rows, got_ids = (
        lax.all_to_all(send_rows, "dp", split_axis=0, concat_axis=0, tiled=True),
        lax.all_to_all(send_ids, "dp", split_axis=0, concat_axis=0, tiled=True),
    )
    key_rows = lax.all_gather(got_rows, "mp", axis=1, tiled=True)
    unit = normalize_rows(key_rows)
    query_start = mp_index * quarter_len
    queries = lax.dynamic_slice_in_dim(unit, query_start, quarter_len, 0)
    query_ids = lax.dynamic_slice_in_dim(got_ids, query_start, quarter_len, 0)
    best_score = best_match(queries, query_ids, query_start, unit, got_ids)
    all_scores = lax.all_gather(best_score, "mp", axis=0, tiled=True)
    returned = lax.all_to_all(all_scores, "dp", split_axis=0, concat_axis=0, tiled=True)
    return returned[slot_index]


def local(embeddings, cluster_ids):
    owners = lax.axis_size("dp")
    fits = embeddings.size * 2 * owners <= GATHER_LIMIT
    if fits and lax.axis_size("mp") == 4 and owners == 8:
        return local_gathered(embeddings, cluster_ids)
    return local_routed(embeddings, cluster_ids)


def solution(mesh):
    in_specs = (P("dp", None), P("dp"))
    out_specs = P("dp")
    return jax.shard_map(local, mesh=mesh, in_specs=in_specs, out_specs=out_specs, check_vma=False)
```

```python
import functools
import jax
import jax.numpy as jnp
from jax import lax
from jax.experimental import pallas as pl
from jax.experimental.pallas import tpu as pltpu
from jax.sharding import PartitionSpec as P

CPO = 4
GATHER_LIMIT = 8 * 1024 * 1024
BLK = 128
SUB = 8
GROUP = 4
PANEL = 256


def refine(value):
    guess = pl.reciprocal(value, approx=True)
    return guess * (2.0 - value * guess)


def invert_factor(block, jobs):
    shape = (SUB, BLK)
    lane = lax.broadcasted_iota(jnp.int32, shape, 1)
    sub = lax.broadcasted_iota(jnp.int32, shape, 0)
    count = BLK // SUB
    slots = (count - 1) * SUB // 2
    jobs = list(jobs)
    total = len(jobs)
    rows = [block[SUB * i : SUB * (i + 1), :] for i in range(count)]

    def spread(i, at):
        return [jnp.broadcast_to(rows[i][:, at + q : at + q + 1], shape) for q in range(SUB)]

    def line(value, p):
        return jnp.broadcast_to(value[p : p + 1, :], shape)

    def follow(i, first, steps):
        cols = spread(i, first)
        value = jnp.where((lane >= first) & (lane < first + SUB), 0.0, rows[i])
        for p, (inverse, tops, pivot_row) in enumerate(steps):
            factor = cols[p] * inverse
            for q in range(p + 1, SUB):
                cols[q] = cols[q] - factor * tops[q]
            value = value - factor * pivot_row
        rows[i] = value

    def follow_group(end, members):
        start = end - SUB * GROUP
        factors = as_right(split(jnp.concatenate(members, axis=0)), 0)
        lines = [
            jnp.where((lane >= start + SUB * (n + 1)) & (lane < end), 0.0, member) for n, member in enumerate(members)
        ]
        a, b, c = split(jnp.concatenate(lines, axis=0))
        change = lax.dot_general(
            factors,
            jnp.concatenate([a, a, b, b, a, c], axis=0),
            (((0,), (0,)), ((), ())),
            preferred_element_type=jnp.float32,
        )
        for i in range(end // SUB + GROUP, count):
            kept = jnp.where((lane >= start) & (lane < end), 0.0, rows[i])
            rows[i] = kept - change[SUB * i : SUB * (i + 1), :]

    done = []
    late = []
    members = []
    cols = spread(0, 0)
    for t in range(count):
        first = SUB * t
        here = (lane >= first) & (lane < first + SUB)
        window = min((t // GROUP + 2) * GROUP, count)
        every = {i: spread(i, first) for i in range(t + 1, min(t + 3, window))}
        if every:
            ahead = spread(t, first + SUB)
            next_cols = spread(t + 1, first + SUB)
        late_total = len(late)
        steps = []
        rows[t] = jnp.where(here, (lane - first == sub).astype(jnp.float32), rows[t])
        for i in every:
            rows[i] = jnp.where(here, 0.0, rows[i])
        pivots = jnp.ones(shape, jnp.float32)
        for p in range(0, SUB, 2):
            first_pivot, cross = line(cols[p], p), line(cols[p + 1], p)
            cross_low, corner = line(cols[p], p + 1), line(cols[p + 1], p + 1)
            det = first_pivot * corner - cross * cross_low
            inv1 = refine(first_pivot)
            guess = pl.reciprocal(det, approx=True)
            inv2 = (first_pivot * guess) * (2.0 - det * guess)
            below1 = jnp.where(sub > p, cols[p], 0.0)
            factor1 = below1 * inv1
            factor2 = jnp.where(sub > p + 1, cols[p + 1] - (below1 * cross) * inv1, 0.0) * inv2
            top1 = {q: line(cols[q], p) for q in range(p + 2, SUB)}
            top2 = {q: line(cols[q], p + 1) - (cross_low * top1[q]) * inv1 for q in range(p + 2, SUB)}
            for q in range(p + 2, SUB):
                cols[q] = (cols[q] - factor1 * top1[q]) - factor2 * top2[q]
            low = cross_low * inv1
            row1 = line(rows[t], p)
            row2 = line(rows[t], p + 1) - low * row1
            rows[t] = (rows[t] - factor1 * row1) - factor2 * row2
            pivots = jnp.where(sub == p, first_pivot, jnp.where(sub == p + 1, det * inv1, pivots))
            top1[p + 1] = cross
            steps += [(inv1, top1, row1), (inv2, top2, row2)]
            if every:
                ahead1 = [line(value, p) for value in ahead]
                ahead2 = [line(value, p + 1) - low * one for value, one in zip(ahead, ahead1)]
                ahead = [(v - factor1 * one) - factor2 * two for v, one, two in zip(ahead, ahead1, ahead2)]
            for i, values in every.items():
                near1 = values[p] * inv1
                near2 = (values[p + 1] - near1 * cross) * inv2
                for q in range(p + 2, SUB):
                    values[q] = (values[q] - near1 * top1[q]) - near2 * top2[q]
                rows[i] = (rows[i] - near1 * row1) - near2 * row2
                if i == t + 1:
                    next_cols = [
                        (v - near1 * one) - near2 * two for v, one, two in zip(next_cols, ahead1, ahead2)
                    ]
            for _ in range(late_total * (p + 2) // SUB - late_total * p // SUB):
                late.pop(0)()
            slot = (t * SUB + p) // 2
            for job in jobs[total * slot // slots : total * (slot + 1) // slots]:
                job()
        scale = lax.rsqrt(pivots)
        scale = scale * (1.5 - 0.5 * pivots * scale * scale)
        scaled = rows[t] * scale
        done.append(jnp.where(lane <= first + sub, scaled, 0.0))
        if every:
            cols = next_cols
        if t + 3 < window:
            follow(t + 3, first, steps)
        late += [functools.partial(follow, i, first, steps) for i in range(t + 4, window)]
        members.append(scaled)
        if len(members) == GROUP:
            if window < count:
                follow_group(first + SUB, members)
            members = []
    return jnp.concatenate(done, axis=0)


def dot_nn(a, b):
    return lax.dot_general(a, b, (((1,), (0,)), ((), ())), preferred_element_type=jnp.float32)


def dot_nt(a, b):
    return lax.dot_general(a, b, (((1,), (1,)), ((), ())), preferred_element_type=jnp.float32)


def split(value):
    high = value.astype(jnp.bfloat16)
    rest = value - high.astype(jnp.float32)
    mid = rest.astype(jnp.bfloat16)
    return high, mid, (rest - mid.astype(jnp.float32)).astype(jnp.bfloat16)


def as_left(terms):
    a, b, c = terms
    return jnp.concatenate([a, a, b, b, a, c], axis=1)


def as_right(terms, axis):
    a, b, c = terms
    return jnp.concatenate([a, b, a, b, c, a], axis=axis)


def score_kernel(sizes, *refs):
    pieces = refs[: len(sizes)]
    ids_ref, out_ref = refs[len(sizes) : len(sizes) + 2]
    rows, flipped, work, left, right, below, white, own_white, sims, sums = refs[len(sizes) + 2 :]
    row_total, width = rows.shape
    own = sizes[0]
    count = width // BLK
    blocks = [slice(BLK * n, BLK * (n + 1)) for n in range(count)]
    chunks = [slice(n, n + 2 * own) for n in range(0, row_total, 2 * own)]

    at = 0
    for size, source in zip(sizes, pieces):
        rows[at : at + size, :] = source[...]
        at += size

    def flip_columns(at, size):
        flipped[at : at + size, :] = rows[:, at : at + size].T

    def moments_of(at, size, to, to_size):
        mean = dot_nn(flipped[at : at + size, :], rows[:, to : to + to_size]) * (1.0 / row_total)
        if at < to + to_size:
            shape = (size, to_size)
            row_i = at + lax.broadcasted_iota(jnp.int32, shape, 0)
            col_i = to + lax.broadcasted_iota(jnp.int32, shape, 1)
            mean = mean + jnp.where(row_i == col_i, 0.001, 0.0)
        work[at : at + size, to : to + to_size] = mean

    def mask_of(at):
        own_col = jnp.broadcast_to(ids_ref[:, 0:own], (BLK, own)).T[:, 0:1]
        same = own_col == ids_ref[:, at : at + BLK]
        if at < own:
            own_pos = lax.broadcasted_iota(jnp.int32, (own, BLK), 0)
            same = same & (own_pos != at + lax.broadcasted_iota(jnp.int32, (own, BLK), 1))
        sims[:, at : at + BLK] = jnp.where(same, 0.0, -1e30)

    def first_jobs():
        jobs = [functools.partial(flip_columns, BLK, PANEL - BLK)]
        jobs.append(functools.partial(moments_of, BLK, PANEL - BLK, 0, PANEL))
        jobs += [functools.partial(flip_columns, at, PANEL) for at in range(PANEL, width, PANEL)]
        for to in range(0, width, PANEL):
            at = max(to, PANEL)
            jobs.append(functools.partial(moments_of, at, width - at, to, PANEL))
        return jobs + [functools.partial(mask_of, at) for at in range(0, row_total, BLK)]

    def left_of(begin, h, inverse_right):
        terms = split(dot_nt(as_left(split(work[begin:width, blocks[h]])), inverse_right))
        left[begin:width, :] = as_left(terms)
        right[begin:width, :] = as_right(terms, 1)

    def below_of(h, inverse_left):
        known = slice(0, BLK * h)
        value = dot_nn(inverse_left, as_right(split(work[blocks[h], known]), 0))
        below[:, known] = as_right(split(value), 0)
        white[blocks[h % 4], known] = value.astype(jnp.bfloat16)

    def reduce_left(begin, h):
        known = slice(0, BLK * (h + 1))
        work[begin:width, blocks[h]] = jnp.zeros((width - begin, BLK), jnp.float32)
        work[begin:width, known] -= dot_nn(left[begin:width, :], below[:, known])

    def reduce_right(begin, size):
        work[begin:width, begin : begin + size] -= dot_nt(left[begin:width, :], right[begin : begin + size, :])

    def whiten_own(h, begin, size):
        feats = slice(0, BLK * (h + 1))
        own_white[:, 0:size] = dot_nt(rows[0:own, feats], white[begin : begin + size, feats]).astype(jnp.bfloat16)

    def whiten(c, h, begin, size):
        feats = slice(0, BLK * (h + 1))
        whitened = dot_nt(white[begin : begin + size, feats], rows[chunks[c], feats]).astype(jnp.bfloat16)
        sims[:, chunks[c]] += dot_nn(own_white[:, 0:size], whitened)
        widened = whitened.astype(jnp.float32)
        squares = sum(widened[n : n + SUB, :] * widened[n : n + SUB, :] for n in range(0, size, SUB))
        sums[:, chunks[c]] = squares if h < 2 else sums[:, chunks[c]] + squares

    def whiten_jobs(h, begin, size):
        jobs = [functools.partial(whiten_own, h, begin, size)]
        return jobs + [functools.partial(whiten, c, h, begin, size) for c in range(len(chunks))]

    def finish_rows(h, inverse):
        white[blocks[h % 4], blocks[h]] = inverse.astype(jnp.bfloat16)
        terms = split(inverse)
        below[:, blocks[h]] = as_right(terms, 0)
        jobs = [functools.partial(below_of, h, as_left(terms))] if h else []
        if h >= count - 2:
            return jobs, whiten_jobs(h, BLK * (h % 4), BLK)
        if h % 2 == 0:
            white[blocks[h % 4], blocks[h + 1]] = jnp.zeros((BLK, BLK), jnp.bfloat16)
            return jobs, []
        return jobs, whiten_jobs(h, BLK * (h % 4 - 1), 2 * BLK)

    flip_columns(0, BLK)
    moments_of(0, BLK, 0, BLK)
    block = work[blocks[0], blocks[0]]
    jobs = first_jobs()
    waiting = []
    for k in range(count):
        inverse = invert_factor(block, jobs)
        jobs, white_jobs = finish_rows(k, inverse)
        if k + 1 == count:
            break
        terms = split(inverse)
        inverse_right = as_right(terms, 1)
        nexts = blocks[k + 1]
        terms = split(dot_nt(as_left(split(work[nexts, blocks[k]])), inverse_right))
        value_left, value_right = as_left(terms), as_right(terms, 1)
        block = work[nexts, nexts] - dot_nt(value_left, value_right)
        left[nexts, :] = value_left
        right[nexts, :] = value_right
        begin = BLK * (k + 1)
        if begin + BLK < width:
            jobs.append(functools.partial(left_of, begin + BLK, k, inverse_right))
            for at in range(begin, width, PANEL):
                jobs.append(functools.partial(reduce_right, at, min(PANEL, width - at)))
        jobs.append(functools.partial(reduce_left, begin, k))
        if k % 2 == 1 and white_jobs:
            waiting = white_jobs[len(white_jobs) // 2 :]
            jobs += white_jobs[: len(white_jobs) // 2]
        else:
            jobs += waiting + white_jobs
            waiting = []
    for job in jobs + white_jobs:
        job()

    key_sums = jnp.sum(sums[...], axis=0, keepdims=True)
    scales = lax.rsqrt(key_sums + 1e-06)
    best = jnp.full((own, BLK), -1e30, jnp.float32)
    for at in range(0, row_total, BLK):
        best = jnp.maximum(best, sims[:, at : at + BLK] * scales[:, at : at + BLK])
    top = jnp.max(best, axis=1, keepdims=True)
    own_scale = jnp.broadcast_to(scales[:, 0:own], (BLK, own)).T[:, 0:1]
    top = jnp.where(top < -1e20, -1.0, jnp.maximum(top * own_scale, -1.0))
    out_ref[...] = jnp.broadcast_to(top, (own, BLK)).T[0:1, :]


def scores_of(pieces, ids):
    sizes = tuple(piece.shape[0] for piece in pieces)
    row_total, width, own = sum(sizes), pieces[0].shape[1], sizes[0]
    vmem = pl.BlockSpec(memory_space=pltpu.VMEM)
    out = pl.pallas_call(
        functools.partial(score_kernel, sizes),
        out_shape=jax.ShapeDtypeStruct((1, own), jnp.float32),
        in_specs=[vmem] * (len(sizes) + 1),
        out_specs=vmem,
        scratch_shapes=[
            pltpu.VMEM((row_total, width), jnp.bfloat16),
            pltpu.VMEM((width, row_total), jnp.bfloat16),
            pltpu.VMEM((width, width), jnp.float32),
            pltpu.VMEM((width, 6 * BLK), jnp.bfloat16),
            pltpu.VMEM((width, 6 * BLK), jnp.bfloat16),
            pltpu.VMEM((6 * BLK, width), jnp.bfloat16),
            pltpu.VMEM((4 * BLK, width), jnp.bfloat16),
            pltpu.VMEM((own, 2 * BLK), jnp.bfloat16),
            pltpu.VMEM((own, row_total), jnp.float32),
            pltpu.VMEM((SUB, row_total), jnp.float32),
        ],
        compiler_params=pltpu.CompilerParams(vmem_limit_bytes=32 * 1024 * 1024),
    )(*pieces, ids.reshape(1, -1))
    return out.reshape(own)


def contract_rows(left_rows, right_rows):
    return lax.dot_general(
        left_rows, right_rows, (((0,), (0,)), ((), ())), preferred_element_type=jnp.float32
    )


def normalize_rows(values):
    widened = values.astype(jnp.float32)
    square_sum = jnp.sum(widened * widened, axis=1, keepdims=True)
    inverse_norm = lax.rsqrt(square_sum + 1e-06)
    return (widened * inverse_norm).astype(jnp.bfloat16)


def best_match(queries, query_ids, query_start, key_units, key_ids):
    similarity = lax.dot_general(
        queries, key_units, (((1,), (1,)), ((), ())), preferred_element_type=jnp.float32
    )
    query_pos = query_start + jnp.arange(queries.shape[0], dtype=jnp.int32)
    key_pos = jnp.arange(key_units.shape[0], dtype=jnp.int32)
    same_cluster = (
        (query_ids[:, None] == key_ids[None, :])
        & (query_ids[:, None] >= 0)
        & (query_pos[:, None] != key_pos[None, :])
    )
    return jnp.max(jnp.where(same_cluster, similarity, -1.0), axis=1)


def whitening_of(moments, row_total):
    identity = jnp.eye(moments.shape[0], dtype=jnp.float32)
    chol_factor = jnp.linalg.cholesky(moments / float(row_total) + 0.001 * identity)
    return jax.scipy.linalg.solve_triangular(chol_factor, identity, lower=True).astype(
        jnp.bfloat16
    )


def exchange(value, axis, flip):
    return lax.ppermute(value, axis, [(i, i ^ flip) for i in range(lax.axis_size(axis))])


def local_gathered(embeddings, cluster_ids):
    row_count = embeddings.shape[0]
    dp_count = lax.axis_size("dp")
    mp_index = lax.axis_index("mp")
    core, side = mp_index % 2, mp_index // 2
    half, quarter = row_count // 2, row_count // 4

    own_half = lax.dynamic_slice_in_dim(embeddings, core * half, half, 0)
    own_quarter = lax.dynamic_slice_in_dim(own_half, side * quarter, quarter, 0)
    far = jnp.concatenate([exchange(own_quarter, "dp", flip) for flip in range(4, dp_count, 2)], axis=0)
    zone = exchange(own_half, "dp", 2)
    near = exchange(own_half, "dp", 1)
    ids = cluster_ids[None]
    next_ids = exchange(ids, "dp", 1)
    far, near, next_ids = lax.optimization_barrier((far, near, next_ids))

    far_near = exchange(far, "dp", 1)
    far_side = exchange(far, "mp", 2)
    zone_near = exchange(zone, "dp", 1)
    ids = jnp.concatenate([ids, next_ids], axis=0)
    far_near, ids = lax.optimization_barrier((far_near, ids))
    far_near_side = exchange(far_near, "mp", 2)
    for flip in (2, 4):
        ids = jnp.concatenate([ids, exchange(ids, "dp", flip)], axis=0)
    held = lax.optimization_barrier([near, zone, zone_near, far, far_side, far_near, far_near_side])
    pieces = [embeddings] + held + [exchange(value, "mp", 1) for value in held]

    def ids_of(sources, start, size):
        return [lax.dynamic_slice_in_dim(ids[n], start, size, 0) for n in sources]

    orders = [cluster_ids]
    for c in (core, 1 - core):
        orders += ids_of((1, 2, 3), c * half, half)
        for first in (4, 5):
            for s in (side, 1 - side):
                orders += ids_of(range(first, dp_count, 2), c * half + s * quarter, quarter)
    return scores_of(pieces, jnp.concatenate(orders))


def local_routed(embeddings, cluster_ids):
    row_count, feat_width = embeddings.shape
    dp_count = lax.axis_size("dp")
    mp_count = lax.axis_size("mp")
    mp_index = lax.axis_index("mp")
    pair_cap = 2 * row_count // dp_count
    slot_count = dp_count * pair_cap
    quarter_len = slot_count // mp_count
    col_share = feat_width // mp_count
    own_cols = lax.dynamic_slice_in_dim(embeddings, mp_index * col_share, col_share, 1)
    column_sums = lax.psum(contract_rows(embeddings, own_cols), "dp")
    moments = lax.all_gather(column_sums, "mp", axis=1, tiled=True)
    whitening = whitening_of(moments, row_count * dp_count)
    owner_ids = cluster_ids // CPO
    owner_hits = (owner_ids[:, None] == jnp.arange(dp_count, dtype=jnp.int32)[None, :]).astype(
        jnp.int32
    )
    earlier_hits = jnp.cumsum(owner_hits, axis=0) - owner_hits
    row_rank = jnp.sum(earlier_hits * owner_hits, axis=1)
    whiten_part = lax.dynamic_slice_in_dim(whitening, mp_index * col_share, col_share, 0)
    whitened = lax.dot_general(
        embeddings, whiten_part, (((1,), (1,)), ((), ())), preferred_element_type=jnp.float32
    ).astype(jnp.bfloat16)
    slot_index = owner_ids * pair_cap + row_rank
    send_rows = jnp.zeros((slot_count, col_share), jnp.bfloat16).at[slot_index].set(whitened)
    send_ids = jnp.full((slot_count,), -1, jnp.int32).at[slot_index].set(cluster_ids)
    got_rows, got_ids = (
        lax.all_to_all(send_rows, "dp", split_axis=0, concat_axis=0, tiled=True),
        lax.all_to_all(send_ids, "dp", split_axis=0, concat_axis=0, tiled=True),
    )
    key_rows = lax.all_gather(got_rows, "mp", axis=1, tiled=True)
    unit = normalize_rows(key_rows)
    query_start = mp_index * quarter_len
    queries = lax.dynamic_slice_in_dim(unit, query_start, quarter_len, 0)
    query_ids = lax.dynamic_slice_in_dim(got_ids, query_start, quarter_len, 0)
    best_score = best_match(queries, query_ids, query_start, unit, got_ids)
    all_scores = lax.all_gather(best_score, "mp", axis=0, tiled=True)
    returned = lax.all_to_all(all_scores, "dp", split_axis=0, concat_axis=0, tiled=True)
    return returned[slot_index]


def local(embeddings, cluster_ids):
    owners = lax.axis_size("dp")
    fits = embeddings.size * 2 * owners <= GATHER_LIMIT
    if fits and lax.axis_size("mp") == 4 and owners == 8:
        return local_gathered(embeddings, cluster_ids)
    return local_routed(embeddings, cluster_ids)


def solution(mesh):
    in_specs = (P("dp", None), P("dp"))
    out_specs = P("dp")
    return jax.shard_map(local, mesh=mesh, in_specs=in_specs, out_specs=out_specs, check_vma=False)
```
